32 devices in a mesh: seq: 8 (over z, x), batch: 4 (over y, core).
Axes of the slice: x: 2, y: 2, z: 4, core: 2. Of those that a mesh axis runs over, the one named last changes fastest.
Arguments:
- tokens: bfloat16 [8, 2048, 1024], P('batch', 'seq'), may hold values from -6 to 6
- starts: int32 [8, 2048], P('batch', 'seq'), may hold values from 0 to 1, as said below
- entry_gain: float32 [1024], replicated, may hold values from 0.25 to 1.75
- query_weight: bfloat16 [1024, 1024], P('seq'), may hold values from -0.1875 to 0.1875
- key_weight: bfloat16 [1024, 1024], P('seq'), may hold values from -0.1875 to 0.1875
- value_weight: bfloat16 [1024, 1024], P('seq'), may hold values from -0.1875 to 0.1875
- gate_weight: bfloat16 [1024, 1024], P('seq'), may hold values from -0.1875 to 0.1875
- head_gain: float32 [1024], replicated, may hold values from 0.25 to 1.75
- output_weight: bfloat16 [1024, 1024], P('seq'), may hold values from -0.375 to 0.375
- middle_gain: float32 [1024], replicated, may hold values from 0.25 to 1.75
- left_weight: bfloat16 [1024, 2816], P('seq'), may hold values from -0.1875 to 0.1875
- right_weight: bfloat16 [1024, 2816], P('seq'), may hold values from -0.1875 to 0.1875
- down_weight: bfloat16 [2816, 1024], P(None, 'seq'), may hold values from -0.109375 to 0.109375
- cotangent: bfloat16 [8, 2048, 1024], P('batch', 'seq'), may hold values from -6 to 6
Outputs:
- mixed: bfloat16 [8, 2048, 1024], P('batch', 'seq')
- input_gradient: float32 [8, 2048, 1024], P('batch', 'seq')
- entry_gradient: float32 [1024], P('seq')
- query_gradient: float32 [1024, 1024], P('seq')
- key_gradient: float32 [1024, 1024], P('seq')
- value_gradient: float32 [1024, 1024], P('seq')
- gate_gradient: float32 [1024, 1024], P('seq')
- head_gradient: float32 [1024], P('seq')
- output_gradient: float32 [1024, 1024], P('seq')
- middle_gradient: float32 [1024], P('seq')
- left_gradient: float32 [1024, 2816], P('seq')
- right_gradient: float32 [1024, 2816], P('seq')
- down_gradient: float32 [2816, 1024], P(None, 'seq')
The draws below stay inside these ranges and needn't reach their ends.
Inputs may be any that keep to these rules, and one draw needn't show every extreme that they name: `starts`: A row's first position never holds a start.
All inputs are finite; a program needn't handle non-finite values.
Results may differ from the reference program's by a relative error of at most 0.019.
Values may be sent and summed in bfloat16 or wider, within the bound.
No kernel may reach another device: no remote copies, remote signals or barrier semaphores. Data moves between devices by JAX's collectives and lax.ppermute only.
A program may use at most 256 MiB of HBM per device.

```python
import jax
import jax.numpy as jnp
from jax import lax

D = 1024
HEADS = 16
HEAD = 64
FF = 2816
BLOCK = 256
ROWS_DEV = 2
ROWS = 8
LENGTH = 2048


def draw_starts(key, part):
    key = jax.random.fold_in(key, 7)
    coin_key, pick_key, begin_key, finish_key = jax.random.split(key, 4)
    coins = jax.random.randint(coin_key, (ROWS, LENGTH), 0, 4 * BLOCK)
    scattered = (coins == 0).astype(jnp.int32)
    chosen = jax.random.randint(pick_key, (ROWS // ROWS_DEV,), 0, ROWS_DEV)
    numbers = jnp.arange(ROWS)
    spanning = numbers == jnp.repeat(chosen, ROWS_DEV) + numbers // ROWS_DEV * ROWS_DEV
    begin = jax.random.randint(begin_key, (ROWS, 1), 1, BLOCK)
    finish = jax.random.randint(finish_key, (ROWS, 1), LENGTH - BLOCK, LENGTH)
    place = jnp.arange(LENGTH)[None, :]
    bridged = ((place == begin) | (place == finish)).astype(jnp.int32)
    picked = jnp.where(spanning[:, None], bridged, scattered)
    return picked * (place > 0).astype(jnp.int32)


def strengthened(entries, rng, source, target, parts, factor):
    def block_of(axis_at):
        return (jnp.arange(entries.shape[axis_at]) // (entries.shape[axis_at] // parts)).reshape((-1,) + (1,) * (entries.ndim - 1 - axis_at))

    one_side = jax.random.permutation(rng, parts)[block_of(target)]
    second = (block_of(target) + parts // 2) % parts
    return jnp.where((block_of(source) == one_side) | (block_of(source) == second), factor * entries, entries)


def levels(own_key, shape, cuts, low, top_value):
    level = 1.0
    for position, parts in cuts:
        steps = jax.random.uniform(jax.random.fold_in(jax.random.fold_in(own_key, 6), position), (parts,), jnp.float32, low / len(cuts), top_value / len(cuts))
        level = level * jnp.repeat(jnp.exp(steps), shape[position] // parts).reshape((-1,) + (1,) * (len(shape) - 1 - position))
    return level


def normal_values(rng, shape, scale, most, pieces=(), held_as=jnp.bfloat16):
    values = scale * jax.random.normal(rng, shape, jnp.float32)
    if pieces:
        values = values * levels(rng, shape, pieces, -0.22, 0.18)
    return jnp.clip(values, -most, most).astype(held_as)


def heavy_noise(rng, extent, width, reach, shards, heavy, kind=jnp.bfloat16):
    entries = width * jax.random.normal(rng, extent, jnp.float32)
    if shards:
        entries = entries * levels(rng, extent, shards, -0.22, 0.18)
    return jnp.clip(strengthened(entries, jax.random.fold_in(rng, 3), *heavy), -reach, reach).astype(kind)


def setup_inputs(seed: int = 0) -> dict:
    streams_of = jax.random.split(jax.random.key(seed), 15)
    tokens = normal_values(streams_of[0], (ROWS, LENGTH, D), 1.0, 6.0, ((0, 4), (1, 8)))
    starts = draw_starts(jax.random.fold_in(streams_of[14], 71), 0)
    entry_gain = jnp.clip(1.0 + 0.15 * jax.random.normal(streams_of[2], (D,), jnp.float32), 0.25, 1.75)
    query_weight = normal_values(streams_of[3], (D, D), D ** -0.5, 0.1875, ((0, 8),))
    key_weight = normal_values(streams_of[4], (D, D), D ** -0.5, 0.1875, ((0, 8),))
    value_weight = normal_values(streams_of[5], (D, D), D ** -0.5, 0.1875, ((0, 8),))
    gate_weight = normal_values(streams_of[6], (D, D), D ** -0.5, 0.1875, ((0, 8),))
    head_gain = jnp.clip(1.0 + 0.15 * jax.random.normal(streams_of[7], (D,), jnp.float32), 0.25, 1.75)
    output_weight = normal_values(streams_of[8], (D, D), (D // 4) ** -0.5, 0.375, ((0, 8),))
    middle_gain = jnp.clip(1.0 + 0.15 * jax.random.normal(streams_of[9], (D,), jnp.float32), 0.25, 1.75)
    left_weight = normal_values(streams_of[10], (D, FF), D ** -0.5, 0.1875, ((0, 8),))
    right_weight = normal_values(streams_of[11], (D, FF), D ** -0.5, 0.1875, ((0, 8),))
    down_weight = normal_values(streams_of[12], (FF, D), FF ** -0.5, 0.109375, ((1, 8),))
    cotangent = heavy_noise(streams_of[13], (ROWS, LENGTH, D), 1.0, 6.0, ((0, 4), (1, 8)), (1, 2, 8, 2.0))
    return dict(tokens=tokens, starts=starts, entry_gain=entry_gain, query_weight=query_weight, key_weight=key_weight, value_weight=value_weight, gate_weight=gate_weight, head_gain=head_gain, output_weight=output_weight, middle_gain=middle_gain, left_weight=left_weight, right_weight=right_weight, down_weight=down_weight, cotangent=cotangent)


EPSILON = 1e-06
HIGHEST = lax.Precision.HIGHEST

@jax.custom_vjp
def low(v):
    return lax.optimization_barrier(v.astype(jnp.bfloat16)).astype(jnp.float32)

@jax.custom_vjp
def low_back(v):
    return v

def low_keep(v):
    return (low(v), None)

def low_pass(kept, grad):
    return (grad,)

def back_keep(v):
    return (v, None)

def back_low(kept, grad):
    return (low(grad),)
low.defvjp(low_keep, low_pass)
low_back.defvjp(back_keep, back_low)

def product(left, right):
    return jnp.dot(left, right, precision=HIGHEST)

def inverse_rms(values):
    return lax.rsqrt(lax.optimization_barrier(jnp.mean(values * values, axis=-1, keepdims=True)) + EPSILON)

def attend_row(query, keys, values, starts):
    segment = jnp.cumsum(starts).astype(jnp.int32)
    count = LENGTH // BLOCK
    shaped = (count, BLOCK, HEADS, HEAD)
    items = (query.reshape(shaped), keys.reshape(shaped), values.reshape(shaped), segment.reshape(count, BLOCK))
    order = jnp.arange(BLOCK)
    causal = order[:, None] >= order[None, :]

    def block_step(carry, item):
        state, prior = carry
        block_query, block_keys, block_values, block_segment = item
        allowed = ((block_segment[:, None] == block_segment[None, :]) & causal).astype(jnp.float32)
        scores = jnp.einsum('thd,shd->hts', block_query, block_keys, precision=HIGHEST) * allowed[None]
        weights = low(low_back(scores))
        inside = jnp.einsum('hts,shd->thd', weights, block_values, precision=HIGHEST)
        inherit = (block_segment == prior).astype(jnp.float32)
        carried = jnp.einsum('thd,hde->the', block_query, low(state), precision=HIGHEST) * inherit[:, None, None]
        last = block_segment[BLOCK - 1]
        tail = (block_segment == last).astype(jnp.float32)
        fresh = low_back(jnp.einsum('shd,she->hde', block_keys, block_values * tail[:, None, None], precision=HIGHEST))
        keep = (last == prior).astype(jnp.float32)
        return ((keep * state + fresh, last), inside + carried)
    initial = (jnp.zeros((HEADS, HEAD, HEAD), jnp.float32), jnp.int32(-1))
    final, outputs = lax.scan(jax.checkpoint(block_step), initial, items)
    return outputs.reshape(LENGTH, HEADS * HEAD)

def layer_row(row, starts, weights):
    entry_gain, query_weight, key_weight, value_weight, gate_weight, head_gain, output_weight, middle_gain, left_weight, right_weight, down_weight = weights
    normed_in = low(row * inverse_rms(row) * entry_gain)
    query = low(jax.nn.softplus(low_back(product(normed_in, query_weight))))
    keys = low(jax.nn.softplus(low_back(product(normed_in, key_weight))))
    values = low(low_back(product(normed_in, value_weight)))
    gate = jax.nn.sigmoid(low_back(product(normed_in, gate_weight)))
    attended = low_back(attend_row(query, keys, values, starts)).reshape(LENGTH, HEADS, HEAD)
    headed = attended * inverse_rms(attended) * head_gain.reshape(HEADS, HEAD)
    gated = low(headed.reshape(LENGTH, HEADS * HEAD) * gate)
    middle = row + low_back(product(gated, output_weight))
    normed_mid = low(middle * inverse_rms(middle) * middle_gain)
    left = low_back(product(normed_mid, left_weight))
    right = low_back(product(normed_mid, right_weight))
    joined = low(left * right)
    return middle + low_back(product(joined, down_weight))

def forward(inputs, starts, weights):

    def one_row(carry, item):
        row, row_starts = item
        return (carry, layer_row(row, row_starts, weights))
    final, outputs = lax.scan(jax.checkpoint(one_row), jnp.float32(0.0), (inputs, starts))
    return outputs

def reference(tokens, starts, entry_gain, query_weight, key_weight, value_weight, gate_weight, head_gain, output_weight, middle_gain, left_weight, right_weight, down_weight, cotangent):
    weights = tuple((item.astype(jnp.float32) for item in (entry_gain, query_weight, key_weight, value_weight, gate_weight, head_gain, output_weight, middle_gain, left_weight, right_weight, down_weight)))
    inputs = tokens.astype(jnp.float32)

    def apply(inputs, *weights):
        return forward(inputs, starts, weights)
    result, pullback = jax.vjp(apply, inputs, *weights)
    gradients = pullback(cotangent.astype(jnp.float32))
    return (result.astype(jnp.bfloat16), gradients[0], gradients[1], gradients[2], gradients[3], gradients[4], gradients[5], gradients[6], gradients[7], gradients[8], gradients[9], gradients[10], gradients[11])
```

```python
import functools

import jax
import jax.numpy as jnp
from jax import lax
from jax.experimental import pallas as pl
from jax.experimental.pallas import tpu as pltpu
from jax.sharding import PartitionSpec as P

HEADS = 16
HEAD = 64
EPSILON = 1e-06
BF = jnp.bfloat16
F32 = jnp.float32
VMEM = pl.BlockSpec(memory_space=pltpu.VMEM)
SMEM = pl.BlockSpec(memory_space=pltpu.SMEM)
ANY = pl.BlockSpec(memory_space=pl.ANY)
LIMIT = 60 * 1024 * 1024


def inverse_rms(values):
    return lax.rsqrt(jnp.mean(values * values, axis=-1, keepdims=True) + EPSILON)


def dot(left, right):
    return jnp.dot(left, right, preferred_element_type=F32)


def dot_nt(left, right):
    return lax.dot_general(left, right, (((1,), (1,)), ((), ())), preferred_element_type=F32)


def dot_tn(left, right):
    return lax.dot_general(left, right, (((0,), (0,)), ((), ())), preferred_element_type=F32)


def norm_back(upstream, values, inverse, gain):
    scaled = upstream * gain
    gain_part = jnp.sum(upstream * values * inverse, axis=0)
    cubed = inverse * inverse * inverse
    return (
        inverse * scaled - values * cubed * jnp.mean(scaled * values, axis=-1, keepdims=True),
        gain_part,
    )


def swap(value, axis, bit, size):
    return lax.ppermute(value, axis, [(i, i ^ bit) for i in range(size)])


class Plan:
    def __init__(self, mesh_shape, width):
        self.seq = mesh_shape["seq"]
        self.batch = mesh_shape["batch"]
        self.rows = width // self.seq
        self.fast = self.seq == 8 and self.batch == 4
        self.place = lax.axis_index("seq")
        self.lane = lax.axis_index("batch")
        self.nz = 4 if self.fast else self.seq
        self.span = width // self.nz
        self.part = self.rows // 2 if self.fast else self.rows
        self.groups = [[z * 2 + x for z in range(self.nz)] for x in range(2)]

    def half(self, bit):
        return (self.lane // bit) % 2

    def bases(self, bit):
        if not self.fast:
            return jnp.zeros((1,), jnp.int32)
        x, b = self.place % 2, self.half(bit)
        return jnp.stack(
            [(x ^ dx) * self.rows + (b ^ db) * self.part for db in range(2) for dx in range(2)]
        ).astype(jnp.int32)

    def gather(self, shard, bit):
        if not self.fast:
            return [lax.all_gather(shard, "seq", axis=0)]
        m, _, w = shard.shape
        mine = lax.dynamic_slice(shard, (0, self.half(bit) * self.part, 0), (m, self.part, w))
        near = lax.all_gather(mine, "seq", axis=0, axis_index_groups=self.groups)
        far = swap(near, "seq", 1, self.seq)
        return [near, far, swap(near, "batch", bit, 4), swap(far, "batch", bit, 4)]

    def reduce(self, keep, send, bit):
        if not self.fast:
            mine = lax.psum_scatter(keep, "seq", scatter_dimension=0)
            return mine
        got = swap(send, "batch", bit, 4)
        near = (keep[0].astype(F32) + got[0].astype(F32)).astype(BF)
        far = (keep[1].astype(F32) + got[1].astype(F32)).astype(BF)
        got = swap(far, "seq", 1, self.seq)
        near = (near.astype(F32) + got.astype(F32)).astype(BF)
        mine = lax.psum_scatter(
            near, "seq", scatter_dimension=0, axis_index_groups=self.groups
        )
        return mine

    def join(self, mine, bit):
        other = swap(mine, "batch", bit, 4)
        first = jnp.where(self.half(bit) == 0, mine, other)
        second = jnp.where(self.half(bit) == 0, other, mine)
        return jnp.concatenate([first, second], axis=1)


def assemble(plan, bit, pieces):
    nz, m, part, w = pieces[0].shape
    nb = len(pieces)

    def body(base_ref, *refs):
        ins, outs, sems = refs[:nb], refs[nb : nb + m], refs[nb + m]
        copies = []
        for b in range(nb):
            start = pl.multiple_of(base_ref[b], 16)
            for i in range(m):
                copies.append(
                    pltpu.make_async_copy(
                        ins[b].at[:, i], outs[i].at[:, pl.ds(start, part), :], sems.at[b, i]
                    )
                )
        for c in copies:
            c.start()
        for c in copies:
            c.wait()

    outs = pl.pallas_call(
        body,
        out_shape=[jax.ShapeDtypeStruct((nz, plan.span, w), BF)] * m,
        in_specs=[SMEM] + [ANY] * nb,
        out_specs=[ANY] * m,
        scratch_shapes=[pltpu.SemaphoreType.DMA((nb, m))],
        compiler_params=pltpu.CompilerParams(vmem_limit_bytes=LIMIT),
        name="assemble",
    )(plan.bases(bit), *pieces)
    return [o.reshape(nz * plan.span, w) for o in outs]


def ff_body(plan, nb, width, first, last, base_ref, nm_ref, up_ref, *refs):
    nz, span, part = plan.nz, plan.span, plan.part
    refs = list(refs)
    pieces = [refs.pop(0) for _ in range(nb)]
    carried = None if first else [refs.pop(0) for _ in range(2)]
    outs = [refs.pop(0) for _ in range(2 if nb > 1 else 1)]
    ends = [refs.pop(0) for _ in range(4 if last else 2)]
    weight, nm_t, up_t, grads, joined_s, left_s, right_s = [refs.pop(0) for _ in range(7)]
    totals = [refs.pop(0) for _ in range(2)] if last else ends
    in_sem, out_sem = refs
    mixed_ref, back_ref = totals
    d = nm_ref.shape[1]
    count = nm_ref.shape[0]
    starts = [pl.multiple_of(base_ref[b], 16) for b in range(nb)]
    tiles = [(s, min(256, width - s)) for s in range(0, width, 256)]

    def copy_in(t, b):
        cols = pl.ds(*tiles[t])
        return pltpu.make_async_copy(
            pieces[b].at[:, :, :, cols],
            weight.at[:, :, pl.ds(starts[b], part), cols],
            in_sem.at[t, b],
        )

    def copy_out(t, b):
        cols = pl.ds(*tiles[t])
        return pltpu.make_async_copy(
            grads.at[t % 2, :, :, pl.ds(starts[b], part), pl.ds(0, tiles[t][1])],
            outs[b // 2].at[b % 2, :, :, :, cols],
            out_sem.at[t % 2, b],
        )

    for t in range(len(tiles)):
        for b in range(nb):
            copy_in(t, b).start()

    def turn(i, _):
        rows = pl.ds(pl.multiple_of(i * 256, 256), 256)
        nm_t[:, rows] = nm_ref[rows, :].T
        up_t[:, rows] = up_ref[rows, :].T
        return 0

    lax.fori_loop(0, count // 256, turn, 0)

    for t, (start, size) in enumerate(tiles):
        cols = slice(start, start + size)
        for b in range(nb):
            copy_in(t, b).wait()

        def tokens(i, _, t=t, cols=cols, size=size):
            rows = pl.ds(pl.multiple_of(i * 256, 256), 256)
            left_w = weight[:, 0, :, cols].reshape(d, size)
            right_w = weight[:, 1, :, cols].reshape(d, size)
            down_w = weight[:, 2, :, cols].reshape(d, size)
            left = dot(nm_ref[rows, :], left_w)
            right = dot(nm_ref[rows, :], right_w)
            joined = (left * right).astype(BF)
            joined_back = dot(up_ref[rows, :], down_w)
            left_back = (joined_back * right).astype(BF)
            right_back = (joined_back * left).astype(BF)
            joined_s[rows, :size] = joined
            left_s[rows, :size] = left_back
            right_s[rows, :size] = right_back
            mixed = dot_nt(joined, down_w)
            back = dot_nt(left_back, left_w) + dot_nt(right_back, right_w)
            if t == 0 and first:
                mixed_ref[rows, :] = mixed
                back_ref[rows, :] = back
            elif t == 0:
                mixed_ref[rows, :] = carried[0][rows, :] + mixed
                back_ref[rows, :] = carried[1][rows, :] + back
            else:
                mixed_ref[rows, :] += mixed
                back_ref[rows, :] += back
            return 0

        lax.fori_loop(0, count // 256, tokens, 0)
        if t >= 2:
            for b in range(nb):
                copy_out(t - 2, b).wait()

        def features(i, _, t=t, size=size):
            rows = pl.ds(pl.multiple_of(i * 256, 256), 256)
            slabs = 256 // span
            at = pl.ds(i * slabs, slabs)
            nm_rows, up_rows = nm_t[rows, :], up_t[rows, :]
            for k, value in enumerate(
                (
                    dot(nm_rows, left_s[:, :size]),
                    dot(nm_rows, right_s[:, :size]),
                    dot(up_rows, joined_s[:, :size]),
                )
            ):
                grads[t % 2, at, k, :, :size] = value.astype(BF).reshape(slabs, span, size)
            return 0

        lax.fori_loop(0, d // 256, features, 0)
        for b in range(nb):
            copy_out(t, b).start()
    for t in range(max(0, len(tiles) - 2), len(tiles)):
        for b in range(nb):
            copy_out(t, b).wait()
    if last:
        half = count // 2
        for k in range(2):
            ends[2 * k][...] = totals[k][:half, :]
            ends[2 * k + 1][...] = totals[k][half:, :].astype(BF)


def feed_forward(plan, bit, pieces, nm, up, carry, last):
    nz, three, part, width = pieces[0].shape
    nb = len(pieces)
    count, d = nm.shape
    first = carry is None
    tiles = -(-width // 256)
    out_shape = [
        jax.ShapeDtypeStruct((2 if nb > 1 else 1, nz, three, part, width), BF)
    ] * (2 if nb > 1 else 1)
    if last:
        ends = [
            jax.ShapeDtypeStruct((count // 2, d), F32),
            jax.ShapeDtypeStruct((count // 2, d), BF),
        ] * 2
    else:
        ends = [jax.ShapeDtypeStruct((count, d), F32)] * 2
    scratch = [
        pltpu.VMEM((nz, three, plan.span, width), BF),
        pltpu.VMEM((d, count), BF),
        pltpu.VMEM((d, count), BF),
        pltpu.VMEM((2, nz, three, plan.span, 256), BF),
        pltpu.VMEM((count, 256), BF),
        pltpu.VMEM((count, 256), BF),
        pltpu.VMEM((count, 256), BF),
    ]
    if last:
        scratch += [pltpu.VMEM((count, d), F32)] * 2
    scratch += [pltpu.SemaphoreType.DMA((tiles, nb)), pltpu.SemaphoreType.DMA((2, nb))]
    got = pl.pallas_call(
        functools.partial(ff_body, plan, nb, width, first, last),
        out_shape=out_shape + ends,
        in_specs=[SMEM, VMEM, VMEM] + [ANY] * nb + ([] if first else [VMEM] * 2),
        out_specs=[ANY] * len(out_shape) + [VMEM] * len(ends),
        scratch_shapes=scratch,
        compiler_params=pltpu.CompilerParams(vmem_limit_bytes=LIMIT),
        cost_estimate=pl.CostEstimate(
            flops=18 * count * d * width, bytes_accessed=12 * d * width + 16 * d * count, transcendentals=0
        ),
        name="feed_forward",
    )(plan.bases(bit), nm, up, *pieces, *(carry or ()))
    return got[: len(out_shape)], got[len(out_shape) :]


def row_mask(segment_row):
    order = jnp.arange(segment_row.shape[0])
    return (
        (segment_row[:, None] == segment_row[None, :]) & (order[:, None] >= order[None, :])
    ).astype(F32)


def row_weights(query_row, keys_row, allowed):
    scores = jnp.einsum("thd,shd->hts", query_row, keys_row, preferred_element_type=F32)
    return (scores * allowed[None]).astype(BF)


def forward_row(item):
    query_row, keys_row, values_row, segment_row, state_low = item
    weights_low = row_weights(query_row, keys_row, row_mask(segment_row))
    inside = jnp.einsum("hts,shd->thd", weights_low, values_row, preferred_element_type=F32)
    inherit = (segment_row == 0).astype(BF)[:, None, None]
    carried = jnp.einsum("thd,hde->the", query_row * inherit, state_low, preferred_element_type=F32)
    return inside + carried


def backward_row(item):
    query_row, keys_row, values_row, segment_row, state_low, after_low, upstream_row = item
    allowed = row_mask(segment_row)
    weights_low = row_weights(query_row, keys_row, allowed)
    inherit = (segment_row == 0).astype(BF)[:, None, None]
    tail = segment_row == segment_row[-1]
    tail_values = values_row * tail.astype(BF)[:, None, None]
    score_back = (
        jnp.einsum("the,she->hts", upstream_row, values_row, preferred_element_type=F32)
        * allowed[None]
    ).astype(BF)
    values_back = jnp.einsum("hts,thd->shd", weights_low, upstream_row, preferred_element_type=F32)
    values_back = (
        values_back
        + jnp.einsum("hde,shd->she", after_low, keys_row, preferred_element_type=F32)
        * tail.astype(F32)[:, None, None]
    )
    query_back = jnp.einsum("hts,shd->thd", score_back, keys_row, preferred_element_type=F32)
    query_back = query_back + jnp.einsum(
        "the,hde->thd", upstream_row * inherit, state_low, preferred_element_type=F32
    )
    keys_back = jnp.einsum("hts,thd->shd", score_back, query_row, preferred_element_type=F32)
    keys_back = keys_back + jnp.einsum(
        "hde,she->shd", after_low, tail_values, preferred_element_type=F32
    )
    return (query_back, keys_back, values_back)


def chain(own, keep, order, size):
    shape = keep.shape + (1,) * (own.ndim - 1)
    total, before, all_kept, between = own, jnp.zeros_like(own), keep, jnp.ones_like(keep)
    step = 1
    while step < size:
        pairs = [
            (i, i + order * step) for i in range(size) if 0 <= i + order * step < size
        ]
        got = lax.ppermute(total.astype(BF), "seq", pairs).astype(F32)
        got_kept = lax.ppermute(all_kept, "seq", pairs)
        before = before + between.reshape(shape) * got
        if step * 2 < size:
            total = total + all_kept.reshape(shape) * got
        between = between * got_kept
        all_kept = all_kept * got_kept
        step *= 2
    return before


def shards(
    mesh_shape,
    tokens,
    starts,
    entry_gain,
    query_weight,
    key_weight,
    value_weight,
    gate_weight,
    head_gain,
    output_weight,
    middle_gain,
    left_weight,
    right_weight,
    down_weight,
    cotangent,
):
    rows_here, span, width = tokens.shape
    count = rows_here * span
    hidden = left_weight.shape[1]
    plan = Plan(mesh_shape, width)
    seq = plan.seq
    core = plan.half(1)

    pair_kv = plan.gather(jnp.stack([key_weight, value_weight]), 1)
    pair_qg = plan.gather(jnp.stack([query_weight, gate_weight]), 1)
    one_o = plan.gather(output_weight[None], 1)
    mine = hidden // 2
    cuts = [0, 768, mine]
    stack = lax.dynamic_slice(
        jnp.stack([left_weight, right_weight, down_weight.T]),
        (0, 0, core * mine),
        (3, plan.rows, mine),
    )
    ff_pieces = [plan.gather(stack[:, :, a:b], 2) for a, b in zip(cuts, cuts[1:])]
    upstream = cotangent.reshape(count, width)
    up_both = jnp.concatenate([upstream, swap(upstream, "batch", 1, plan.batch)])

    source = tokens.reshape(count, width).astype(F32)
    inverse_in = inverse_rms(source)
    normed_in = (source * inverse_in * entry_gain).astype(BF)
    key_full, value_full = assemble(plan, 1, pair_kv)
    key_linear = dot(normed_in, key_full)
    value_linear = dot(normed_in, value_full)
    shaped = (rows_here, span, HEADS, HEAD)
    keys = jax.nn.softplus(key_linear).astype(BF).reshape(shaped)
    values = value_linear.astype(BF).reshape(shaped)
    place = jnp.arange(span)
    segment = dot(starts.astype(BF), (place[:, None] <= place[None, :]).astype(BF)).astype(jnp.int32)
    last = segment[:, span - 1 :]
    tail = (segment == last).astype(BF)
    keep = (last[:, 0] == 0).astype(F32)
    inherit = (segment == 0).astype(BF)[:, :, None, None]
    fresh = jnp.einsum(
        "rshd,rshe->rhde", keys, values * tail[:, :, None, None], preferred_element_type=F32
    )
    state_low = chain(fresh, keep, 1, seq).astype(BF)
    query_full, gate_full = assemble(plan, 1, pair_qg)
    query_linear = dot(normed_in, query_full)
    gate_linear = dot(normed_in, gate_full)
    query = jax.nn.softplus(query_linear).astype(BF).reshape(shaped)
    gate = jax.nn.sigmoid(gate_linear)
    attended = lax.map(forward_row, (query, keys, values, segment, state_low))
    inverse_head = inverse_rms(attended)
    head_shaped = head_gain.reshape(HEADS, HEAD)
    headed = (attended * inverse_head * head_shaped).reshape(count, width)
    gated = (headed * gate).astype(BF)
    (output_full,) = assemble(plan, 1, one_o)
    middle = source + dot(gated, output_full)
    inverse_mid = inverse_rms(middle)
    normed_mid = (middle * inverse_mid * middle_gain).astype(BF)

    nm_both = jnp.concatenate([normed_mid, swap(normed_mid, "batch", 1, plan.batch)])
    carry, terms = None, []
    for i, pieces in enumerate(ff_pieces):
        term, carry = feed_forward(plan, 2, pieces, nm_both, up_both, carry, i == len(ff_pieces) - 1)
        terms.append(term)
    mixed_own, mixed_send, back_own, back_send = carry
    normed_mid_back = back_own + swap(back_send, "batch", 1, plan.batch).astype(F32)
    mixed = (
        (middle + (mixed_own + swap(mixed_send, "batch", 1, plan.batch).astype(F32)))
        .astype(BF)
        .reshape(tokens.shape)
    )

    middle_back, middle_term = norm_back(normed_mid_back, middle, inverse_mid, middle_gain)
    middle_back = middle_back + upstream.astype(F32)
    branch_back = middle_back.astype(BF)
    output_term = dot_tn(gated, branch_back)
    gated_back = dot_nt(branch_back, output_full)
    gate_linear_back = (gated_back * headed * gate * (1.0 - gate)).astype(BF)
    attended_grad, head_part = norm_back(
        (gated_back * gate).reshape(count, HEADS, HEAD),
        attended.reshape(count, HEADS, HEAD),
        inverse_head.reshape(count, HEADS, 1),
        head_shaped,
    )
    head_term = head_part.reshape(width)
    attended_back = attended_grad.astype(BF).reshape(shaped)
    direct = jnp.einsum("rthd,rthe->rhde", query * inherit, attended_back, preferred_element_type=F32)
    after_low = chain(direct, keep, -1, seq).astype(BF)
    query_back, keys_back, values_back = lax.map(
        backward_row, (query, keys, values, segment, state_low, after_low, attended_back)
    )
    query_linear_back = (query_back.reshape(count, width) * jax.nn.sigmoid(query_linear)).astype(BF)
    key_linear_back = (keys_back.reshape(count, width) * jax.nn.sigmoid(key_linear)).astype(BF)
    value_linear_back = values_back.reshape(count, width).astype(BF)
    query_term = dot_tn(normed_in, query_linear_back)
    key_term = dot_tn(normed_in, key_linear_back)
    value_term = dot_tn(normed_in, value_linear_back)
    gate_term = dot_tn(normed_in, gate_linear_back)
    normed_in_back = dot_nt(query_linear_back, query_full) + dot_nt(key_linear_back, key_full)
    normed_in_back = (
        normed_in_back + dot_nt(value_linear_back, value_full) + dot_nt(gate_linear_back, gate_full)
    )
    input_back, entry_term = norm_back(normed_in_back, source, inverse_in, entry_gain)
    input_gradient = (input_back + middle_back).reshape(tokens.shape)

    def square_sum(term_list):
        m = len(term_list)
        whole = jnp.stack([t.astype(BF) for t in term_list])
        if not plan.fast:
            whole = whole.reshape(m, plan.nz, plan.span, width).swapaxes(0, 1)
            part = plan.reduce(whole, None, 1)
            return lax.psum(part, "batch").astype(F32)
        whole = whole.reshape(m, 4, 2, 2, plan.part, width).transpose(3, 2, 1, 0, 4, 5)
        x = plan.place % 2

        def side(db):
            half = lax.dynamic_index_in_dim(whole, core ^ db, 0, keepdims=False)
            return jnp.stack(
                [lax.dynamic_index_in_dim(half, x ^ dx, 0, keepdims=False) for dx in range(2)]
            )

        part = plan.reduce(side(0), side(1), 1)
        part = (part.astype(F32) + swap(part, "batch", 2, 4).astype(F32)).astype(BF)
        return plan.join(part, 1).astype(F32)

    wide = []
    for term in terms:
        if plan.fast:
            wide.append(plan.join(plan.reduce(term[0], term[1], 2), 2))
        else:
            part = plan.reduce(term[0][0], None, 2)
            groups = [[i for i in range(plan.batch) if i % 2 == c] for c in range(2)]
            wide.append(lax.psum(part, "batch", axis_index_groups=groups))
    wide = jnp.concatenate(wide, axis=2)
    other = swap(wide, "batch", 1, plan.batch)
    wide = jnp.concatenate(
        [jnp.where(core == 0, wide, other), jnp.where(core == 0, other, wide)], axis=2
    ).astype(F32)
    left_total, right_total, down_total = wide[0], wide[1], wide[2].T
    (output_total, gate_total) = square_sum([output_term, gate_term])
    (query_total, key_total, value_total) = square_sum([query_term, key_term, value_term])
    gains = lax.psum(jnp.stack([entry_term, head_term, middle_term]), ("seq", "batch"))
    gains = lax.dynamic_slice(gains, (0, plan.place * plan.rows), (3, plan.rows))
    return (
        mixed,
        input_gradient,
        gains[0],
        query_total,
        key_total,
        value_total,
        gate_total,
        gains[1],
        output_total,
        gains[2],
        left_total,
        right_total,
        down_total,
    )


def solution(mesh):
    row, cut, wide = P("batch", "seq", None), P("seq", None), P(None, "seq")
    in_specs = (row, P("batch", "seq"), P(), cut, cut, cut, cut, P(), cut, P(), cut, cut, wide, row)
    out_specs = (row, row, P("seq"), cut, cut, cut, cut, P("seq"), cut, P("seq"), cut, cut, wide)
    return jax.shard_map(
        functools.partial(shards, dict(mesh.shape)),
        mesh=mesh,
        in_specs=in_specs,
        out_specs=out_specs,
        check_vma=False,
    )
```

```python
import functools

import jax
import jax.numpy as jnp
from jax import lax
from jax.experimental import pallas as pl
from jax.experimental.pallas import tpu as pltpu
from jax.sharding import PartitionSpec as P

HEADS = 16
HEAD = 64
EPSILON = 1e-06
BF = jnp.bfloat16
F32 = jnp.float32
VMEM = pl.BlockSpec(memory_space=pltpu.VMEM)
SMEM = pl.BlockSpec(memory_space=pltpu.SMEM)
ANY = pl.BlockSpec(memory_space=pl.ANY)
LIMIT = 60 * 1024 * 1024
LIGHT = pl.CostEstimate(flops=1, bytes_accessed=1, transcendentals=0)


def inverse_rms(values):
    return lax.rsqrt(jnp.mean(values * values, axis=-1, keepdims=True) + EPSILON)


def dot(left, right):
    return jnp.dot(left, right, preferred_element_type=F32)


def dot_nt(left, right):
    return lax.dot_general(left, right, (((1,), (1,)), ((), ())), preferred_element_type=F32)


def dot_tn(left, right):
    return lax.dot_general(left, right, (((0,), (0,)), ((), ())), preferred_element_type=F32)


def swap(value, axis, bit, size):
    return lax.ppermute(value, axis, [(i, i ^ bit) for i in range(size)])


def tie(value, *others):
    return lax.optimization_barrier((value,) + others)[0]


class Plan:
    def __init__(self, mesh_shape, width):
        self.seq = mesh_shape["seq"]
        self.batch = mesh_shape["batch"]
        self.rows = width // self.seq
        self.fast = self.seq == 8 and self.batch == 4
        self.place = lax.axis_index("seq")
        self.lane = lax.axis_index("batch")
        self.nz = 4 if self.fast else self.seq
        self.span = width // self.nz
        self.groups = [[z * 2 + x for z in range(self.nz)] for x in range(2)]

    def half(self, bit):
        return (self.lane // bit) % 2

    def bases(self, bits):
        first = jnp.zeros((1,), jnp.int32)
        if self.fast:
            size = self.rows
            x = self.place % 2
            first = jnp.stack([x * size, (1 - x) * size])
            for bit in bits:
                size //= 2
                mine = self.half(bit)
                first = jnp.concatenate([first + mine * size, first + (1 - mine) * size])
        return first.astype(jnp.int32)

    def mine(self, shard, bits):
        if self.fast:
            for bit in bits:
                m, rows, w = shard.shape
                shard = lax.dynamic_slice(shard, (0, self.half(bit) * (rows // 2), 0), (m, rows // 2, w))
        return shard

    def along(self, mine, direct):
        if not self.fast:
            return lax.all_gather(mine, "seq", axis=0)
        if direct:
            copies = jnp.broadcast_to(mine[None], (self.nz,) + mine.shape)
            return lax.all_to_all(copies, "seq", 0, 0, axis_index_groups=self.groups)
        return lax.all_gather(mine, "seq", axis=0, axis_index_groups=self.groups)

    def across(self, near):
        return [near, swap(near, "seq", 1, self.seq)] if self.fast else [near]

    def pair(self, pieces, bit):
        return pieces + [swap(p, "batch", bit, 4) for p in pieces] if self.fast else pieces

    def sum_along(self, near):
        return lax.psum_scatter(near, "seq", scatter_dimension=0, axis_index_groups=self.groups)

    def join(self, mine, bit, axis):
        other = swap(mine, "batch", bit, self.batch)
        lower = self.half(bit) == 0
        return jnp.concatenate([jnp.where(lower, mine, other), jnp.where(lower, other, mine)], axis=axis)


def add(left, right):
    return (left.astype(F32) + right.astype(F32)).astype(BF)


def params(mib):
    return pltpu.CompilerParams(vmem_limit_bytes=mib * 1024 * 1024)


def low_lanes():
    return lax.broadcasted_iota(jnp.int32, (1, 128), 1) < HEAD


def spread(state):
    low = low_lanes()
    zero = jnp.zeros_like(state)
    return jnp.concatenate([jnp.where(low, state, zero), jnp.where(low, zero, state)], axis=0)


def squeeze(full):
    return jnp.where(low_lanes(), full[:HEAD], full[HEAD:])


def head_sums(values):
    row = lax.broadcasted_iota(jnp.int32, (128, 128), 0) < HEAD
    col = lax.broadcasted_iota(jnp.int32, (128, 128), 1) < HEAD
    ones = (row == col).astype(BF)
    high = values.astype(BF)
    rest = values - high.astype(F32)
    mid = rest.astype(BF)
    return dot(high, ones) + dot(mid, ones)


def block(i, size=256):
    return pl.ds(pl.multiple_of(i * size, size), size)


def fetch(base_ref, pieces, weight, sem, picks):
    return [
        [
            pltpu.make_async_copy(
                piece.at[:, pick],
                weight.at[:, k, pl.ds(pl.multiple_of(base_ref[b], 16), piece.shape[2]), :],
                sem.at[k, b],
            )
            for b, piece in enumerate(pieces)
        ]
        for k, pick in enumerate(picks)
    ]


def hand_out(base_ref, grads, outs, sem):
    m = grads.shape[1]
    return [
        [
            pltpu.make_async_copy(
                grads.at[:, k, pl.ds(pl.multiple_of(base_ref[b], 16), out.shape[-2]), :],
                out.at[:, k],
                sem.at[k, b],
            )
            for b, out in enumerate(outs)
        ]
        for k in range(m)
    ]


def piece_shapes(plan, m, part, w, count):
    return [jax.ShapeDtypeStruct((plan.nz, m, part, w), BF)] * (count if plan.fast else 1)


def start_all(copies):
    for c in copies:
        c.start()


def wait_all(copies):
    for c in copies:
        c.wait()


def soft(x):
    e = jnp.exp(-jnp.abs(x))
    return jnp.maximum(x, 0.0) + jnp.log1p(e), jnp.where(x >= 0.0, 1.0, e) / (1.0 + e)


def kv_body(plan, nb, base_ref, tokens_ref, gain_ref, tail_ref, *refs):
    pieces = refs[:nb]
    normed_ref, keys_ref, sig_ref, values_ref, fresh_ref, weight, sem = refs[nb:]
    d = tokens_ref.shape[1]
    copies = fetch(base_ref, pieces, weight, sem, (0, 1))
    for c in copies:
        start_all(c)

    def norm(i, _):
        source = tokens_ref[block(i), :].astype(F32)
        normed_ref[block(i), :] = (source * inverse_rms(source) * gain_ref[...]).astype(BF)
        return 0

    lax.fori_loop(0, 2, norm, 0)
    wait_all(copies[0])

    def key_part(j, _):
        linear = dot(normed_ref[...], weight[:, 0, :, block(j)].reshape(d, 256))
        plus, sig = soft(linear)
        keys_ref[:, block(j)] = plus.astype(BF)
        sig_ref[:, block(j)] = sig.astype(BF)
        return 0

    lax.fori_loop(0, d // 256, key_part, 0)
    wait_all(copies[1])

    def value_part(j, _):
        linear = dot(normed_ref[...], weight[:, 1, :, block(j)].reshape(d, 256))
        values_ref[:, block(j)] = linear.astype(BF)
        return 0

    lax.fori_loop(0, d // 256, value_part, 0)

    def states(i, _):
        rows, lanes = block(i // 8), block(i % 8, 128)
        tail = tail_ref[rows, :].astype(BF)
        fresh_ref[i] = squeeze(dot_tn(keys_ref[rows, lanes], values_ref[rows, lanes] * tail))
        return 0

    lax.fori_loop(0, 16, states, 0, unroll=2)


def kv_call(plan, bases, tokens, gain, tail, pieces):
    nb = len(pieces)
    count, d = tokens.shape
    shape = jax.ShapeDtypeStruct((count, d), BF)
    return pl.pallas_call(
        functools.partial(kv_body, plan, nb),
        out_shape=[shape] * 4 + [jax.ShapeDtypeStruct((16, HEAD, 128), F32)],
        in_specs=[SMEM] + [VMEM] * 3 + [ANY] * nb,
        out_specs=[VMEM] * 5,
        scratch_shapes=[
            pltpu.VMEM((plan.nz, 2, plan.span, d), BF),
            pltpu.SemaphoreType.DMA((2, nb)),
        ],
        compiler_params=params(24),
        cost_estimate=LIGHT,
        name="keys_values",
    )(bases, tokens, gain, tail, *pieces)


def qg_body(plan, nb, base_ref, normed_ref, *refs):
    pieces = refs[:nb]
    query_ref, sig_ref, gate_ref, weight, sem = refs[nb:]
    d = normed_ref.shape[1]
    copies = fetch(base_ref, pieces, weight, sem, (0, 1))
    for c in copies:
        start_all(c)
    wait_all(copies[0])

    def query_part(j, _):
        linear = dot(normed_ref[...], weight[:, 0, :, block(j)].reshape(d, 256))
        plus, sig = soft(linear)
        query_ref[:, block(j)] = plus.astype(BF)
        sig_ref[:, block(j)] = sig.astype(BF)
        return 0

    lax.fori_loop(0, d // 256, query_part, 0)
    wait_all(copies[1])

    def gate_part(j, _):
        linear = dot(normed_ref[...], weight[:, 1, :, block(j)].reshape(d, 256))
        gate_ref[:, block(j)] = jax.nn.sigmoid(linear)
        return 0

    lax.fori_loop(0, d // 256, gate_part, 0)


def qg_call(plan, bases, normed, pieces):
    nb = len(pieces)
    count, d = normed.shape
    shape = jax.ShapeDtypeStruct((count, d), BF)
    return pl.pallas_call(
        functools.partial(qg_body, plan, nb),
        out_shape=[shape, shape, jax.ShapeDtypeStruct((count, d), F32)],
        in_specs=[SMEM, VMEM] + [ANY] * nb,
        out_specs=[VMEM] * 3,
        scratch_shapes=[
            pltpu.VMEM((plan.nz, 2, plan.span, d), BF),
            pltpu.SemaphoreType.DMA((2, nb)),
        ],
        compiler_params=params(24),
        cost_estimate=LIGHT,
        name="query_gate",
    )(bases, normed, *pieces)


def pair_mask(segcol_ref, segrow_ref, r):
    t = lax.broadcasted_iota(jnp.int32, (256, 256), 0)
    s = lax.broadcasted_iota(jnp.int32, (256, 256), 1)
    return (segcol_ref[block(r), :] == segrow_ref[r]) & (t >= s)


def attend_body(
    plan, nb, base_ref, query_ref, keys_ref, values_ref, gate_ref, state_ref, segcol_ref, segrow_ref,
    gain_ref, tokens_ref, midgain_ref, *refs
):
    pieces = refs[:nb]
    attended_ref, gated_ref, middle_ref, normed_ref, mask_ref, weight, sem = refs[nb:]
    d = query_ref.shape[1]
    (copies,) = fetch(base_ref, pieces, weight, sem, (2,))
    start_all(copies)
    for r in range(2):
        mask_ref[r] = pair_mask(segcol_ref, segrow_ref, r).astype(F32)

    def pair(i, _):
        r = i // 8
        rows, lanes = block(r), block(i % 8, 128)
        low = low_lanes()
        mask = mask_ref[r]
        q, k, v = query_ref[rows, lanes], keys_ref[rows, lanes], values_ref[rows, lanes]
        zero = jnp.zeros_like(q)
        inherit = (segcol_ref[rows, :] == 0.0).astype(BF)
        q0, q1 = jnp.where(low, q, zero), jnp.where(low, zero, q)
        w0 = (dot_nt(q0, k) * mask).astype(BF)
        w1 = (dot_nt(q1, k) * mask).astype(BF)
        carried = dot(q * inherit, spread(state_ref[i]))
        attended = jnp.where(low, dot(w0, v), dot(w1, v)) + carried
        inverse = lax.rsqrt(head_sums(attended * attended) * (1.0 / HEAD) + EPSILON)
        headed = attended * inverse * gain_ref[:, lanes]
        attended_ref[rows, lanes] = attended
        gated_ref[rows, lanes] = (headed * gate_ref[rows, lanes]).astype(BF)
        return 0

    lax.fori_loop(0, 16, pair, 0, unroll=2)
    wait_all(copies)

    def project(j, _):
        out = dot(gated_ref[...], weight[:, 0, :, block(j)].reshape(d, 256))
        middle_ref[:, block(j)] = tokens_ref[:, block(j)].astype(F32) + out
        return 0

    lax.fori_loop(0, d // 256, project, 0)

    def norm(i, _):
        middle = middle_ref[block(i), :]
        normed_ref[block(i), :] = (middle * inverse_rms(middle) * midgain_ref[...]).astype(BF)
        return 0

    lax.fori_loop(0, 2, norm, 0)


def attend_call(plan, bases, query, keys, values, gate, state, segcol, segrow, gain, tokens, midgain, pieces):
    nb = len(pieces)
    count, d = query.shape
    low, high = jax.ShapeDtypeStruct((count, d), BF), jax.ShapeDtypeStruct((count, d), F32)
    return pl.pallas_call(
        functools.partial(attend_body, plan, nb),
        out_shape=[high, low, high, low],
        in_specs=[SMEM] + [VMEM] * 10 + [ANY] * nb,
        out_specs=[VMEM] * 4,
        scratch_shapes=[
            pltpu.VMEM((2, 256, 256), F32),
            pltpu.VMEM((plan.nz, 1, plan.span, d), BF),
            pltpu.SemaphoreType.DMA((1, nb)),
        ],
        compiler_params=params(28),
        cost_estimate=LIGHT,
        name="attend",
    )(bases, query, keys, values, gate, state, segcol, segrow, gain, tokens, midgain, *pieces)


def mid_body(
    plan, nb, base_ref, back_ref, got_ref, middle_ref, midgain_ref, upstream_ref, gate_ref, attended_ref,
    gain_ref, query_ref, segcol_ref, *refs
):
    pieces = refs[:nb]
    midback_ref, branch_ref, gateback_ref, attback_ref, direct_ref, gains_ref, gated_back, weight, sem = refs[nb:]
    d = query_ref.shape[1]
    (copies,) = fetch(base_ref, pieces, weight, sem, (2,))
    start_all(copies)

    def norm(i, total):
        rows = block(i, 128)
        dy = back_ref[rows, :].astype(F32) + got_ref[rows, :].astype(F32)
        v = middle_ref[rows, :]
        r = inverse_rms(v)
        scaled = dy * midgain_ref[...]
        mean = jnp.mean(scaled * v, axis=-1, keepdims=True)
        back = upstream_ref[rows, :].astype(F32) + r * scaled - v * (r * r * r * mean)
        midback_ref[rows, :] = back
        branch_ref[rows, :] = back.astype(BF)
        return total + jnp.sum(dy * v * r, axis=0, keepdims=True)

    gains_ref[0:1, :] = lax.fori_loop(0, 4, norm, jnp.zeros((1, d), F32))
    wait_all(copies)

    slabs = 256 // plan.span

    def through(j, _):
        out_w = weight[pl.ds(j * slabs, slabs), 0].reshape(256, d)
        gated_back[:, block(j)] = dot_nt(branch_ref[...], out_w)
        return 0

    lax.fori_loop(0, d // 256, through, 0)

    def pair(p, _):
        lanes = block(p, 128)
        gain = gain_ref[:, lanes]
        total = jnp.zeros((1, 128), F32)
        for r in range(2):
            rows = pl.ds(r * 256, 256)
            att = attended_ref[rows, lanes]
            inverse = lax.rsqrt(head_sums(att * att) * (1.0 / HEAD) + EPSILON)
            gate = gate_ref[rows, lanes]
            back = gated_back[rows, lanes]
            unit = att * inverse
            gateback_ref[rows, lanes] = (back * (unit * gain) * gate * (1.0 - gate)).astype(BF)
            dy = back * gate
            total = total + jnp.sum(dy * unit, axis=0, keepdims=True)
            scaled = dy * gain
            mean = head_sums(scaled * unit) * (1.0 / HEAD)
            attback = (inverse * (scaled - unit * mean)).astype(BF)
            attback_ref[rows, lanes] = attback
            inherit = (segcol_ref[rows, :] == 0.0).astype(BF)
            direct_ref[r * 8 + p] = squeeze(dot_tn(query_ref[rows, lanes] * inherit, attback))
        gains_ref[1:2, lanes] = total
        return 0

    lax.fori_loop(0, 8, pair, 0)


def mid_call(plan, bases, back, got, middle, midgain, upstream, gate, attended, gain, query, segcol, pieces):
    nb = len(pieces)
    count, d = query.shape
    low, high = jax.ShapeDtypeStruct((count, d), BF), jax.ShapeDtypeStruct((count, d), F32)
    return pl.pallas_call(
        functools.partial(mid_body, plan, nb),
        out_shape=[
            high, low, low, low,
            jax.ShapeDtypeStruct((16, HEAD, 128), F32),
            jax.ShapeDtypeStruct((2, d), F32),
        ],
        in_specs=[SMEM] + [VMEM] * 10 + [ANY] * nb,
        out_specs=[VMEM] * 6,
        scratch_shapes=[
            pltpu.VMEM((count, d), F32),
            pltpu.VMEM((plan.nz, 1, plan.span, d), BF),
            pltpu.SemaphoreType.DMA((1, nb)),
        ],
        compiler_params=params(32),
        cost_estimate=LIGHT,
        name="middle_back",
    )(bases, back, got, middle, midgain, upstream, gate, attended, gain, query, segcol, *pieces)


def turn_rows(source_ref, turned):
    def turn(i, _):
        turned[block(i), :] = source_ref[:, block(i)].T
        return 0

    lax.fori_loop(0, source_ref.shape[1] // 256, turn, 0)


def gradient_rows(plan, turned, right_ref, grads, k):
    d = turned.shape[0]
    slabs = 256 // plan.span

    def features(i, _):
        value = dot(turned[block(i), :], right_ref[...]).astype(BF)
        grads[pl.ds(i * slabs, slabs), k] = value.reshape(slabs, plan.span, d)
        return 0

    lax.fori_loop(0, d // 256, features, 0)


def grads_body(plan, which, base_ref, *refs):
    m, n = len(which), max(which) + 1
    lefts, rights = refs[:n], refs[n : n + m]
    outs = refs[n + m : -3]
    turned, grads, sem = refs[-3:]
    copies = hand_out(base_ref, grads, outs, sem)
    for k in range(m):
        if k == 0 or which[k] != which[k - 1]:
            turn_rows(lefts[which[k]], turned)
        gradient_rows(plan, turned, rights[k], grads, k)
        start_all(copies[k])
    for k in range(m):
        wait_all(copies[k])


def grads_call(plan, bases, lefts, which, rights):
    m = len(rights)
    count, d = lefts[0].shape
    outs = piece_shapes(plan, m, plan.rows // 2 if plan.fast else plan.rows, d, 4)
    return pl.pallas_call(
        functools.partial(grads_body, plan, which),
        out_shape=outs,
        in_specs=[SMEM] + [VMEM] * (len(lefts) + m),
        out_specs=[ANY] * len(outs),
        scratch_shapes=[
            pltpu.VMEM((d, count), BF),
            pltpu.VMEM((plan.nz, m, plan.span, d), BF),
            pltpu.SemaphoreType.DMA((m, len(outs))),
        ],
        compiler_params=params(24),
        cost_estimate=LIGHT,
        name="square_gradients",
    )(bases, *lefts, *rights)


def inner_body(
    plan, query_ref, keys_ref, values_ref, qsig_ref, attback_ref, state_ref, segcol_ref, segrow_ref,
    qback_ref, kin_ref, vin_ref, mask_ref, turn_ref
):
    for r in range(2):
        mask = pair_mask(segcol_ref, segrow_ref, r).astype(F32)
        mask_ref[r] = mask
        turn_ref[r] = mask.T

    def pair(i, _):
        r = i // 8
        rows, lanes = block(r), block(i % 8, 128)
        low = low_lanes()
        mask, mask_t = mask_ref[r], turn_ref[r]
        q, k, v, ab = (x[rows, lanes] for x in (query_ref, keys_ref, values_ref, attback_ref))
        zero = jnp.zeros_like(q)
        inherit = (segcol_ref[rows, :] == 0.0).astype(BF)
        halves = []
        for h in range(2):
            pick = (lambda x: jnp.where(low, x, zero)) if h == 0 else (lambda x: jnp.where(low, zero, x))
            k_h, v_h, ab_h = pick(k), pick(v), pick(ab)
            w_t = (dot_nt(k_h, q) * mask_t).astype(BF)
            sb = (dot_nt(ab_h, v) * mask).astype(BF)
            sb_t = (dot_nt(v_h, ab) * mask_t).astype(BF)
            halves.append((dot(sb, k), dot(sb_t, q), dot(w_t, ab)))
        qb, kb, vb = (jnp.where(low, a, b) for a, b in zip(*halves))
        qb = qb + dot_nt(ab * inherit, spread(state_ref[i]))
        qback_ref[rows, lanes] = (qb * qsig_ref[rows, lanes].astype(F32)).astype(BF)
        kin_ref[rows, lanes] = kb
        vin_ref[rows, lanes] = vb
        return 0

    lax.fori_loop(0, 16, pair, 0)


def inner_call(plan, query, keys, values, qsig, attback, state, segcol, segrow):
    count, d = query.shape
    low, high = jax.ShapeDtypeStruct((count, d), BF), jax.ShapeDtypeStruct((count, d), F32)
    return pl.pallas_call(
        functools.partial(inner_body, plan),
        out_shape=[low, high, high],
        in_specs=[VMEM] * 8,
        out_specs=[VMEM] * 3,
        scratch_shapes=[pltpu.VMEM((2, 256, 256), F32), pltpu.VMEM((2, 256, 256), F32)],
        compiler_params=params(20),
        cost_estimate=LIGHT,
        name="attend_back",
    )(query, keys, values, qsig, attback, state, segcol, segrow)


def outer_body(
    plan, sides, base_ref, keys_ref, values_ref, ksig_ref, kin_ref, vin_ref, after_ref, segcol_ref, segrow_ref,
    normed_ref, *refs
):
    outs = refs[:sides]
    kback_ref, vback_ref, turned, grads, sem = refs[sides:]
    copies = hand_out(base_ref, grads, outs, sem)

    def pair(i, _):
        r = i // 8
        rows, lanes = block(r), block(i % 8, 128)
        tail = (segcol_ref[rows, :] == segrow_ref[r][:, 255:256]).astype(F32)
        after = spread(after_ref[i])
        kb = kin_ref[rows, lanes] + dot_nt(values_ref[rows, lanes], after) * tail
        vb = vin_ref[rows, lanes] + dot(keys_ref[rows, lanes], after) * tail
        kback_ref[rows, lanes] = (kb * ksig_ref[rows, lanes].astype(F32)).astype(BF)
        vback_ref[rows, lanes] = vb.astype(BF)
        return 0

    lax.fori_loop(0, 16, pair, 0, unroll=2)
    turn_rows(normed_ref, turned)
    for k, right in enumerate((kback_ref, vback_ref)):
        gradient_rows(plan, turned, right, grads, k)
        start_all(copies[k])
    for k in range(2):
        wait_all(copies[k])


def outer_call(plan, bases, keys, values, ksig, kin, vin, after, segcol, segrow, normed):
    count, d = keys.shape
    outs = piece_shapes(plan, 2, plan.rows // 2 if plan.fast else plan.rows, d, 4)
    low = jax.ShapeDtypeStruct((count, d), BF)
    got = pl.pallas_call(
        functools.partial(outer_body, plan, len(outs)),
        out_shape=outs + [low] * 2,
        in_specs=[SMEM] + [VMEM] * 9,
        out_specs=[ANY] * len(outs) + [VMEM] * 2,
        scratch_shapes=[
            pltpu.VMEM((d, count), BF),
            pltpu.VMEM((plan.nz, 2, plan.span, d), BF),
            pltpu.SemaphoreType.DMA((2, len(outs))),
        ],
        compiler_params=params(24),
        cost_estimate=LIGHT,
        name="key_value_gradients",
    )(bases, keys, values, ksig, kin, vin, after, segcol, segrow, normed)
    return got[: len(outs)], got[len(outs) :]


def entry_body(plan, nb, base_ref, tokens_ref, gain_ref, midback_ref, qb_ref, kb_ref, vb_ref, gb_ref, *refs):
    kv, qg = refs[:nb], refs[nb : 2 * nb]
    out_ref, gains_ref, total, weight, more, sem = refs[2 * nb :]
    d = tokens_ref.shape[1]
    copies = fetch(base_ref, qg, weight, sem.at[0], (0, 1)) + fetch(
        base_ref, kv, more, sem.at[1], (0, 1)
    )
    for c in copies:
        start_all(c)
    slabs = 256 // plan.span
    for c, (back, scr, k) in zip(
        copies, ((qb_ref, weight, 0), (gb_ref, weight, 1), (kb_ref, more, 0), (vb_ref, more, 1))
    ):
        wait_all(c)
        first = back is qb_ref

        def through(j, _, back=back, scr=scr, k=k, first=first):
            rows_w = scr[pl.ds(j * slabs, slabs), k].reshape(256, d)
            value = dot_nt(back[...], rows_w)
            if first:
                total[:, block(j)] = value
            else:
                total[:, block(j)] += value
            return 0

        lax.fori_loop(0, d // 256, through, 0)

    def norm(i, gains):
        rows = block(i, 128)
        dy = total[rows, :]
        v = tokens_ref[rows, :].astype(F32)
        r = inverse_rms(v)
        scaled = dy * gain_ref[...]
        mean = jnp.mean(scaled * v, axis=-1, keepdims=True)
        out_ref[rows, :] = midback_ref[rows, :] + r * scaled - v * (r * r * r * mean)
        return gains + jnp.sum(dy * v * r, axis=0, keepdims=True)

    gains_ref[...] = lax.fori_loop(0, 4, norm, jnp.zeros((1, d), F32))


def entry_call(plan, bases, tokens, gain, midback, qb, kb, vb, gb, kv, qg):
    nb = len(kv)
    count, d = tokens.shape
    return pl.pallas_call(
        functools.partial(entry_body, plan, nb),
        out_shape=[jax.ShapeDtypeStruct((count, d), F32), jax.ShapeDtypeStruct((1, d), F32)],
        in_specs=[SMEM] + [VMEM] * 7 + [ANY] * (2 * nb),
        out_specs=[VMEM] * 2,
        scratch_shapes=[
            pltpu.VMEM((count, d), F32),
            pltpu.VMEM((plan.nz, 2, plan.span, d), BF),
            pltpu.VMEM((plan.nz, 2, plan.span, d), BF),
            pltpu.SemaphoreType.DMA((2, 2, nb)),
        ],
        compiler_params=params(32),
        cost_estimate=LIGHT,
        name="entry_back",
    )(bases, tokens, gain, midback, qb, kb, vb, gb, *kv, *qg)


def blocks(base_ref, pieces, whole, sem, inward):
    d = whole.shape[2]
    copies = []
    for k in range(3):
        copies.append([])
        for b, piece in enumerate(pieces):
            n = piece.shape[0]
            for z in range(n):
                lanes = pl.ds(pl.multiple_of(base_ref[b] + z * (d // n), 128), 128)
                ends = (piece.at[z, k], whole.at[k, :, lanes])
                copies[-1].append(pltpu.make_async_copy(*(ends if inward else ends[::-1]), sem.at[k, b, z]))
    return copies


def ff_body(nb, base_ref, nm0_ref, nm1_ref, up0_ref, up1_ref, *refs):
    pieces = refs[:nb]
    mixed_ref, back_ref, joined_t, left_t, right_t, weight, joined_s, left_s, right_s, sem = refs[nb:]
    count, d = nm0_ref.shape
    hidden = weight.shape[1]
    copies = blocks(base_ref, pieces, weight, sem, True)
    for c in copies:
        start_all(c)
    for c in copies:
        wait_all(c)
    for h, (nm_ref, up_ref) in enumerate(((nm0_ref, up0_ref), (nm1_ref, up1_ref))):
        rows = pl.ds(h * count, count)
        for start in range(0, hidden, 256):
            some = slice(start, min(start + 256, hidden))
            left = dot_nt(nm_ref[...], weight[0, some, :])
            right = dot_nt(nm_ref[...], weight[1, some, :])
            joined_back = dot_nt(up_ref[...], weight[2, some, :])
            for value, straight, turned in (
                (left * right, joined_s, joined_t),
                (joined_back * right, left_s, left_t),
                (joined_back * left, right_s, right_t),
            ):
                value = value.astype(BF)
                straight[rows, some] = value
                turned[some, rows] = value.T

    def through(j, _):
        for h in range(2):
            rows = pl.ds(h * count, count)
            mixed_ref[rows, block(j)] = dot(joined_s[rows, :], weight[2, :, block(j)]).astype(BF)
            back = dot(left_s[rows, :], weight[0, :, block(j)]) + dot(right_s[rows, :], weight[1, :, block(j)])
            back_ref[rows, block(j)] = back.astype(BF)
        return 0

    lax.fori_loop(0, d // 256, through, 0)


def ff_call(bases, nm, up, pieces):
    nb = len(pieces)
    n, three, hidden, _ = pieces[0].shape
    count, d = nm[0].shape
    whole, some = jax.ShapeDtypeStruct((2 * count, d), BF), jax.ShapeDtypeStruct((hidden, 2 * count), BF)
    return pl.pallas_call(
        functools.partial(ff_body, nb),
        out_shape=[whole, whole, some, some, some],
        in_specs=[SMEM] + [VMEM] * 4 + [ANY] * nb,
        out_specs=[VMEM] * 5,
        scratch_shapes=[pltpu.VMEM((three, hidden, d), BF)]
        + [pltpu.VMEM((2 * count, hidden), BF)] * 3
        + [pltpu.SemaphoreType.DMA((3, nb, n))],
        compiler_params=params(40),
        cost_estimate=LIGHT,
        name="feed_forward",
    )(bases, *nm, *up, *pieces)


def ffgrad_body(base_ref, *refs):
    nms, ups = refs[:4], refs[4:8]
    joined, left, right = [refs[8 + k : 14 : 3] for k in range(3)]
    outs, (grads, sem) = refs[14:-2], refs[-2:]
    count, d = nms[0].shape
    copies = blocks(base_ref, outs, grads, sem, False)
    for k, (turned, straight) in enumerate(((left, nms), (right, nms), (joined, ups))):

        def some(j, _, k=k, turned=turned, straight=straight):
            value = None
            for h in range(4):
                part = dot(turned[h // 2][:, pl.ds(h % 2 * count, count)], straight[h][:, block(j)])
                value = part if value is None else value + part
            grads[k, :, block(j)] = value.astype(BF)
            return 0

        lax.fori_loop(0, d // 256, some, 0)
        start_all(copies[k])
    for k in range(3):
        wait_all(copies[k])


def ffgrad_call(bases, nms, ups, first, second, shapes):
    hidden = first[0].shape[0]
    d = nms[0].shape[1]
    return pl.pallas_call(
        ffgrad_body,
        out_shape=[jax.ShapeDtypeStruct(shape, BF) for shape in shapes],
        in_specs=[SMEM] + [VMEM] * 14,
        out_specs=[ANY] * len(shapes),
        scratch_shapes=[
            pltpu.VMEM((3, hidden, d), BF),
            pltpu.SemaphoreType.DMA((3, len(shapes), shapes[0][0])),
        ],
        compiler_params=params(40),
        cost_estimate=LIGHT,
        name="feed_forward_gradients",
    )(bases, *nms, *ups, *first, *second)


def beyond(order, step, size):
    return [(i, i + order * step) for i in range(size) if 0 <= i + order * step < size]


def kept(keep, order, size):
    own, between, steps, step = keep, jnp.ones_like(keep), [], 1
    while step < size:
        steps.append((between, own))
        if step * 2 < size:
            got = lax.ppermute(own, "seq", beyond(order, step, size))
            between, own = between * got, own * got
        step *= 2
    return steps


def chain(own, steps, order, size, beside):
    total, before = own, jnp.zeros_like(own)
    for i, (between, whole) in enumerate(steps):
        sent = tie(total.astype(BF), *beside[i]) if i < len(beside) else total.astype(BF)
        got = lax.ppermute(sent, "seq", beyond(order, 2**i, size)).astype(F32)
        shape = between.shape + (1,) * (own.ndim - 1)
        before = before + between.reshape(shape) * got
        total = total + whole.reshape(shape) * got
    return before


def shards(
    mesh_shape,
    tokens,
    starts,
    entry_gain,
    query_weight,
    key_weight,
    value_weight,
    gate_weight,
    head_gain,
    output_weight,
    middle_gain,
    left_weight,
    right_weight,
    down_weight,
    cotangent,
):
    rows_here, span, width = tokens.shape
    count = rows_here * span
    hidden = left_weight.shape[1]
    plan = Plan(mesh_shape, width)
    seq = plan.seq
    by_x, by_half, by_quarter = plan.bases(()), plan.bases((1,)), plan.bases((2, 1))

    def square(shards, behind):
        near = plan.along(tie(plan.mine(jnp.stack(shards), (2, 1)), *behind), True)
        return near, plan.pair(plan.pair(plan.across(near), 2), 1)

    kv_z, kv = square([key_weight, value_weight], ())
    mine = hidden // 4
    stack = lax.dynamic_slice(
        jnp.stack([left_weight.T, right_weight.T, down_weight]),
        (0, plan.lane * mine, 0),
        (3, mine, plan.rows),
    )
    ff_z = plan.along(stack, False)
    qgo_z, qgo = square([query_weight, gate_weight, output_weight], (kv_z,))
    ff_pieces = plan.across(ff_z)
    if not plan.fast:
        whole = ff_z.transpose(1, 2, 0, 3).reshape(3, mine, width // 128, 128)
        ff_pieces = [whole.transpose(2, 0, 1, 3)]
    upstream = cotangent.reshape(count, width)

    def spread_tokens(own):
        beside, above = swap(own, "batch", 1, plan.batch), swap(own, "batch", 2, plan.batch)
        return [own, beside, above, swap(above, "batch", 1, plan.batch)]

    up_all = spread_tokens(upstream)

    place = jnp.arange(span)
    segment = dot(starts.astype(BF), (place[:, None] <= place[None, :]).astype(BF))
    last = segment[:, span - 1 :]
    keep = (last[:, 0] == 0).astype(F32)
    tail = (segment == last).astype(F32).reshape(count, 1)
    segcol, segrow = segment.reshape(count, 1), segment.reshape(rows_here, 1, span)
    source = tokens.reshape(count, width)
    entry_row, head_row, mid_row = (g.reshape(1, width) for g in (entry_gain, head_gain, middle_gain))

    ahead, behind = kept(keep, 1, seq), kept(keep, -1, seq)

    def scan(own, steps, order, beside):
        own = own.reshape(rows_here, -1, HEAD, 128)
        return chain(own, steps, order, seq, beside).astype(BF).reshape(-1, HEAD, 128)

    early = tie(by_quarter, *(f for pair in ahead + behind for f in pair))
    normed_in, keys, ksig, values, fresh = kv_call(plan, early, source, entry_row, tail, kv)
    state = scan(fresh, ahead, 1, ())
    query, qsig, gate = qg_call(plan, by_quarter, normed_in, qgo)
    attended, gated, middle, normed_mid = attend_call(
        plan, by_quarter, query, keys, values, gate, state, segcol, segrow, head_row, source, mid_row, qgo
    )
    nm_all = spread_tokens(normed_mid)
    mixed_a, back_a, *saved_a = ff_call(by_x, nm_all[:2], up_all[:2], ff_pieces)
    mixed_b, back_b, *saved_b = ff_call(by_x, nm_all[2:], up_all[2:], ff_pieces)

    def collect(mine_a, mine_b):
        other = swap(jnp.stack([mine_a[count:], mine_b[count:]]), "batch", 1, plan.batch)
        return add(mine_a[:count], other[0]), swap(add(mine_b[:count], other[1]), "batch", 2, plan.batch)

    back_own, back_got = collect(back_a, back_b)
    ff_terms = ffgrad_call(by_x, nm_all, up_all, saved_a, saved_b, [p.shape for p in ff_pieces])
    if plan.fast:
        ff_far = swap(ff_terms[1], "seq", 1, seq)
    mixed_own, mixed_got = collect(mixed_a, mixed_b)
    mixed = (middle + (mixed_own.astype(F32) + mixed_got.astype(F32))).astype(BF).reshape(tokens.shape)

    midback, branch, gateback, attback, direct, two_gains = mid_call(
        plan, by_quarter, back_own, back_got, middle, mid_row, upstream, gate, attended, head_row, query, segcol, qgo
    )
    qback, kin, vin = inner_call(plan, query, keys, values, qsig, attback, state, segcol, segrow)
    ogq_terms = grads_call(plan, by_half, [gated, normed_in], (0, 1, 1), [branch, gateback, qback])
    after = scan(direct, behind, -1, ((), (kin,), ogq_terms[:1]))
    kv_terms, (kback, vback) = outer_call(
        plan, by_half, keys, values, ksig, kin, vin, after, segcol, segrow, normed_in
    )

    def from_core(term):
        return [add(mine, swap(other, "batch", 1, 4)) for mine, other in zip(term[:2], term[2:])]

    def finish(part):
        return plan.join(add(part, swap(part, "batch", 2, 4)), 1, 1).astype(F32)

    if plan.fast:
        ff_part = plan.sum_along(add(ff_terms[0], tie(ff_far, kin)))
        ogq_near, ogq_far = from_core(ogq_terms)
        ogq_got = swap(ogq_far, "seq", 1, seq)
        kv_near, kv_far = from_core(kv_terms)
        kv_got = swap(kv_far, "seq", 1, seq)
    else:
        turned = ff_terms[0].transpose(1, 2, 0, 3).reshape(3, mine, seq, plan.rows)
        ff_part = lax.psum_scatter(turned.transpose(2, 0, 1, 3), "seq", scatter_dimension=0)
    input_gradient, entry_term = entry_call(
        plan, tie(by_quarter, kv_far) if plan.fast else by_quarter,
        source, entry_row, midback, qback, kback, vback, gateback, kv, qgo,
    )
    input_gradient = input_gradient.reshape(tokens.shape)
    if plan.fast:
        ogq_part = plan.sum_along(add(ogq_near, ogq_got))
        kv_part = plan.sum_along(add(kv_near, tie(kv_got, entry_term)))
        wide = plan.join(plan.join(tie(ff_part, kv_part), 1, 1), 2, 1).astype(F32)
        output_total, gate_total, query_total = finish(ogq_part)
        key_total, value_total = finish(kv_part)
    else:
        wide = plan.join(plan.join(ff_part, 1, 1), 2, 1).astype(F32)
        output_total, gate_total, query_total, key_total, value_total = (
            total
            for term in (ogq_terms, kv_terms)
            for total in lax.psum(lax.psum_scatter(term[0], "seq", scatter_dimension=0), "batch").astype(F32)
        )
    left_total, right_total, down_total = wide[0].T, wide[1].T, wide[2]
    gains = jnp.concatenate([two_gains, entry_term])
    if plan.fast:
        for axis, size in (("batch", plan.batch), ("seq", seq)):
            step = 1
            while step < size:
                gains = gains + swap(gains, axis, step, size)
                step *= 2
    else:
        gains = lax.psum(gains, ("seq", "batch"))
    gains = lax.dynamic_slice(gains, (0, plan.place * plan.rows), (3, plan.rows))
    return (
        mixed,
        input_gradient,
        gains[2],
        query_total,
        key_total,
        value_total,
        gate_total,
        gains[1],
        output_total,
        gains[0],
        left_total,
        right_total,
        down_total,
    )


def solution(mesh):
    row, cut, wide = P("batch", "seq", None), P("seq", None), P(None, "seq")
    in_specs = (row, P("batch", "seq"), P(), cut, cut, cut, cut, P(), cut, P(), cut, cut, wide, row)
    out_specs = (row, row, P("seq"), cut, cut, cut, cut, P("seq"), cut, P("seq"), cut, cut, wide)
    return jax.shard_map(
        functools.partial(shards, dict(mesh.shape)),
        mesh=mesh,
        in_specs=in_specs,
        out_specs=out_specs,
        check_vma=False,
    )
```

```python
import functools

import jax
import jax.numpy as jnp
from jax import lax
from jax.experimental import pallas as pl
from jax.experimental.pallas import tpu as pltpu
from jax.sharding import PartitionSpec as P

HEADS = 16
HEAD = 64
EPSILON = 1e-06
BF = jnp.bfloat16
F32 = jnp.float32
VMEM = pl.BlockSpec(memory_space=pltpu.VMEM)
SMEM = pl.BlockSpec(memory_space=pltpu.SMEM)
ANY = pl.BlockSpec(memory_space=pl.ANY)
STAGE = None
DEAR = {'feed_forward_gradients': 90}
WAITS = {'first': (), 'qgoz': ('kvz',), 'qgox': ('kvk',), 'qgon': ('kvk',), 'ffg': ('kvx',), 'kvn': (), 'ffa': ('up', 'upb'), 'att': (), 'nmd': ('ffa',), 'ffb': ('bo',), 'ffr': ('bt',), 'fs': ('bg',), 'mid': ('ffr',), 'mo': ('mid',), 'mt1': ('mid',), 's2': ('inn',), 'gra': ('s1',), 's3': ('gra',), 'out': ('oc', 'mg'), 'ent': ('kc',), 'ks': ('ent',), 'os': ('kc',), 'fw': ('ks',), 'up': ('kvf',)}


def cost(name):
    return pl.CostEstimate(flops=1 + DEAR.get(name, 0) * 10**9, bytes_accessed=1, transcendentals=0)


def inverse_rms(values):
    return lax.rsqrt(jnp.mean(values * values, axis=-1, keepdims=True) + EPSILON)


def dot(left, right):
    return jnp.dot(left, right, preferred_element_type=F32)


def dot_nt(left, right):
    return lax.dot_general(left, right, (((1,), (1,)), ((), ())), preferred_element_type=F32)


def dot_tn(left, right):
    return lax.dot_general(left, right, (((0,), (0,)), ((), ())), preferred_element_type=F32)


def swap(value, axis, bit, size):
    return lax.ppermute(value, axis, [(i, i ^ bit) for i in range(size)])


def tie(value, *others):
    return lax.optimization_barrier((value,) + others)[0]


class Plan:
    def __init__(self, mesh_shape, width):
        self.seq = mesh_shape["seq"]
        self.batch = mesh_shape["batch"]
        self.rows = width // self.seq
        self.fast = self.seq == 8 and self.batch == 4
        self.place = lax.axis_index("seq")
        self.lane = lax.axis_index("batch")
        self.nz = 4 if self.fast else self.seq
        self.span = width // self.nz
        self.groups = [[z * 2 + x for z in range(self.nz)] for x in range(2)]

    def half(self, bit):
        return (self.lane // bit) % 2

    def bases(self, bits):
        first = jnp.zeros((1,), jnp.int32)
        if self.fast:
            size = self.rows
            x = self.place % 2
            first = jnp.stack([x * size, (1 - x) * size])
            for bit in bits:
                size //= 2
                mine = self.half(bit)
                first = jnp.concatenate([first + mine * size, first + (1 - mine) * size])
        return first.astype(jnp.int32)

    def mine(self, shard, bits):
        if self.fast:
            for bit in bits:
                m, rows, w = shard.shape
                shard = lax.dynamic_slice(shard, (0, self.half(bit) * (rows // 2), 0), (m, rows // 2, w))
        return shard

    def along(self, mine, direct):
        if not self.fast:
            return lax.all_gather(mine, "seq", axis=0)
        if direct:
            copies = jnp.broadcast_to(mine[None], (self.nz,) + mine.shape)
            return lax.all_to_all(copies, "seq", 0, 0, axis_index_groups=self.groups)
        return lax.all_gather(mine, "seq", axis=0, axis_index_groups=self.groups)

    def across(self, near):
        return [near, swap(near, "seq", 1, self.seq)] if self.fast else [near]

    def pair(self, pieces, bit):
        return pieces + [swap(p, "batch", bit, 4) for p in pieces] if self.fast else pieces

    def sum_along(self, near, direct=False):
        if direct:
            z = self.place // 2
            total = lax.dynamic_index_in_dim(near, z, 0, keepdims=False).astype(F32)
            for k in range(1, self.nz):
                sent = lax.dynamic_index_in_dim(near, z ^ k, 0, keepdims=False)
                pairs = [(i, i ^ (2 * k)) for i in range(self.seq)]
                total = total + lax.ppermute(sent, "seq", pairs).astype(F32)
            return total.astype(BF)
        if near.shape[1] == 3:
            got = lax.all_to_all(near, "seq", 0, 0, axis_index_groups=self.groups)
            return jnp.sum(got.astype(F32), axis=0).astype(BF)
        return lax.psum_scatter(near, "seq", scatter_dimension=0, axis_index_groups=self.groups)

    def join(self, mine, bit, axis):
        other = swap(mine, "batch", bit, self.batch)
        lower = self.half(bit) == 0
        return jnp.concatenate([jnp.where(lower, mine, other), jnp.where(lower, other, mine)], axis=axis)


def add(left, right):
    return (left.astype(F32) + right.astype(F32)).astype(BF)


def params(mib):
    return pltpu.CompilerParams(vmem_limit_bytes=mib * 1024 * 1024)


def staged(name, body, out_shape, in_specs, out_specs, scratch):
    ins = [i for i, spec in enumerate(in_specs) if spec is STAGE]
    outs = [i for i, spec in enumerate(out_specs) if spec is STAGE]
    n_in, n_out, n_own = len(in_specs), len(out_specs), len(scratch)

    def kernel(*refs):
        operands, results = list(refs[:n_in]), list(refs[n_in : n_in + n_out])
        own, extra = refs[n_in + n_out : n_in + n_out + n_own], refs[n_in + n_out + n_own :]
        in_sem, out_sem = extra[-2:]
        loads, stores = {}, {}
        for k, i in enumerate(ins):
            loads[i] = pltpu.make_async_copy(operands[i], extra[k], in_sem.at[k])
            operands[i] = extra[k]
        for k, i in enumerate(outs):
            held = extra[len(ins) + k]
            stores[i] = pltpu.make_async_copy(held, results[i], out_sem.at[k])
            results[i] = held
        start_all(loads.values())
        flushed = []

        def ready(*some):
            for i in some or list(loads):
                if i in loads:
                    loads.pop(i).wait()

        def flush(*some):
            for i in some:
                if i in stores and i not in flushed:
                    flushed.append(i)
                    stores[i].start()

        body(ready, flush, *operands, *results, *own)
        ready()
        flush(*stores)
        wait_all(stores.values())

    def call(*operands):
        return pl.pallas_call(
            kernel,
            out_shape=out_shape,
            in_specs=[ANY if spec is STAGE else spec for spec in in_specs],
            out_specs=[ANY if spec is STAGE else spec for spec in out_specs],
            scratch_shapes=list(scratch)
            + [pltpu.VMEM(operands[i].shape, operands[i].dtype) for i in ins]
            + [pltpu.VMEM(out_shape[i].shape, out_shape[i].dtype) for i in outs]
            + [pltpu.SemaphoreType.DMA((max(1, len(ins)),)), pltpu.SemaphoreType.DMA((max(1, len(outs)),))],
            compiler_params=params(60),
            cost_estimate=cost(name),
            name=name,
        )(*operands)

    return call


def low_lanes():
    return lax.broadcasted_iota(jnp.int32, (1, 128), 1) < HEAD


def spread(state):
    low = low_lanes()
    zero = jnp.zeros_like(state)
    return jnp.concatenate([jnp.where(low, state, zero), jnp.where(low, zero, state)], axis=0)


def squeeze(full):
    return jnp.where(low_lanes(), full[:HEAD], full[HEAD:])


def head_sums(values):
    row = lax.broadcasted_iota(jnp.int32, (128, 128), 0) < HEAD
    col = lax.broadcasted_iota(jnp.int32, (128, 128), 1) < HEAD
    ones = (row == col).astype(BF)
    high = values.astype(BF)
    rest = values - high.astype(F32)
    mid = rest.astype(BF)
    return dot(high, ones) + dot(mid, ones)


def block(i, size=256):
    return pl.ds(pl.multiple_of(i * size, size), size)


def fetch(base_ref, pieces, weight, sem, picks):
    return [
        [
            pltpu.make_async_copy(
                piece.at[:, pick],
                weight.at[:, k, pl.ds(pl.multiple_of(base_ref[b], 16), piece.shape[2]), :],
                sem.at[k, b],
            )
            for b, piece in enumerate(pieces)
        ]
        for k, pick in enumerate(picks)
    ]


def hand_out(base_ref, grads, outs, sem):
    m = grads.shape[1]
    return [
        [
            pltpu.make_async_copy(
                grads.at[:, k, pl.ds(pl.multiple_of(base_ref[b], 16), out.shape[-2]), :],
                out.at[:, k],
                sem.at[k, b],
            )
            for b, out in enumerate(outs)
        ]
        for k in range(m)
    ]


def piece_shapes(plan, m, part, w, count):
    return [jax.ShapeDtypeStruct((plan.nz, m, part, w), BF)] * (count if plan.fast else 1)


def start_all(copies):
    for c in copies:
        c.start()


def wait_all(copies):
    for c in copies:
        c.wait()


def soft(x):
    e = jnp.exp(-jnp.abs(x))
    return jnp.maximum(x, 0.0) + jnp.log1p(e), jnp.where(x >= 0.0, 1.0, e) / (1.0 + e)


def kv_body(plan, nb, ready, flush, base_ref, tokens_ref, gain_ref, tail_ref, *refs):
    pieces = refs[:nb]
    normed_ref, keys_ref, sig_ref, values_ref, fresh_ref, weight, sem = refs[nb:]
    d = tokens_ref.shape[1]
    copies = fetch(base_ref, pieces, weight, sem, (0, 1))
    for c in copies:
        start_all(c)
    ready()

    def norm(i, _):
        source = tokens_ref[block(i), :].astype(F32)
        normed_ref[block(i), :] = (source * inverse_rms(source) * gain_ref[...]).astype(BF)
        return 0

    lax.fori_loop(0, 2, norm, 0)
    flush(0)
    wait_all(copies[0])

    def key_part(j, _):
        linear = dot(normed_ref[...], weight[:, 0, :, block(j)].reshape(d, 256))
        plus, sig = soft(linear)
        keys_ref[:, block(j)] = plus.astype(BF)
        sig_ref[:, block(j)] = sig.astype(BF)
        return 0

    lax.fori_loop(0, d // 256, key_part, 0)
    flush(1, 2)
    wait_all(copies[1])

    def value_part(j, _):
        linear = dot(normed_ref[...], weight[:, 1, :, block(j)].reshape(d, 256))
        values_ref[:, block(j)] = linear.astype(BF)
        return 0

    lax.fori_loop(0, d // 256, value_part, 0)
    flush(3)

    def states(i, _):
        rows, lanes = block(i // 8), block(i % 8, 128)
        tail = tail_ref[rows, :].astype(BF)
        fresh_ref[i] = squeeze(dot_tn(keys_ref[rows, lanes], values_ref[rows, lanes] * tail))
        return 0

    lax.fori_loop(0, 16, states, 0, unroll=2)


def kv_call(plan, bases, tokens, gain, tail, pieces):
    nb = len(pieces)
    count, d = tokens.shape
    shape = jax.ShapeDtypeStruct((count, d), BF)
    return staged(
        "keys_values",
        functools.partial(kv_body, plan, nb),
        [shape] * 4 + [jax.ShapeDtypeStruct((16, HEAD, 128), F32)],
        [SMEM, STAGE, VMEM, VMEM] + [ANY] * nb,
        [STAGE] * 5,
        [
            pltpu.VMEM((plan.nz, 2, plan.span, d), BF),
            pltpu.SemaphoreType.DMA((2, nb)),
        ],
    )(bases, tokens, gain, tail, *pieces)


def qg_body(plan, nb, ready, flush, base_ref, normed_ref, *refs):
    pieces = refs[:nb]
    query_ref, sig_ref, gate_ref, weight, sem = refs[nb:]
    d = normed_ref.shape[1]
    copies = fetch(base_ref, pieces, weight, sem, (0, 1))
    for c in copies:
        start_all(c)
    ready()
    wait_all(copies[0])

    def query_part(j, _):
        linear = dot(normed_ref[...], weight[:, 0, :, block(j)].reshape(d, 256))
        plus, sig = soft(linear)
        query_ref[:, block(j)] = plus.astype(BF)
        sig_ref[:, block(j)] = sig.astype(BF)
        return 0

    lax.fori_loop(0, d // 256, query_part, 0)
    flush(0, 1)
    wait_all(copies[1])

    def gate_part(j, _):
        linear = dot(normed_ref[...], weight[:, 1, :, block(j)].reshape(d, 256))
        gate_ref[:, block(j)] = jax.nn.sigmoid(linear)
        return 0

    lax.fori_loop(0, d // 256, gate_part, 0)


def qg_call(plan, bases, normed, pieces):
    nb = len(pieces)
    count, d = normed.shape
    shape = jax.ShapeDtypeStruct((count, d), BF)
    return staged(
        "query_gate",
        functools.partial(qg_body, plan, nb),
        [shape, shape, jax.ShapeDtypeStruct((count, d), F32)],
        [SMEM, STAGE] + [ANY] * nb,
        [STAGE] * 3,
        [
            pltpu.VMEM((plan.nz, 2, plan.span, d), BF),
            pltpu.SemaphoreType.DMA((2, nb)),
        ],
    )(bases, normed, *pieces)


def pair_mask(segcol_ref, segrow_ref, r):
    t = lax.broadcasted_iota(jnp.int32, (256, 256), 0)
    s = lax.broadcasted_iota(jnp.int32, (256, 256), 1)
    return (segcol_ref[block(r), :] == segrow_ref[r]) & (t >= s)


def attend_body(
    plan, nb, ready, flush, base_ref, query_ref, keys_ref, values_ref, gate_ref, state_ref, segcol_ref, segrow_ref,
    gain_ref, tokens_ref, midgain_ref, *refs
):
    pieces = refs[:nb]
    attended_ref, gated_ref, middle_ref, normed_ref, mask_ref, weight, sem = refs[nb:]
    d = query_ref.shape[1]
    (copies,) = fetch(base_ref, pieces, weight, sem, (2,))
    start_all(copies)
    ready(1, 2, 3, 4, 5)
    for r in range(2):
        mask_ref[r] = pair_mask(segcol_ref, segrow_ref, r).astype(F32)

    def pair(i, _):
        r = i // 8
        rows, lanes = block(r), block(i % 8, 128)
        low = low_lanes()
        mask = mask_ref[r]
        q, k, v = query_ref[rows, lanes], keys_ref[rows, lanes], values_ref[rows, lanes]
        zero = jnp.zeros_like(q)
        inherit = (segcol_ref[rows, :] == 0.0).astype(BF)
        q0, q1 = jnp.where(low, q, zero), jnp.where(low, zero, q)
        w0 = (dot_nt(q0, k) * mask).astype(BF)
        w1 = (dot_nt(q1, k) * mask).astype(BF)
        carried = dot(q * inherit, spread(state_ref[i]))
        attended = jnp.where(low, dot(w0, v), dot(w1, v)) + carried
        inverse = lax.rsqrt(head_sums(attended * attended) * (1.0 / HEAD) + EPSILON)
        headed = attended * inverse * gain_ref[:, lanes]
        attended_ref[rows, lanes] = attended
        gated_ref[rows, lanes] = (headed * gate_ref[rows, lanes]).astype(BF)
        return 0

    lax.fori_loop(0, 16, pair, 0, unroll=2)
    flush(0, 1)
    wait_all(copies)

    ready()

    def project(j, _):
        out = dot(gated_ref[...], weight[:, 0, :, block(j)].reshape(d, 256))
        middle_ref[:, block(j)] = tokens_ref[:, block(j)].astype(F32) + out
        return 0

    lax.fori_loop(0, d // 256, project, 0)
    flush(2)

    def norm(i, _):
        middle = middle_ref[block(i), :]
        normed_ref[block(i), :] = (middle * inverse_rms(middle) * midgain_ref[...]).astype(BF)
        return 0

    lax.fori_loop(0, 2, norm, 0)


def attend_call(plan, bases, query, keys, values, gate, state, segcol, segrow, gain, tokens, midgain, pieces):
    nb = len(pieces)
    count, d = query.shape
    low, high = jax.ShapeDtypeStruct((count, d), BF), jax.ShapeDtypeStruct((count, d), F32)
    return staged(
        "attend",
        functools.partial(attend_body, plan, nb),
        [high, low, high, low],
        [SMEM] + [STAGE] * 5 + [VMEM] * 3 + [STAGE, VMEM] + [ANY] * nb,
        [STAGE] * 4,
        [
            pltpu.VMEM((2, 256, 256), F32),
            pltpu.VMEM((plan.nz, 1, plan.span, d), BF),
            pltpu.SemaphoreType.DMA((1, nb)),
        ],
    )(bases, query, keys, values, gate, state, segcol, segrow, gain, tokens, midgain, *pieces)


def mid_body(
    plan, nb, ready, flush, base_ref, back_ref, got_ref, middle_ref, midgain_ref, upstream_ref, gate_ref, attended_ref,
    gain_ref, query_ref, segcol_ref, *refs
):
    pieces = refs[:nb]
    midback_ref, branch_ref, gateback_ref, attback_ref, direct_ref, gains_ref, gated_back, weight, sem = refs[nb:]
    d = query_ref.shape[1]
    (copies,) = fetch(base_ref, pieces, weight, sem, (2,))
    start_all(copies)
    ready(1, 2, 3, 5)

    def norm(i, total):
        rows = block(i, 128)
        dy = back_ref[rows, :].astype(F32) + got_ref[rows, :].astype(F32)
        v = middle_ref[rows, :]
        r = inverse_rms(v)
        scaled = dy * midgain_ref[...]
        mean = jnp.mean(scaled * v, axis=-1, keepdims=True)
        back = upstream_ref[rows, :].astype(F32) + r * scaled - v * (r * r * r * mean)
        midback_ref[rows, :] = back
        branch_ref[rows, :] = back.astype(BF)
        return total + jnp.sum(dy * v * r, axis=0, keepdims=True)

    gains_ref[0:1, :] = lax.fori_loop(0, 4, norm, jnp.zeros((1, d), F32))
    flush(0, 1)
    wait_all(copies)

    slabs = 256 // plan.span

    def through(j, _):
        out_w = weight[pl.ds(j * slabs, slabs), 0].reshape(256, d)
        gated_back[:, block(j)] = dot_nt(branch_ref[...], out_w)
        return 0

    lax.fori_loop(0, d // 256, through, 0)

    ready()

    def pair(p, _):
        lanes = block(p, 128)
        gain = gain_ref[:, lanes]
        total = jnp.zeros((1, 128), F32)
        for r in range(2):
            rows = pl.ds(r * 256, 256)
            att = attended_ref[rows, lanes]
            inverse = lax.rsqrt(head_sums(att * att) * (1.0 / HEAD) + EPSILON)
            gate = gate_ref[rows, lanes]
            back = gated_back[rows, lanes]
            unit = att * inverse
            gateback_ref[rows, lanes] = (back * (unit * gain) * gate * (1.0 - gate)).astype(BF)
            dy = back * gate
            total = total + jnp.sum(dy * unit, axis=0, keepdims=True)
            scaled = dy * gain
            mean = head_sums(scaled * unit) * (1.0 / HEAD)
            attback = (inverse * (scaled - unit * mean)).astype(BF)
            attback_ref[rows, lanes] = attback
            inherit = (segcol_ref[rows, :] == 0.0).astype(BF)
            direct_ref[r * 8 + p] = squeeze(dot_tn(query_ref[rows, lanes] * inherit, attback))
        gains_ref[1:2, lanes] = total
        return 0

    lax.fori_loop(0, 8, pair, 0)


def mid_call(plan, bases, back, got, middle, midgain, upstream, gate, attended, gain, query, segcol, pieces):
    nb = len(pieces)
    count, d = query.shape
    low, high = jax.ShapeDtypeStruct((count, d), BF), jax.ShapeDtypeStruct((count, d), F32)
    return staged(
        "middle_back",
        functools.partial(mid_body, plan, nb),
        [
            high, low, low, low,
            jax.ShapeDtypeStruct((16, HEAD, 128), F32),
            jax.ShapeDtypeStruct((2, d), F32),
        ],
        [SMEM] + [STAGE] * 3 + [VMEM] + [STAGE] * 3 + [VMEM, STAGE, VMEM] + [ANY] * nb,
        [STAGE] * 5 + [VMEM],
        [
            pltpu.VMEM((count, d), F32),
            pltpu.VMEM((plan.nz, 1, plan.span, d), BF),
            pltpu.SemaphoreType.DMA((1, nb)),
        ],
    )(bases, back, got, middle, midgain, upstream, gate, attended, gain, query, segcol, *pieces)


def turn_rows(source_ref, turned):
    def turn(i, _):
        turned[block(i), :] = source_ref[:, block(i)].T
        return 0

    lax.fori_loop(0, source_ref.shape[1] // 256, turn, 0)


def gradient_rows(plan, turned, right_ref, grads, k):
    d = turned.shape[0]
    slabs = 256 // plan.span

    def features(i, _):
        value = dot(turned[block(i), :], right_ref[...]).astype(BF)
        grads[pl.ds(i * slabs, slabs), k] = value.reshape(slabs, plan.span, d)
        return 0

    lax.fori_loop(0, d // 256, features, 0)


def grads_body(plan, which, ready, flush, base_ref, *refs):
    m, n = len(which), max(which) + 1
    lefts, rights = refs[:n], refs[n : n + m]
    outs = refs[n + m : -3]
    turned, grads, sem = refs[-3:]
    ready()
    copies = hand_out(base_ref, grads, outs, sem)
    for k in range(m):
        if k == 0 or which[k] != which[k - 1]:
            turn_rows(lefts[which[k]], turned)
        gradient_rows(plan, turned, rights[k], grads, k)
        start_all(copies[k])
    for k in range(m):
        wait_all(copies[k])


def grads_call(plan, bases, lefts, which, rights):
    m = len(rights)
    count, d = lefts[0].shape
    outs = piece_shapes(plan, m, plan.rows // 2 if plan.fast else plan.rows, d, 4)
    return staged(
        "square_gradients",
        functools.partial(grads_body, plan, which),
        outs,
        [SMEM] + [STAGE] * (len(lefts) + m),
        [ANY] * len(outs),
        [
            pltpu.VMEM((d, count), BF),
            pltpu.VMEM((plan.nz, m, plan.span, d), BF),
            pltpu.SemaphoreType.DMA((m, len(outs))),
        ],
    )(bases, *lefts, *rights)


def inner_body(
    plan, ready, flush, query_ref, keys_ref, values_ref, qsig_ref, attback_ref, state_ref, segcol_ref, segrow_ref,
    qback_ref, kin_ref, vin_ref, mask_ref, turn_ref
):
    for r in range(2):
        mask = pair_mask(segcol_ref, segrow_ref, r).astype(F32)
        mask_ref[r] = mask
        turn_ref[r] = mask.T

    ready()

    def pair(i, _):
        r = i // 8
        rows, lanes = block(r), block(i % 8, 128)
        low = low_lanes()
        mask, mask_t = mask_ref[r], turn_ref[r]
        q, k, v, ab = (x[rows, lanes] for x in (query_ref, keys_ref, values_ref, attback_ref))
        zero = jnp.zeros_like(q)
        inherit = (segcol_ref[rows, :] == 0.0).astype(BF)
        halves = []
        for h in range(2):
            pick = (lambda x: jnp.where(low, x, zero)) if h == 0 else (lambda x: jnp.where(low, zero, x))
            k_h, v_h, ab_h = pick(k), pick(v), pick(ab)
            w_t = (dot_nt(k_h, q) * mask_t).astype(BF)
            sb = (dot_nt(ab_h, v) * mask).astype(BF)
            sb_t = (dot_nt(v_h, ab) * mask_t).astype(BF)
            halves.append((dot(sb, k), dot(sb_t, q), dot(w_t, ab)))
        qb, kb, vb = (jnp.where(low, a, b) for a, b in zip(*halves))
        qb = qb + dot_nt(ab * inherit, spread(state_ref[i]))
        qback_ref[rows, lanes] = (qb * qsig_ref[rows, lanes].astype(F32)).astype(BF)
        kin_ref[rows, lanes] = kb
        vin_ref[rows, lanes] = vb
        return 0

    lax.fori_loop(0, 16, pair, 0)


def inner_call(plan, query, keys, values, qsig, attback, state, segcol, segrow):
    count, d = query.shape
    low, high = jax.ShapeDtypeStruct((count, d), BF), jax.ShapeDtypeStruct((count, d), F32)
    return staged(
        "attend_back",
        functools.partial(inner_body, plan),
        [low, high, high],
        [STAGE] * 6 + [VMEM] * 2,
        [STAGE] * 3,
        [pltpu.VMEM((2, 256, 256), F32), pltpu.VMEM((2, 256, 256), F32)],
    )(query, keys, values, qsig, attback, state, segcol, segrow)


def outer_body(
    plan, sides, ready, flush, base_ref, keys_ref, values_ref, ksig_ref, kin_ref, vin_ref, after_ref, segcol_ref, segrow_ref,
    normed_ref, *refs
):
    outs = refs[:sides]
    kback_ref, vback_ref, turned, grads, sem = refs[sides:]
    ready(9)
    copies = hand_out(base_ref, grads, outs, sem)

    turn_rows(normed_ref, turned)
    ready()

    def pair(i, _):
        r = i // 8
        rows, lanes = block(r), block(i % 8, 128)
        tail = (segcol_ref[rows, :] == segrow_ref[r][:, 255:256]).astype(F32)
        after = spread(after_ref[i])
        kb = kin_ref[rows, lanes] + dot_nt(values_ref[rows, lanes], after) * tail
        vb = vin_ref[rows, lanes] + dot(keys_ref[rows, lanes], after) * tail
        kback_ref[rows, lanes] = (kb * ksig_ref[rows, lanes].astype(F32)).astype(BF)
        vback_ref[rows, lanes] = vb.astype(BF)
        return 0

    lax.fori_loop(0, 16, pair, 0, unroll=2)
    flush(sides, sides + 1)
    for k, right in enumerate((kback_ref, vback_ref)):
        gradient_rows(plan, turned, right, grads, k)
        start_all(copies[k])
    for k in range(2):
        wait_all(copies[k])


def outer_call(plan, bases, keys, values, ksig, kin, vin, after, segcol, segrow, normed):
    count, d = keys.shape
    outs = piece_shapes(plan, 2, plan.rows // 2 if plan.fast else plan.rows, d, 4)
    low = jax.ShapeDtypeStruct((count, d), BF)
    got = staged(
        "key_value_gradients",
        functools.partial(outer_body, plan, len(outs)),
        outs + [low] * 2,
        [SMEM] + [STAGE] * 6 + [VMEM] * 2 + [STAGE],
        [ANY] * len(outs) + [STAGE] * 2,
        [
            pltpu.VMEM((d, count), BF),
            pltpu.VMEM((plan.nz, 2, plan.span, d), BF),
            pltpu.SemaphoreType.DMA((2, len(outs))),
        ],
    )(bases, keys, values, ksig, kin, vin, after, segcol, segrow, normed)
    return got[: len(outs)], got[len(outs) :]


def entry_body(plan, nb, ready, flush, base_ref, tokens_ref, gain_ref, midback_ref, qb_ref, kb_ref, vb_ref, gb_ref, *refs):
    kv, qg = refs[:nb], refs[nb : 2 * nb]
    out_ref, gains_ref, total, weight, more, sem = refs[2 * nb :]
    d = tokens_ref.shape[1]
    copies = fetch(base_ref, qg, weight, sem.at[0], (0, 1)) + fetch(
        base_ref, kv, more, sem.at[1], (0, 1)
    )
    for c in copies:
        start_all(c)
    slabs = 256 // plan.span
    for c, (back, scr, k) in zip(
        copies, ((qb_ref, weight, 0), (gb_ref, weight, 1), (kb_ref, more, 0), (vb_ref, more, 1))
    ):
        wait_all(c)
        first = back is qb_ref
        ready({id(qb_ref): 4, id(kb_ref): 5, id(vb_ref): 6, id(gb_ref): 7}[id(back)])

        def through(j, _, back=back, scr=scr, k=k, first=first):
            rows_w = scr[pl.ds(j * slabs, slabs), k].reshape(256, d)
            value = dot_nt(back[...], rows_w)
            if first:
                total[:, block(j)] = value
            else:
                total[:, block(j)] += value
            return 0

        lax.fori_loop(0, d // 256, through, 0)

    ready()

    def norm(i, gains):
        rows = block(i, 128)
        dy = total[rows, :]
        v = tokens_ref[rows, :].astype(F32)
        r = inverse_rms(v)
        scaled = dy * gain_ref[...]
        mean = jnp.mean(scaled * v, axis=-1, keepdims=True)
        out_ref[rows, :] = midback_ref[rows, :] + r * scaled - v * (r * r * r * mean)
        return gains + jnp.sum(dy * v * r, axis=0, keepdims=True)

    gains_ref[...] = lax.fori_loop(0, 4, norm, jnp.zeros((1, d), F32))


def entry_call(plan, bases, tokens, gain, midback, qb, kb, vb, gb, kv, qg):
    nb = len(kv)
    count, d = tokens.shape
    return staged(
        "entry_back",
        functools.partial(entry_body, plan, nb),
        [jax.ShapeDtypeStruct((count, d), F32), jax.ShapeDtypeStruct((1, d), F32)],
        [SMEM, STAGE, VMEM] + [STAGE] * 5 + [ANY] * (2 * nb),
        [STAGE, VMEM],
        [
            pltpu.VMEM((count, d), F32),
            pltpu.VMEM((plan.nz, 2, plan.span, d), BF),
            pltpu.VMEM((plan.nz, 2, plan.span, d), BF),
            pltpu.SemaphoreType.DMA((2, 2, nb)),
        ],
    )(bases, tokens, gain, midback, qb, kb, vb, gb, *kv, *qg)


def blocks(base_ref, pieces, whole, sem, inward):
    d = whole.shape[2]
    copies = []
    for k in range(3):
        copies.append([])
        for b, piece in enumerate(pieces):
            n = piece.shape[0]
            for z in range(n):
                lanes = pl.ds(pl.multiple_of(base_ref[b] + z * (d // n), 128), 128)
                ends = (piece.at[z, k], whole.at[k, :, lanes])
                copies[-1].append(pltpu.make_async_copy(*(ends if inward else ends[::-1]), sem.at[k, b, z]))
    return copies


def ff_body(nb, ready, flush, base_ref, nm0_ref, nm1_ref, up0_ref, up1_ref, *refs):
    pieces = refs[:nb]
    mixed_refs, back_refs = refs[nb : nb + 2], refs[nb + 2 : nb + 4]
    joined_t, left_t, right_t, weight, joined_s, left_s, right_s, sem = refs[nb + 4 :]
    count, d = nm0_ref.shape
    hidden = weight.shape[1]
    copies = blocks(base_ref, pieces, weight, sem, True)
    for c in copies:
        start_all(c)
    for h, (nm_ref, up_ref) in enumerate(((nm0_ref, up0_ref), (nm1_ref, up1_ref))):
        rows = pl.ds(h * count, count)
        for start in range(0, hidden, 256):
            some = slice(start, min(start + 256, hidden))
            ready(1 + h)
            if h == 0 and start == 0:
                wait_all(copies[0])
            left = dot_nt(nm_ref[...], weight[0, some, :])
            if h == 0 and start == 0:
                wait_all(copies[1])
            right = dot_nt(nm_ref[...], weight[1, some, :])
            ready(3 + h)
            if h == 0 and start == 0:
                wait_all(copies[2])
            joined_back = dot_nt(up_ref[...], weight[2, some, :])
            for value, straight, turned in (
                (left * right, joined_s, joined_t),
                (joined_back * right, left_s, left_t),
                (joined_back * left, right_s, right_t),
            ):
                value = value.astype(BF)
                straight[rows, some] = value
                turned[some, rows] = value.T

    flush(4, 5, 6)

    for h in range(2):

        def through(j, _, h=h):
            rows = pl.ds(h * count, count)
            mixed_refs[h][:, block(j)] = dot(joined_s[rows, :], weight[2, :, block(j)]).astype(BF)
            back = dot(left_s[rows, :], weight[0, :, block(j)]) + dot(right_s[rows, :], weight[1, :, block(j)])
            back_refs[h][:, block(j)] = back.astype(BF)
            return 0

        lax.fori_loop(0, d // 256, through, 0)
        flush(h, 2 + h)


def ff_call(bases, nm, up, pieces):
    nb = len(pieces)
    n, three, hidden, _ = pieces[0].shape
    count, d = nm[0].shape
    whole, some = jax.ShapeDtypeStruct((count, d), BF), jax.ShapeDtypeStruct((hidden, 2 * count), BF)
    return staged(
        "feed_forward",
        functools.partial(ff_body, nb),
        [whole] * 4 + [some] * 3,
        [SMEM] + [STAGE] * 4 + [ANY] * nb,
        [STAGE] * 7,
        [pltpu.VMEM((three, hidden, d), BF)]
        + [pltpu.VMEM((2 * count, hidden), BF)] * 3
        + [pltpu.SemaphoreType.DMA((3, nb, n))],
    )(bases, *nm, *up, *pieces)


def ffgrad_body(ready, flush, base_ref, *refs):
    nms, ups = refs[:4], refs[4:8]
    joined, left, right = [refs[8 + k : 14 : 3] for k in range(3)]
    outs, (grads, sem) = refs[14:-2], refs[-2:]
    count, d = nms[0].shape
    copies = blocks(base_ref, outs, grads, sem, False)
    for k, (turned, straight) in enumerate(((left, nms), (right, nms), (joined, ups))):

        ready(*((1, 2, 3, 4, 10, 13), (11, 14), ())[k])

        def some(j, _, k=k, turned=turned, straight=straight):
            value = None
            for h in range(4):
                part = dot(turned[h // 2][:, pl.ds(h % 2 * count, count)], straight[h][:, block(j)])
                value = part if value is None else value + part
            grads[k, :, block(j)] = value.astype(BF)
            return 0

        lax.fori_loop(0, d // 256, some, 0)
        start_all(copies[k])
    for k in range(3):
        wait_all(copies[k])


def ffgrad_call(bases, nms, ups, first, second, shapes):
    hidden = first[0].shape[0]
    d = nms[0].shape[1]
    return staged(
        "feed_forward_gradients",
        ffgrad_body,
        [jax.ShapeDtypeStruct(shape, BF) for shape in shapes],
        [SMEM] + [STAGE] * 14,
        [ANY] * len(shapes),
        [
            pltpu.VMEM((3, hidden, d), BF),
            pltpu.SemaphoreType.DMA((3, len(shapes), shapes[0][0])),
        ],
    )(bases, *nms, *ups, *first, *second)


def beyond(order, step, size):
    return [(i, i + order * step) for i in range(size) if 0 <= i + order * step < size]


class Chain:
    def __init__(self, own, keep, order, size):
        self.total, self.before = own, jnp.zeros_like(own)
        self.whole, self.between = keep[:, None, None], jnp.ones_like(keep)[:, None, None]
        self.order, self.size, self.reach = order, size, 1

    def step(self, *others):
        rows, n, lanes = self.total.shape
        flags = jnp.broadcast_to(self.whole, (rows, 16, lanes))
        sent = tie(jnp.concatenate([self.total, flags], axis=1).astype(BF), *others)
        received = lax.ppermute(sent, "seq", beyond(self.order, self.reach, self.size))
        got, got_whole = received[:, :n].astype(F32), received[:, n : n + 1, :1].astype(F32)
        self.before = self.before + self.between * got
        self.total = self.total + self.whole * got
        self.between, self.whole = self.between * got_whole, self.whole * got_whole
        self.reach *= 2
        return received

    def result(self):
        while self.reach < self.size:
            self.step()
        return self.before.astype(BF).reshape(-1, HEAD, 128)


def shards(
    mesh_shape,
    tokens,
    starts,
    entry_gain,
    query_weight,
    key_weight,
    value_weight,
    gate_weight,
    head_gain,
    output_weight,
    middle_gain,
    left_weight,
    right_weight,
    down_weight,
    cotangent,
):
    rows_here, span, width = tokens.shape
    count = rows_here * span
    hidden = left_weight.shape[1]
    plan = Plan(mesh_shape, width)
    seq = plan.seq
    by_whole, by_half, by_quarter = jnp.zeros((1,), jnp.int32), plan.bases((1,)), plan.bases((2, 1))

    place = jnp.arange(span)
    segment = dot(starts.astype(BF), (place[:, None] <= place[None, :]).astype(BF))
    last = segment[:, span - 1 :]
    keep = (last[:, 0] == 0).astype(F32)
    tail = (segment == last).astype(F32).reshape(count, 1)
    segcol, segrow = segment.reshape(count, 1), segment.reshape(rows_here, 1, span)
    source = tokens.reshape(count, width)
    entry_row, head_row, mid_row = (g.reshape(1, width) for g in (entry_gain, head_gain, middle_gain))

    def scan(own, order):
        return Chain(own.reshape(rows_here, -1, 128), keep, order, seq)

    done = {}

    def held(name, value):
        return tie(value, *(done[other] for other in WAITS.get(name, ()) if other in done))

    def note(name, value):
        done[name] = value
        return value

    def send(name, value, axis, bit):
        return note(name, swap(held(name, value), axis, bit, plan.seq if axis == "seq" else plan.batch))

    def quarter(weights):
        return plan.mine(jnp.stack(weights), (2, 1))

    kv_z = note("kvz", plan.along(quarter([key_weight, value_weight]), True))
    qgo_z = quarter([query_weight, gate_weight, output_weight])
    qgo_z = note("qgoz", plan.along(held("qgoz", qgo_z), True))
    mine = hidden // 4
    stack = lax.dynamic_slice(
        jnp.stack([left_weight.T, right_weight.T, down_weight]),
        (0, plan.lane * mine, 0),
        (3, mine, plan.rows),
    )
    ff_seq = lax.all_gather(held("ffg", stack), "seq", axis=0)
    if plan.rows != 128:
        ff_seq = ff_seq.transpose(1, 2, 0, 3).reshape(3, mine, width // 128, 128).transpose(2, 0, 1, 3)
    upstream = cotangent.reshape(count, width)
    kv, qgo = [kv_z], [qgo_z]
    if "up" in WAITS.get("first", ()):
        up_above = send("up", upstream, "batch", 2)
    if plan.fast:
        kv.append(send("kvx", kv_z, "seq", 1))
        kv += [send("kvn", kv_z, "batch", 2), send("kvf", kv[1], "batch", 2)]
        kv += [send("kvc", piece, "batch", 1) for piece in kv]
    if plan.fast and "qgox" in WAITS.get("first", ()):
        qgo.append(send("qgox", qgo_z, "seq", 1))
        qgo.append(send("qgon", qgo_z, "batch", 2))

    normed_in, keys, ksig, values, fresh = kv_call(
        plan, held("kvk", by_quarter), source, entry_row, tail, kv
    )
    note("kvk", keys)
    chain = scan(fresh, 1)
    if "r1" in WAITS.get("first", ()):
        note("r1", chain.step(*(done[other] for other in WAITS.get("r1", ()))))
    if plan.fast and len(qgo) == 1:
        qgo.append(send("qgox", qgo_z, "seq", 1))
        qgo.append(send("qgon", qgo_z, "batch", 2))
    if "r1" not in done:
        note("r1", chain.step(*(done[other] for other in WAITS.get("r1", ()) if other in done)))
    if plan.fast:
        qgo.append(send("qgof", qgo[1], "batch", 2))
    note("r2", chain.step(*(done[other] for other in WAITS.get("r2", ()) if other in done)))
    if plan.fast:
        qgo += [send("qgoc", piece, "batch", 1) for piece in qgo]
    if "up" not in done:
        up_above = send("up", upstream, "batch", 2)
    up_all = [upstream, send("upb", upstream, "batch", 1), up_above, send("upd", up_above, "batch", 1)]
    note("r3", chain.step(*(done[other] for other in WAITS.get("r3", ()) if other in done)))
    state = chain.result()
    query, qsig, gate = qg_call(plan, held("qgk", by_quarter), normed_in, qgo)
    note("qgk", query)
    attended, gated, middle, normed_mid = attend_call(
        plan, held("att", by_quarter), query, keys, values, gate, state, segcol, segrow, head_row, source, mid_row, qgo
    )
    note("att", gated)
    nm_above = send("nma", normed_mid, "batch", 2)
    nm_all = [normed_mid, send("nmb", normed_mid, "batch", 1)]
    mixed_0, mixed_1, back_0, back_1, *saved_a = ff_call(held("ffa", by_whole), nm_all, up_all[:2], [ff_seq])
    note("ffa", back_0)
    nm_above = held("nmd", nm_above)
    nm_all += [nm_above, send("nmd", nm_above, "batch", 1)]
    back_own = note("bo", add(back_0, send("bo1", back_1, "batch", 1)))
    mixed_2, mixed_3, back_2, back_3, *saved_b = ff_call(held("ffb", by_whole), nm_all[2:], up_all[2:], [ff_seq])
    note("ffb", back_2)
    back_there = note("bt", add(back_2, send("bt1", back_3, "batch", 1)))
    back_got = send("bg", back_there, "batch", 2)
    ff_terms = ffgrad_call(held("ffr", by_whole), nm_all, up_all, saved_a, saved_b, [ff_seq.shape])
    note("ffr", ff_terms[0])
    ff_share = held("fs", ff_terms[0])
    if plan.rows != 128:
        ff_share = ff_share.transpose(1, 2, 0, 3).reshape(3, mine, seq, plan.rows).transpose(2, 0, 1, 3)
    ff_part = note("fs", lax.psum_scatter(ff_share, "seq", scatter_dimension=0))

    midback, branch, gateback, attback, direct, two_gains = mid_call(
        plan, held("mid", by_quarter), back_own, back_got, middle, mid_row, upstream, gate, attended, head_row,
        query, segcol, qgo,
    )
    note("mid", attback)
    chain = scan(direct, -1)
    note("s1", chain.step())
    qback, kin, vin = inner_call(plan, query, keys, values, held("inn", qsig), attback, state, segcol, segrow)
    note("inn", kin)
    mixed_own = add(mixed_0, send("mo", mixed_1, "batch", 1))
    mixed_there = note("mt", add(mixed_2, send("mt1", mixed_3, "batch", 1)))
    mixed_got = send("mg", mixed_there, "batch", 2)
    note("s2", chain.step(*(done[other] for other in WAITS.get("s2", ()) if other in done)))
    ogq_terms = grads_call(
        plan, held("gra", by_half), [gated, normed_in], (0, 1, 1), [branch, gateback, qback]
    )
    note("gra", ogq_terms[0])

    def finish(part):
        return plan.join(add(part, swap(part, "batch", 2, 4)), 1, 1).astype(F32)

    def quarters(part):
        above = swap(part, "batch", 2, plan.batch)
        lower = plan.half(2) == 0
        mine = jnp.stack([jnp.where(lower, part, above), jnp.where(lower, above, part)])
        return mine, swap(mine, "batch", 1, plan.batch)

    if plan.fast and "oc" in WAITS.get("first", ()):
        ogq_far = note("oc", add(ogq_terms[1], send("oc1", ogq_terms[3], "batch", 1)))
        ogq_near = add(ogq_terms[0], send("oc0", ogq_terms[2], "batch", 1))
        ogq_got = send("ox", ogq_far, "seq", 1)
    note("s3", chain.step(*(done[other] for other in WAITS.get("s3", ()) if other in done)))
    if plan.fast and "oc" not in done:
        ogq_far = note("oc", add(ogq_terms[1], send("oc1", ogq_terms[3], "batch", 1)))
        ogq_near = add(ogq_terms[0], send("oc0", ogq_terms[2], "batch", 1))
        ogq_got = send("ox", ogq_far, "seq", 1)
    after = chain.result()
    kv_terms, (kback, vback) = outer_call(
        plan, held("out", by_half), keys, values, ksig, kin, vin, after, segcol, segrow, normed_in
    )
    note("out", kback)
    if plan.fast:
        kv_far = note("kc", add(kv_terms[1], send("kc1", kv_terms[3], "batch", 1)))
        kv_got = send("kx", kv_far, "seq", 1)
        kv_near = add(kv_terms[0], send("kc0", kv_terms[2], "batch", 1))
    input_gradient, entry_term = entry_call(
        plan, held("ent", by_quarter), source, entry_row, midback, qback, kback, vback, gateback, kv, qgo
    )
    note("ent", entry_term)
    input_gradient = input_gradient.reshape(tokens.shape)
    mixed = (middle + (mixed_own.astype(F32) + held("mx", mixed_got).astype(F32))).astype(BF)
    mixed = mixed.reshape(tokens.shape)
    if plan.fast:
        kv_sum = note("ks", add(kv_near, held("ks", kv_got)))
        kv_part = note("kz", plan.sum_along(kv_sum, True))
        ogq_sum = note("os", add(ogq_near, held("os", ogq_got)))
        ogq_part = note("oz", plan.sum_along(ogq_sum))
        wide = quarters(held("fw", ff_part))
        note("fw", wide[0])
        output_total, gate_total, query_total = finish(held("of", ogq_part))
        key_total, value_total = finish(held("kf", kv_part))
    else:
        wide = quarters(ff_part)
        output_total, gate_total, query_total, key_total, value_total = (
            total
            for term in (ogq_terms, kv_terms)
            for total in lax.psum(lax.psum_scatter(term[0], "seq", scatter_dimension=0), "batch").astype(F32)
        )
    own, other = wide
    lower = plan.half(1) == 0
    first, second = jnp.where(lower, own, other), jnp.where(lower, other, own)
    wide = jnp.concatenate([first[0], second[0], first[1], second[1]], axis=1).astype(F32)
    left_total, right_total, down_total = wide[0].T, wide[1].T, wide[2]
    gains = held("gains", jnp.concatenate([two_gains, entry_term]))
    if plan.fast:
        for axis, size in (("batch", plan.batch), ("seq", seq)):
            step = 1
            while step < size:
                gains = gains + swap(gains, axis, step, size)
                step *= 2
    else:
        gains = lax.psum(gains, ("seq", "batch"))
    gains = lax.dynamic_slice(gains, (0, plan.place * plan.rows), (3, plan.rows))
    return (
        mixed,
        input_gradient,
        gains[2],
        query_total,
        key_total,
        value_total,
        gate_total,
        gains[1],
        output_total,
        gains[0],
        left_total,
        right_total,
        down_total,
    )


def solution(mesh):
    row, cut, wide = P("batch", "seq", None), P("seq", None), P(None, "seq")
    in_specs = (row, P("batch", "seq"), P(), cut, cut, cut, cut, P(), cut, P(), cut, cut, wide, row)
    out_specs = (row, row, P("seq"), cut, cut, cut, cut, P("seq"), cut, P("seq"), cut, cut, wide)
    return jax.shard_map(
        functools.partial(shards, dict(mesh.shape)),
        mesh=mesh,
        in_specs=in_specs,
        out_specs=out_specs,
        check_vma=False,
    )
```

```python
import functools

import jax
import jax.numpy as jnp
from jax import lax
from jax.experimental import pallas as pl
from jax.experimental.pallas import tpu as pltpu
from jax.sharding import PartitionSpec as P

HEADS = 16
HEAD = 64
EPSILON = 1e-06
BF = jnp.bfloat16
F32 = jnp.float32
VMEM = pl.BlockSpec(memory_space=pltpu.VMEM)
SMEM = pl.BlockSpec(memory_space=pltpu.SMEM)
ANY = pl.BlockSpec(memory_space=pl.ANY)
STAGE = None
DEAR = {'feed_forward_gradients': 90}
WAITS = {'first': (), 'qgoz': ('kvz',), 'qgox': ('kvk',), 'qgon': ('kvk',), 'ffg': ('kvx',), 'kvn': (), 'ffa': ('up', 'upb'), 'att': (), 'nmd': ('ffa',), 'ffb': ('bo',), 'ffr': ('bt',), 'fs': ('bg',), 'mid': ('ffr',), 'mo': ('mid',), 'mt1': ('mid',), 's2': ('inn',), 'gra': ('s1',), 's3': ('gra',), 'out': ('oc', 'mg'), 'ent': ('kc',), 'ks': ('ent',), 'os': ('kc',), 'fw': ('ks',), 'up': ('kvf',), 'of': ('fw',)}


def cost(name):
    return pl.CostEstimate(flops=1 + DEAR.get(name, 0) * 10**9, bytes_accessed=1, transcendentals=0)


def inverse_rms(values):
    return lax.rsqrt(jnp.mean(values * values, axis=-1, keepdims=True) + EPSILON)


def dot(left, right):
    return jnp.dot(left, right, preferred_element_type=F32)


def dot_nt(left, right):
    return lax.dot_general(left, right, (((1,), (1,)), ((), ())), preferred_element_type=F32)


def dot_tn(left, right):
    return lax.dot_general(left, right, (((0,), (0,)), ((), ())), preferred_element_type=F32)


def swap(value, axis, bit, size):
    return lax.ppermute(value, axis, [(i, i ^ bit) for i in range(size)])


def tie(value, *others):
    return lax.optimization_barrier((value,) + others)[0]


class Plan:
    def __init__(self, mesh_shape, width):
        self.seq = mesh_shape["seq"]
        self.batch = mesh_shape["batch"]
        self.rows = width // self.seq
        self.fast = self.seq == 8 and self.batch == 4
        self.place = lax.axis_index("seq")
        self.lane = lax.axis_index("batch")
        self.nz = 4 if self.fast else self.seq
        self.span = width // self.nz
        self.groups = [[z * 2 + x for z in range(self.nz)] for x in range(2)]

    def half(self, bit):
        return (self.lane // bit) % 2

    def bases(self, bits):
        first = jnp.zeros((1,), jnp.int32)
        if self.fast:
            size = self.rows
            x = self.place % 2
            first = jnp.stack([x * size, (1 - x) * size])
            for bit in bits:
                size //= 2
                mine = self.half(bit)
                first = jnp.concatenate([first + mine * size, first + (1 - mine) * size])
        return first.astype(jnp.int32)

    def mine(self, shard, bits):
        if self.fast:
            for bit in bits:
                m, rows, w = shard.shape
                shard = lax.dynamic_slice(shard, (0, self.half(bit) * (rows // 2), 0), (m, rows // 2, w))
        return shard

    def along(self, mine, direct):
        if not self.fast:
            return lax.all_gather(mine, "seq", axis=0)
        if direct:
            copies = jnp.broadcast_to(mine[None], (self.nz,) + mine.shape)
            return lax.all_to_all(copies, "seq", 0, 0, axis_index_groups=self.groups)
        return lax.all_gather(mine, "seq", axis=0, axis_index_groups=self.groups)

    def across(self, near):
        return [near, swap(near, "seq", 1, self.seq)] if self.fast else [near]

    def pair(self, pieces, bit):
        return pieces + [swap(p, "batch", bit, 4) for p in pieces] if self.fast else pieces

    def sum_along(self, near, direct=False):
        if direct:
            z = self.place // 2
            total = lax.dynamic_index_in_dim(near, z, 0, keepdims=False).astype(F32)
            for k in range(1, self.nz):
                sent = lax.dynamic_index_in_dim(near, z ^ k, 0, keepdims=False)
                pairs = [(i, i ^ (2 * k)) for i in range(self.seq)]
                total = total + lax.ppermute(sent, "seq", pairs).astype(F32)
            return total.astype(BF)
        if near.shape[1] == 3:
            got = lax.all_to_all(near, "seq", 0, 0, axis_index_groups=self.groups)
            return jnp.sum(got.astype(F32), axis=0).astype(BF)
        return lax.psum_scatter(near, "seq", scatter_dimension=0, axis_index_groups=self.groups)

    def join(self, mine, bit, axis):
        other = swap(mine, "batch", bit, self.batch)
        lower = self.half(bit) == 0
        return jnp.concatenate([jnp.where(lower, mine, other), jnp.where(lower, other, mine)], axis=axis)


def add(left, right):
    return (left.astype(F32) + right.astype(F32)).astype(BF)


def params(mib):
    return pltpu.CompilerParams(vmem_limit_bytes=mib * 1024 * 1024)


def staged(name, body, out_shape, in_specs, out_specs, scratch):
    ins = [i for i, spec in enumerate(in_specs) if spec is STAGE]
    outs = [i for i, spec in enumerate(out_specs) if spec is STAGE]
    n_in, n_out, n_own = len(in_specs), len(out_specs), len(scratch)

    def kernel(*refs):
        operands, results = list(refs[:n_in]), list(refs[n_in : n_in + n_out])
        own, extra = refs[n_in + n_out : n_in + n_out + n_own], refs[n_in + n_out + n_own :]
        in_sem, out_sem = extra[-2:]
        loads, stores = {}, {}
        for k, i in enumerate(ins):
            loads[i] = pltpu.make_async_copy(operands[i], extra[k], in_sem.at[k])
            operands[i] = extra[k]
        for k, i in enumerate(outs):
            held = extra[len(ins) + k]
            stores[i] = pltpu.make_async_copy(held, results[i], out_sem.at[k])
            results[i] = held
        start_all(loads.values())
        flushed = []

        def ready(*some):
            for i in some or list(loads):
                if i in loads:
                    loads.pop(i).wait()

        def flush(*some):
            for i in some:
                if i in stores and i not in flushed:
                    flushed.append(i)
                    stores[i].start()

        body(ready, flush, *operands, *results, *own)
        ready()
        flush(*stores)
        wait_all(stores.values())

    def call(*operands):
        return pl.pallas_call(
            kernel,
            out_shape=out_shape,
            in_specs=[ANY if spec is STAGE else spec for spec in in_specs],
            out_specs=[ANY if spec is STAGE else spec for spec in out_specs],
            scratch_shapes=list(scratch)
            + [pltpu.VMEM(operands[i].shape, operands[i].dtype) for i in ins]
            + [pltpu.VMEM(out_shape[i].shape, out_shape[i].dtype) for i in outs]
            + [pltpu.SemaphoreType.DMA((max(1, len(ins)),)), pltpu.SemaphoreType.DMA((max(1, len(outs)),))],
            compiler_params=params(60),
            cost_estimate=cost(name),
            name=name,
        )(*operands)

    return call


def low_lanes():
    return lax.broadcasted_iota(jnp.int32, (1, 128), 1) < HEAD


def spread(state):
    low = low_lanes()
    zero = jnp.zeros_like(state)
    return jnp.concatenate([jnp.where(low, state, zero), jnp.where(low, zero, state)], axis=0)


def squeeze(full):
    return jnp.where(low_lanes(), full[:HEAD], full[HEAD:])


def head_sums(values):
    row = lax.broadcasted_iota(jnp.int32, (128, 128), 0) < HEAD
    col = lax.broadcasted_iota(jnp.int32, (128, 128), 1) < HEAD
    ones = (row == col).astype(BF)
    high = values.astype(BF)
    rest = values - high.astype(F32)
    mid = rest.astype(BF)
    return dot(high, ones) + dot(mid, ones)


def block(i, size=256):
    return pl.ds(pl.multiple_of(i * size, size), size)


def fetch(base_ref, pieces, weight, sem, picks):
    return [
        [
            pltpu.make_async_copy(
                piece.at[:, pick],
                weight.at[:, k, pl.ds(pl.multiple_of(base_ref[b], 16), piece.shape[2]), :],
                sem.at[k, b],
            )
            for b, piece in enumerate(pieces)
        ]
        for k, pick in enumerate(picks)
    ]


def hand_out(base_ref, grads, outs, sem):
    m = grads.shape[1]
    return [
        [
            pltpu.make_async_copy(
                grads.at[:, k, pl.ds(pl.multiple_of(base_ref[b], 16), out.shape[-2]), :],
                out.at[:, k],
                sem.at[k, b],
            )
            for b, out in enumerate(outs)
        ]
        for k in range(m)
    ]


def piece_shapes(plan, m, part, w, count):
    return [jax.ShapeDtypeStruct((plan.nz, m, part, w), BF)] * (count if plan.fast else 1)


def start_all(copies):
    for c in copies:
        c.start()


def wait_all(copies):
    for c in copies:
        c.wait()


def soft(x):
    e = jnp.exp(-jnp.abs(x))
    return jnp.maximum(x, 0.0) + jnp.log1p(e), jnp.where(x >= 0.0, 1.0, e) / (1.0 + e)


def kv_body(plan, nb, ready, flush, base_ref, tokens_ref, gain_ref, tail_ref, *refs):
    pieces = refs[:nb]
    normed_ref, keys_ref, sig_ref, values_ref, fresh_ref, weight, sem = refs[nb:]
    d = tokens_ref.shape[1]
    copies = fetch(base_ref, pieces, weight, sem, (0, 1))
    for c in copies:
        start_all(c)
    ready()

    def norm(i, _):
        source = tokens_ref[block(i), :].astype(F32)
        normed_ref[block(i), :] = (source * inverse_rms(source) * gain_ref[...]).astype(BF)
        return 0

    lax.fori_loop(0, 2, norm, 0)
    flush(0)
    wait_all(copies[0])

    def key_part(j, _):
        linear = dot(normed_ref[...], weight[:, 0, :, block(j)].reshape(d, 256))
        plus, sig = soft(linear)
        keys_ref[:, block(j)] = plus.astype(BF)
        sig_ref[:, block(j)] = sig.astype(BF)
        return 0

    lax.fori_loop(0, d // 256, key_part, 0)
    flush(1, 2)
    wait_all(copies[1])

    def value_part(j, _):
        linear = dot(normed_ref[...], weight[:, 1, :, block(j)].reshape(d, 256))
        values_ref[:, block(j)] = linear.astype(BF)
        return 0

    lax.fori_loop(0, d // 256, value_part, 0)
    flush(3)

    def states(i, _):
        rows, lanes = block(i // 8), block(i % 8, 128)
        tail = tail_ref[rows, :].astype(BF)
        fresh_ref[i] = squeeze(dot_tn(keys_ref[rows, lanes], values_ref[rows, lanes] * tail))
        return 0

    lax.fori_loop(0, 16, states, 0, unroll=2)


def kv_call(plan, bases, tokens, gain, tail, pieces):
    nb = len(pieces)
    count, d = tokens.shape
    shape = jax.ShapeDtypeStruct((count, d), BF)
    return staged(
        "keys_values",
        functools.partial(kv_body, plan, nb),
        [shape] * 4 + [jax.ShapeDtypeStruct((16, HEAD, 128), F32)],
        [SMEM, STAGE, VMEM, VMEM] + [ANY] * nb,
        [STAGE] * 5,
        [
            pltpu.VMEM((plan.nz, 2, plan.span, d), BF),
            pltpu.SemaphoreType.DMA((2, nb)),
        ],
    )(bases, tokens, gain, tail, *pieces)


def qg_body(plan, nb, ready, flush, base_ref, normed_ref, *refs):
    pieces = refs[:nb]
    query_ref, sig_ref, gate_ref, weight, sem = refs[nb:]
    d = normed_ref.shape[1]
    copies = fetch(base_ref, pieces, weight, sem, (0, 1))
    for c in copies:
        start_all(c)
    ready()
    wait_all(copies[0])

    def query_part(j, _):
        linear = dot(normed_ref[...], weight[:, 0, :, block(j)].reshape(d, 256))
        plus, sig = soft(linear)
        query_ref[:, block(j)] = plus.astype(BF)
        sig_ref[:, block(j)] = sig.astype(BF)
        return 0

    lax.fori_loop(0, d // 256, query_part, 0)
    flush(0, 1)
    wait_all(copies[1])

    def gate_part(j, _):
        linear = dot(normed_ref[...], weight[:, 1, :, block(j)].reshape(d, 256))
        gate_ref[:, block(j)] = jax.nn.sigmoid(linear)
        return 0

    lax.fori_loop(0, d // 256, gate_part, 0)


def qg_call(plan, bases, normed, pieces):
    nb = len(pieces)
    count, d = normed.shape
    shape = jax.ShapeDtypeStruct((count, d), BF)
    return staged(
        "query_gate",
        functools.partial(qg_body, plan, nb),
        [shape, shape, jax.ShapeDtypeStruct((count, d), F32)],
        [SMEM, STAGE] + [ANY] * nb,
        [STAGE] * 3,
        [
            pltpu.VMEM((plan.nz, 2, plan.span, d), BF),
            pltpu.SemaphoreType.DMA((2, nb)),
        ],
    )(bases, normed, *pieces)


def pair_mask(segcol_ref, segrow_ref, r):
    t = lax.broadcasted_iota(jnp.int32, (256, 256), 0)
    s = lax.broadcasted_iota(jnp.int32, (256, 256), 1)
    return (segcol_ref[block(r), :] == segrow_ref[r]) & (t >= s)


def attend_body(
    plan, nb, ready, flush, base_ref, query_ref, keys_ref, values_ref, gate_ref, state_ref, segcol_ref, segrow_ref,
    gain_ref, tokens_ref, midgain_ref, *refs
):
    pieces = refs[:nb]
    attended_ref, gated_ref, middle_ref, normed_ref, mask_ref, weight, sem = refs[nb:]
    d = query_ref.shape[1]
    (copies,) = fetch(base_ref, pieces, weight, sem, (2,))
    start_all(copies)
    ready(1, 2, 3, 4, 5)
    for r in range(2):
        mask_ref[r] = pair_mask(segcol_ref, segrow_ref, r).astype(F32)

    def pair(i, _):
        r = i // 8
        rows, lanes = block(r), block(i % 8, 128)
        low = low_lanes()
        mask = mask_ref[r]
        q, k, v = query_ref[rows, lanes], keys_ref[rows, lanes], values_ref[rows, lanes]
        zero = jnp.zeros_like(q)
        inherit = (segcol_ref[rows, :] == 0.0).astype(BF)
        q0, q1 = jnp.where(low, q, zero), jnp.where(low, zero, q)
        w0 = (dot_nt(q0, k) * mask).astype(BF)
        w1 = (dot_nt(q1, k) * mask).astype(BF)
        carried = dot(q * inherit, spread(state_ref[i]))
        attended = jnp.where(low, dot(w0, v), dot(w1, v)) + carried
        inverse = lax.rsqrt(head_sums(attended * attended) * (1.0 / HEAD) + EPSILON)
        headed = attended * inverse * gain_ref[:, lanes]
        attended_ref[rows, lanes] = attended
        gated_ref[rows, lanes] = (headed * gate_ref[rows, lanes]).astype(BF)
        return 0

    lax.fori_loop(0, 16, pair, 0, unroll=2)
    flush(0, 1)
    wait_all(copies)

    ready()

    def project(j, _):
        out = dot(gated_ref[...], weight[:, 0, :, block(j)].reshape(d, 256))
        middle_ref[:, block(j)] = tokens_ref[:, block(j)].astype(F32) + out
        return 0

    lax.fori_loop(0, d // 256, project, 0)
    flush(2)

    def norm(i, _):
        middle = middle_ref[block(i), :]
        normed_ref[block(i), :] = (middle * inverse_rms(middle) * midgain_ref[...]).astype(BF)
        return 0

    lax.fori_loop(0, 2, norm, 0)


def attend_call(plan, bases, query, keys, values, gate, state, segcol, segrow, gain, tokens, midgain, pieces):
    nb = len(pieces)
    count, d = query.shape
    low, high = jax.ShapeDtypeStruct((count, d), BF), jax.ShapeDtypeStruct((count, d), F32)
    return staged(
        "attend",
        functools.partial(attend_body, plan, nb),
        [high, low, high, low],
        [SMEM] + [STAGE] * 5 + [VMEM] * 3 + [STAGE, VMEM] + [ANY] * nb,
        [STAGE] * 4,
        [
            pltpu.VMEM((2, 256, 256), F32),
            pltpu.VMEM((plan.nz, 1, plan.span, d), BF),
            pltpu.SemaphoreType.DMA((1, nb)),
        ],
    )(bases, query, keys, values, gate, state, segcol, segrow, gain, tokens, midgain, *pieces)


def mid_body(
    plan, nb, ready, flush, base_ref, back_ref, got_ref, middle_ref, midgain_ref, upstream_ref, gate_ref, attended_ref,
    gain_ref, query_ref, segcol_ref, *refs
):
    pieces = refs[:nb]
    midback_ref, branch_ref, gateback_ref, attback_ref, direct_ref, gains_ref, gated_back, weight, sem = refs[nb:]
    d = query_ref.shape[1]
    (copies,) = fetch(base_ref, pieces, weight, sem, (2,))
    start_all(copies)
    ready(1, 2, 3, 5)

    def norm(i, total):
        rows = block(i, 128)
        dy = back_ref[rows, :].astype(F32) + got_ref[rows, :].astype(F32)
        v = middle_ref[rows, :]
        r = inverse_rms(v)
        scaled = dy * midgain_ref[...]
        mean = jnp.mean(scaled * v, axis=-1, keepdims=True)
        back = upstream_ref[rows, :].astype(F32) + r * scaled - v * (r * r * r * mean)
        midback_ref[rows, :] = back
        branch_ref[rows, :] = back.astype(BF)
        return total + jnp.sum(dy * v * r, axis=0, keepdims=True)

    gains_ref[0:1, :] = lax.fori_loop(0, 4, norm, jnp.zeros((1, d), F32))
    flush(0, 1)
    wait_all(copies)

    slabs = 256 // plan.span

    def through(j, _):
        out_w = weight[pl.ds(j * slabs, slabs), 0].reshape(256, d)
        gated_back[:, block(j)] = dot_nt(branch_ref[...], out_w)
        return 0

    lax.fori_loop(0, d // 256, through, 0)

    ready()

    def pair(p, _):
        lanes = block(p, 128)
        gain = gain_ref[:, lanes]
        total = jnp.zeros((1, 128), F32)
        for r in range(2):
            rows = pl.ds(r * 256, 256)
            att = attended_ref[rows, lanes]
            inverse = lax.rsqrt(head_sums(att * att) * (1.0 / HEAD) + EPSILON)
            gate = gate_ref[rows, lanes]
            back = gated_back[rows, lanes]
            unit = att * inverse
            gateback_ref[rows, lanes] = (back * (unit * gain) * gate * (1.0 - gate)).astype(BF)
            dy = back * gate
            total = total + jnp.sum(dy * unit, axis=0, keepdims=True)
            scaled = dy * gain
            mean = head_sums(scaled * unit) * (1.0 / HEAD)
            attback = (inverse * (scaled - unit * mean)).astype(BF)
            attback_ref[rows, lanes] = attback
            inherit = (segcol_ref[rows, :] == 0.0).astype(BF)
            direct_ref[r * 8 + p] = squeeze(dot_tn(query_ref[rows, lanes] * inherit, attback))
        gains_ref[1:2, lanes] = total
        return 0

    lax.fori_loop(0, 8, pair, 0)


def mid_call(plan, bases, back, got, middle, midgain, upstream, gate, attended, gain, query, segcol, pieces):
    nb = len(pieces)
    count, d = query.shape
    low, high = jax.ShapeDtypeStruct((count, d), BF), jax.ShapeDtypeStruct((count, d), F32)
    return staged(
        "middle_back",
        functools.partial(mid_body, plan, nb),
        [
            high, low, low, low,
            jax.ShapeDtypeStruct((16, HEAD, 128), F32),
            jax.ShapeDtypeStruct((2, d), F32),
        ],
        [SMEM] + [STAGE] * 3 + [VMEM] + [STAGE] * 3 + [VMEM, STAGE, VMEM] + [ANY] * nb,
        [STAGE] * 5 + [VMEM],
        [
            pltpu.VMEM((count, d), F32),
            pltpu.VMEM((plan.nz, 1, plan.span, d), BF),
            pltpu.SemaphoreType.DMA((1, nb)),
        ],
    )(bases, back, got, middle, midgain, upstream, gate, attended, gain, query, segcol, *pieces)


def turn_rows(source_ref, turned):
    def turn(i, _):
        turned[block(i), :] = source_ref[:, block(i)].T
        return 0

    lax.fori_loop(0, source_ref.shape[1] // 256, turn, 0)


def gradient_rows(plan, turned, right_ref, grads, k):
    d = turned.shape[0]
    slabs = 256 // plan.span

    def features(i, _):
        value = dot(turned[block(i), :], right_ref[...]).astype(BF)
        grads[pl.ds(i * slabs, slabs), k] = value.reshape(slabs, plan.span, d)
        return 0

    lax.fori_loop(0, d // 256, features, 0)


def grads_body(plan, which, ready, flush, base_ref, *refs):
    m, n = len(which), max(which) + 1
    lefts, rights = refs[:n], refs[n : n + m]
    outs = refs[n + m : -3]
    turned, grads, sem = refs[-3:]
    ready()
    copies = hand_out(base_ref, grads, outs, sem)
    for k in range(m):
        if k == 0 or which[k] != which[k - 1]:
            turn_rows(lefts[which[k]], turned)
        gradient_rows(plan, turned, rights[k], grads, k)
        start_all(copies[k])
    for k in range(m):
        wait_all(copies[k])


def grads_call(plan, bases, lefts, which, rights):
    m = len(rights)
    count, d = lefts[0].shape
    outs = piece_shapes(plan, m, plan.rows // 2 if plan.fast else plan.rows, d, 4)
    return staged(
        "square_gradients",
        functools.partial(grads_body, plan, which),
        outs,
        [SMEM] + [STAGE] * (len(lefts) + m),
        [ANY] * len(outs),
        [
            pltpu.VMEM((d, count), BF),
            pltpu.VMEM((plan.nz, m, plan.span, d), BF),
            pltpu.SemaphoreType.DMA((m, len(outs))),
        ],
    )(bases, *lefts, *rights)


def inner_body(
    plan, ready, flush, query_ref, keys_ref, values_ref, qsig_ref, attback_ref, state_ref, segcol_ref, segrow_ref,
    qback_ref, kin_ref, vin_ref, mask_ref, turn_ref
):
    for r in range(2):
        mask = pair_mask(segcol_ref, segrow_ref, r).astype(F32)
        mask_ref[r] = mask
        turn_ref[r] = mask.T

    ready()

    def pair(i, _):
        r = i // 8
        rows, lanes = block(r), block(i % 8, 128)
        low = low_lanes()
        mask, mask_t = mask_ref[r], turn_ref[r]
        q, k, v, ab = (x[rows, lanes] for x in (query_ref, keys_ref, values_ref, attback_ref))
        zero = jnp.zeros_like(q)
        inherit = (segcol_ref[rows, :] == 0.0).astype(BF)
        halves = []
        for h in range(2):
            pick = (lambda x: jnp.where(low, x, zero)) if h == 0 else (lambda x: jnp.where(low, zero, x))
            k_h, v_h, ab_h = pick(k), pick(v), pick(ab)
            w_t = (dot_nt(k_h, q) * mask_t).astype(BF)
            sb = (dot_nt(ab_h, v) * mask).astype(BF)
            sb_t = (dot_nt(v_h, ab) * mask_t).astype(BF)
            halves.append((dot(sb, k), dot(sb_t, q), dot(w_t, ab)))
        qb, kb, vb = (jnp.where(low, a, b) for a, b in zip(*halves))
        qb = qb + dot_nt(ab * inherit, spread(state_ref[i]))
        qback_ref[rows, lanes] = (qb * qsig_ref[rows, lanes].astype(F32)).astype(BF)
        kin_ref[rows, lanes] = kb
        vin_ref[rows, lanes] = vb
        return 0

    lax.fori_loop(0, 16, pair, 0)


def inner_call(plan, query, keys, values, qsig, attback, state, segcol, segrow):
    count, d = query.shape
    low, high = jax.ShapeDtypeStruct((count, d), BF), jax.ShapeDtypeStruct((count, d), F32)
    return staged(
        "attend_back",
        functools.partial(inner_body, plan),
        [low, high, high],
        [STAGE] * 6 + [VMEM] * 2,
        [STAGE] * 3,
        [pltpu.VMEM((2, 256, 256), F32), pltpu.VMEM((2, 256, 256), F32)],
    )(query, keys, values, qsig, attback, state, segcol, segrow)


def outer_body(
    plan, sides, ready, flush, base_ref, keys_ref, values_ref, ksig_ref, kin_ref, vin_ref, after_ref, segcol_ref, segrow_ref,
    normed_ref, *refs
):
    outs = refs[:sides]
    kback_ref, vback_ref, turned, grads, sem = refs[sides:]
    ready(9)
    copies = hand_out(base_ref, grads, outs, sem)

    turn_rows(normed_ref, turned)
    ready()

    def pair(i, _):
        r = i // 8
        rows, lanes = block(r), block(i % 8, 128)
        tail = (segcol_ref[rows, :] == segrow_ref[r][:, 255:256]).astype(F32)
        after = spread(after_ref[i])
        kb = kin_ref[rows, lanes] + dot_nt(values_ref[rows, lanes], after) * tail
        vb = vin_ref[rows, lanes] + dot(keys_ref[rows, lanes], after) * tail
        kback_ref[rows, lanes] = (kb * ksig_ref[rows, lanes].astype(F32)).astype(BF)
        vback_ref[rows, lanes] = vb.astype(BF)
        return 0

    lax.fori_loop(0, 16, pair, 0, unroll=2)
    flush(sides, sides + 1)
    for k, right in enumerate((kback_ref, vback_ref)):
        gradient_rows(plan, turned, right, grads, k)
        start_all(copies[k])
    for k in range(2):
        wait_all(copies[k])


def outer_call(plan, bases, keys, values, ksig, kin, vin, after, segcol, segrow, normed):
    count, d = keys.shape
    outs = piece_shapes(plan, 2, plan.rows // 2 if plan.fast else plan.rows, d, 4)
    low = jax.ShapeDtypeStruct((count, d), BF)
    got = staged(
        "key_value_gradients",
        functools.partial(outer_body, plan, len(outs)),
        outs + [low] * 2,
        [SMEM] + [STAGE] * 6 + [VMEM] * 2 + [STAGE],
        [ANY] * len(outs) + [STAGE] * 2,
        [
            pltpu.VMEM((d, count), BF),
            pltpu.VMEM((plan.nz, 2, plan.span, d), BF),
            pltpu.SemaphoreType.DMA((2, len(outs))),
        ],
    )(bases, keys, values, ksig, kin, vin, after, segcol, segrow, normed)
    return got[: len(outs)], got[len(outs) :]


def entry_body(plan, nb, ready, flush, base_ref, tokens_ref, gain_ref, midback_ref, qb_ref, kb_ref, vb_ref, gb_ref, *refs):
    kv, qg = refs[:nb], refs[nb : 2 * nb]
    out_ref, gains_ref, total, weight, more, sem = refs[2 * nb :]
    d = tokens_ref.shape[1]
    copies = fetch(base_ref, qg, weight, sem.at[0], (0, 1)) + fetch(
        base_ref, kv, more, sem.at[1], (0, 1)
    )
    for c in copies:
        start_all(c)
    slabs = 256 // plan.span
    for c, (back, scr, k) in zip(
        copies, ((qb_ref, weight, 0), (gb_ref, weight, 1), (kb_ref, more, 0), (vb_ref, more, 1))
    ):
        wait_all(c)
        first = back is qb_ref
        ready({id(qb_ref): 4, id(kb_ref): 5, id(vb_ref): 6, id(gb_ref): 7}[id(back)])

        def through(j, _, back=back, scr=scr, k=k, first=first):
            rows_w = scr[pl.ds(j * slabs, slabs), k].reshape(256, d)
            value = dot_nt(back[...], rows_w)
            if first:
                total[:, block(j)] = value
            else:
                total[:, block(j)] += value
            return 0

        lax.fori_loop(0, d // 256, through, 0)

    ready()

    def norm(i, gains):
        rows = block(i, 128)
        dy = total[rows, :]
        v = tokens_ref[rows, :].astype(F32)
        r = inverse_rms(v)
        scaled = dy * gain_ref[...]
        mean = jnp.mean(scaled * v, axis=-1, keepdims=True)
        out_ref[rows, :] = midback_ref[rows, :] + r * scaled - v * (r * r * r * mean)
        return gains + jnp.sum(dy * v * r, axis=0, keepdims=True)

    gains_ref[...] = lax.fori_loop(0, 4, norm, jnp.zeros((1, d), F32))


def entry_call(plan, bases, tokens, gain, midback, qb, kb, vb, gb, kv, qg):
    nb = len(kv)
    count, d = tokens.shape
    return staged(
        "entry_back",
        functools.partial(entry_body, plan, nb),
        [jax.ShapeDtypeStruct((count, d), F32), jax.ShapeDtypeStruct((1, d), F32)],
        [SMEM, STAGE, VMEM] + [STAGE] * 5 + [ANY] * (2 * nb),
        [STAGE, VMEM],
        [
            pltpu.VMEM((count, d), F32),
            pltpu.VMEM((plan.nz, 2, plan.span, d), BF),
            pltpu.VMEM((plan.nz, 2, plan.span, d), BF),
            pltpu.SemaphoreType.DMA((2, 2, nb)),
        ],
    )(bases, tokens, gain, midback, qb, kb, vb, gb, *kv, *qg)


def blocks(base_ref, pieces, whole, sem, inward):
    d = whole.shape[2]
    copies = []
    for k in range(3):
        copies.append([])
        for b, piece in enumerate(pieces):
            n = piece.shape[0]
            for z in range(n):
                lanes = pl.ds(pl.multiple_of(base_ref[b] + z * (d // n), 128), 128)
                ends = (piece.at[z, k], whole.at[k, :, lanes])
                copies[-1].append(pltpu.make_async_copy(*(ends if inward else ends[::-1]), sem.at[k, b, z]))
    return copies


def ff_body(nb, ready, flush, base_ref, nm0_ref, nm1_ref, up0_ref, up1_ref, *refs):
    pieces = refs[:nb]
    mixed_refs, back_refs = refs[nb : nb + 2], refs[nb + 2 : nb + 4]
    joined_t, left_t, right_t, weight, joined_s, left_s, right_s, sem = refs[nb + 4 :]
    count, d = nm0_ref.shape
    hidden = weight.shape[1]
    copies = blocks(base_ref, pieces, weight, sem, True)
    for c in copies:
        start_all(c)
    for h, (nm_ref, up_ref) in enumerate(((nm0_ref, up0_ref), (nm1_ref, up1_ref))):
        rows = pl.ds(h * count, count)
        for start in range(0, hidden, 256):
            some = slice(start, min(start + 256, hidden))
            ready(1 + h)
            if h == 0 and start == 0:
                wait_all(copies[0])
            left = dot_nt(nm_ref[...], weight[0, some, :])
            if h == 0 and start == 0:
                wait_all(copies[1])
            right = dot_nt(nm_ref[...], weight[1, some, :])
            ready(3 + h)
            if h == 0 and start == 0:
                wait_all(copies[2])
            joined_back = dot_nt(up_ref[...], weight[2, some, :])
            for value, straight, turned in (
                (left * right, joined_s, joined_t),
                (joined_back * right, left_s, left_t),
                (joined_back * left, right_s, right_t),
            ):
                value = value.astype(BF)
                straight[rows, some] = value
                turned[some, rows] = value.T

    flush(4, 5, 6)

    def through(j, _):
        for h in range(2):
            rows = pl.ds(h * count, count)
            mixed_refs[h][:, block(j)] = dot(joined_s[rows, :], weight[2, :, block(j)]).astype(BF)
            back = dot(left_s[rows, :], weight[0, :, block(j)]) + dot(right_s[rows, :], weight[1, :, block(j)])
            back_refs[h][:, block(j)] = back.astype(BF)
        return 0

    lax.fori_loop(0, d // 256, through, 0)


def ff_call(bases, nm, up, pieces):
    nb = len(pieces)
    n, three, hidden, _ = pieces[0].shape
    count, d = nm[0].shape
    whole, some = jax.ShapeDtypeStruct((count, d), BF), jax.ShapeDtypeStruct((hidden, 2 * count), BF)
    return staged(
        "feed_forward",
        functools.partial(ff_body, nb),
        [whole] * 4 + [some] * 3,
        [SMEM] + [STAGE] * 4 + [ANY] * nb,
        [STAGE] * 7,
        [pltpu.VMEM((three, hidden, d), BF)]
        + [pltpu.VMEM((2 * count, hidden), BF)] * 3
        + [pltpu.SemaphoreType.DMA((3, nb, n))],
    )(bases, *nm, *up, *pieces)


def ffgrad_body(ready, flush, base_ref, *refs):
    nms, ups = refs[:4], refs[4:8]
    joined, left, right = [refs[8 + k : 14 : 3] for k in range(3)]
    outs, (grads, sem) = refs[14:-2], refs[-2:]
    count, d = nms[0].shape
    copies = blocks(base_ref, outs, grads, sem, False)
    for k, (turned, straight) in enumerate(((left, nms), (right, nms), (joined, ups))):

        ready(*((1, 2, 3, 4, 10, 13), (11, 14), ())[k])

        def some(j, _, k=k, turned=turned, straight=straight):
            value = None
            for h in range(4):
                part = dot(turned[h // 2][:, pl.ds(h % 2 * count, count)], straight[h][:, block(j)])
                value = part if value is None else value + part
            grads[k, :, block(j)] = value.astype(BF)
            return 0

        lax.fori_loop(0, d // 256, some, 0)
        start_all(copies[k])
    for k in range(3):
        wait_all(copies[k])


def ffgrad_call(bases, nms, ups, first, second, shapes):
    hidden = first[0].shape[0]
    d = nms[0].shape[1]
    return staged(
        "feed_forward_gradients",
        ffgrad_body,
        [jax.ShapeDtypeStruct(shape, BF) for shape in shapes],
        [SMEM] + [STAGE] * 14,
        [ANY] * len(shapes),
        [
            pltpu.VMEM((3, hidden, d), BF),
            pltpu.SemaphoreType.DMA((3, len(shapes), shapes[0][0])),
        ],
    )(bases, *nms, *ups, *first, *second)


def beyond(order, step, size):
    return [(i, i + order * step) for i in range(size) if 0 <= i + order * step < size]


class Chain:
    def __init__(self, own, keep, order, size):
        self.total, self.before = own, jnp.zeros_like(own)
        self.whole, self.between = keep[:, None, None], jnp.ones_like(keep)[:, None, None]
        self.order, self.size, self.reach = order, size, 1

    def step(self, *others):
        rows, n, lanes = self.total.shape
        flags = jnp.broadcast_to(self.whole, (rows, 16, lanes))
        sent = tie(jnp.concatenate([self.total, flags], axis=1).astype(BF), *others)
        received = lax.ppermute(sent, "seq", beyond(self.order, self.reach, self.size))
        got, got_whole = received[:, :n].astype(F32), received[:, n : n + 1, :1].astype(F32)
        self.before = self.before + self.between * got
        self.total = self.total + self.whole * got
        self.between, self.whole = self.between * got_whole, self.whole * got_whole
        self.reach *= 2
        return received

    def result(self):
        while self.reach < self.size:
            self.step()
        return self.before.astype(BF).reshape(-1, HEAD, 128)


def shards(
    mesh_shape,
    tokens,
    starts,
    entry_gain,
    query_weight,
    key_weight,
    value_weight,
    gate_weight,
    head_gain,
    output_weight,
    middle_gain,
    left_weight,
    right_weight,
    down_weight,
    cotangent,
):
    rows_here, span, width = tokens.shape
    count = rows_here * span
    hidden = left_weight.shape[1]
    plan = Plan(mesh_shape, width)
    seq = plan.seq
    by_whole, by_half, by_quarter = jnp.zeros((1,), jnp.int32), plan.bases((1,)), plan.bases((2, 1))

    place = jnp.arange(span)
    segment = dot(starts.astype(BF), (place[:, None] <= place[None, :]).astype(BF))
    last = segment[:, span - 1 :]
    keep = (last[:, 0] == 0).astype(F32)
    tail = (segment == last).astype(F32).reshape(count, 1)
    segcol, segrow = segment.reshape(count, 1), segment.reshape(rows_here, 1, span)
    source = tokens.reshape(count, width)
    entry_row, head_row, mid_row = (g.reshape(1, width) for g in (entry_gain, head_gain, middle_gain))

    def scan(own, order):
        return Chain(own.reshape(rows_here, -1, 128), keep, order, seq)

    done = {}

    def held(name, value):
        return tie(value, *(done[other] for other in WAITS.get(name, ()) if other in done))

    def note(name, value):
        done[name] = value
        return value

    def send(name, value, axis, bit):
        return note(name, swap(held(name, value), axis, bit, plan.seq if axis == "seq" else plan.batch))

    def quarter(weights):
        return plan.mine(jnp.stack(weights), (2, 1))

    kv_z = note("kvz", plan.along(quarter([key_weight, value_weight]), True))
    qgo_z = quarter([query_weight, gate_weight, output_weight])
    qgo_z = note("qgoz", plan.along(held("qgoz", qgo_z), True))
    mine = hidden // 4
    stack = lax.dynamic_slice(
        jnp.stack([left_weight.T, right_weight.T, down_weight]),
        (0, plan.lane * mine, 0),
        (3, mine, plan.rows),
    )
    ff_seq = lax.all_gather(held("ffg", stack), "seq", axis=0)
    if plan.rows != 128:
        ff_seq = ff_seq.transpose(1, 2, 0, 3).reshape(3, mine, width // 128, 128).transpose(2, 0, 1, 3)
    upstream = cotangent.reshape(count, width)
    kv, qgo = [kv_z], [qgo_z]
    if "up" in WAITS.get("first", ()):
        up_above = send("up", upstream, "batch", 2)
    if plan.fast:
        kv.append(send("kvx", kv_z, "seq", 1))
        kv += [send("kvn", kv_z, "batch", 2), send("kvf", kv[1], "batch", 2)]
        kv += [send("kvc", piece, "batch", 1) for piece in kv]
    if plan.fast and "qgox" in WAITS.get("first", ()):
        qgo.append(send("qgox", qgo_z, "seq", 1))
        qgo.append(send("qgon", qgo_z, "batch", 2))

    normed_in, keys, ksig, values, fresh = kv_call(
        plan, held("kvk", by_quarter), source, entry_row, tail, kv
    )
    note("kvk", keys)
    chain = scan(fresh, 1)
    if "r1" in WAITS.get("first", ()):
        note("r1", chain.step(*(done[other] for other in WAITS.get("r1", ()))))
    if plan.fast and len(qgo) == 1:
        qgo.append(send("qgox", qgo_z, "seq", 1))
        qgo.append(send("qgon", qgo_z, "batch", 2))
    if "r1" not in done:
        note("r1", chain.step(*(done[other] for other in WAITS.get("r1", ()) if other in done)))
    if plan.fast:
        qgo.append(send("qgof", qgo[1], "batch", 2))
    note("r2", chain.step(*(done[other] for other in WAITS.get("r2", ()) if other in done)))
    if plan.fast:
        qgo += [send("qgoc", piece, "batch", 1) for piece in qgo]
    if "up" not in done:
        up_above = send("up", upstream, "batch", 2)
    up_all = [upstream, send("upb", upstream, "batch", 1), up_above, send("upd", up_above, "batch", 1)]
    note("r3", chain.step(*(done[other] for other in WAITS.get("r3", ()) if other in done)))
    state = chain.result()
    query, qsig, gate = qg_call(plan, held("qgk", by_quarter), normed_in, qgo)
    note("qgk", query)
    attended, gated, middle, normed_mid = attend_call(
        plan, held("att", by_quarter), query, keys, values, gate, state, segcol, segrow, head_row, source, mid_row, qgo
    )
    note("att", gated)
    nm_above = send("nma", normed_mid, "batch", 2)
    nm_all = [normed_mid, send("nmb", normed_mid, "batch", 1)]
    mixed_0, mixed_1, back_0, back_1, *saved_a = ff_call(held("ffa", by_whole), nm_all, up_all[:2], [ff_seq])
    note("ffa", back_0)
    nm_above = held("nmd", nm_above)
    nm_all += [nm_above, send("nmd", nm_above, "batch", 1)]
    back_own = note("bo", add(back_0, send("bo1", back_1, "batch", 1)))
    mixed_2, mixed_3, back_2, back_3, *saved_b = ff_call(held("ffb", by_whole), nm_all[2:], up_all[2:], [ff_seq])
    note("ffb", back_2)
    back_there = note("bt", add(back_2, send("bt1", back_3, "batch", 1)))
    back_got = send("bg", back_there, "batch", 2)
    ff_terms = ffgrad_call(held("ffr", by_whole), nm_all, up_all, saved_a, saved_b, [ff_seq.shape])
    note("ffr", ff_terms[0])
    ff_share = held("fs", ff_terms[0])
    if plan.rows != 128:
        ff_share = ff_share.transpose(1, 2, 0, 3).reshape(3, mine, seq, plan.rows).transpose(2, 0, 1, 3)
    ff_part = note("fs", lax.psum_scatter(ff_share, "seq", scatter_dimension=0))

    midback, branch, gateback, attback, direct, two_gains = mid_call(
        plan, held("mid", by_quarter), back_own, back_got, middle, mid_row, upstream, gate, attended, head_row,
        query, segcol, qgo,
    )
    note("mid", attback)
    chain = scan(direct, -1)
    note("s1", chain.step())
    qback, kin, vin = inner_call(plan, query, keys, values, held("inn", qsig), attback, state, segcol, segrow)
    note("inn", kin)
    mixed_own = add(mixed_0, send("mo", mixed_1, "batch", 1))
    mixed_there = note("mt", add(mixed_2, send("mt1", mixed_3, "batch", 1)))
    mixed_got = send("mg", mixed_there, "batch", 2)
    note("s2", chain.step(*(done[other] for other in WAITS.get("s2", ()) if other in done)))
    ogq_terms = grads_call(
        plan, held("gra", by_half), [gated, normed_in], (0, 1, 1), [branch, gateback, qback]
    )
    note("gra", ogq_terms[0])

    def finish(part):
        return plan.join(add(part, swap(part, "batch", 2, 4)), 1, 1).astype(F32)

    def quarters(part):
        above = swap(part, "batch", 2, plan.batch)
        lower = plan.half(2) == 0
        mine = jnp.stack([jnp.where(lower, part, above), jnp.where(lower, above, part)])
        return mine, swap(mine, "batch", 1, plan.batch)

    if plan.fast and "oc" in WAITS.get("first", ()):
        ogq_far = note("oc", add(ogq_terms[1], send("oc1", ogq_terms[3], "batch", 1)))
        ogq_near = add(ogq_terms[0], send("oc0", ogq_terms[2], "batch", 1))
        ogq_got = send("ox", ogq_far, "seq", 1)
    note("s3", chain.step(*(done[other] for other in WAITS.get("s3", ()) if other in done)))
    if plan.fast and "oc" not in done:
        ogq_far = note("oc", add(ogq_terms[1], send("oc1", ogq_terms[3], "batch", 1)))
        ogq_near = add(ogq_terms[0], send("oc0", ogq_terms[2], "batch", 1))
        ogq_got = send("ox", ogq_far, "seq", 1)
    after = chain.result()
    kv_terms, (kback, vback) = outer_call(
        plan, held("out", by_half), keys, values, ksig, kin, vin, after, segcol, segrow, normed_in
    )
    note("out", kback)
    if plan.fast:
        kv_far = note("kc", add(kv_terms[1], send("kc1", kv_terms[3], "batch", 1)))
        kv_got = send("kx", kv_far, "seq", 1)
        kv_near = add(kv_terms[0], send("kc0", kv_terms[2], "batch", 1))
    input_gradient, entry_term = entry_call(
        plan, held("ent", by_quarter), source, entry_row, midback, qback, kback, vback, gateback, kv, qgo
    )
    note("ent", entry_term)
    input_gradient = input_gradient.reshape(tokens.shape)
    mixed = (middle + (mixed_own.astype(F32) + held("mx", mixed_got).astype(F32))).astype(BF)
    mixed = mixed.reshape(tokens.shape)
    if plan.fast:
        kv_sum = note("ks", add(kv_near, held("ks", kv_got)))
        kv_part = note("kz", plan.sum_along(kv_sum, True))
        ogq_sum = note("os", add(ogq_near, held("os", ogq_got)))
        ogq_part = note("oz", plan.sum_along(ogq_sum))
        wide = quarters(held("fw", ff_part))
        note("fw", wide[0])
        output_total, gate_total, query_total = finish(held("of", ogq_part))
        key_total, value_total = finish(held("kf", kv_part))
    else:
        wide = quarters(ff_part)
        output_total, gate_total, query_total, key_total, value_total = (
            total
            for term in (ogq_terms, kv_terms)
            for total in lax.psum(lax.psum_scatter(term[0], "seq", scatter_dimension=0), "batch").astype(F32)
        )
    own, other = wide
    lower = plan.half(1) == 0
    first, second = jnp.where(lower, own, other), jnp.where(lower, other, own)
    wide = jnp.concatenate([first[0], second[0], first[1], second[1]], axis=1).astype(F32)
    left_total, right_total, down_total = wide[0].T, wide[1].T, wide[2]
    gains = held("gains", jnp.concatenate([two_gains, entry_term]))
    if plan.fast:
        for axis, size in (("batch", plan.batch), ("seq", seq)):
            step = 1
            while step < size:
                gains = gains + swap(gains, axis, step, size)
                step *= 2
    else:
        gains = lax.psum(gains, ("seq", "batch"))
    gains = lax.dynamic_slice(gains, (0, plan.place * plan.rows), (3, plan.rows))
    return (
        mixed,
        input_gradient,
        gains[2],
        query_total,
        key_total,
        value_total,
        gate_total,
        gains[1],
        output_total,
        gains[0],
        left_total,
        right_total,
        down_total,
    )


def solution(mesh):
    row, cut, wide = P("batch", "seq", None), P("seq", None), P(None, "seq")
    in_specs = (row, P("batch", "seq"), P(), cut, cut, cut, cut, P(), cut, P(), cut, cut, wide, row)
    out_specs = (row, row, P("seq"), cut, cut, cut, cut, P("seq"), cut, P("seq"), cut, cut, wide)
    return jax.shard_map(
        functools.partial(shards, dict(mesh.shape)),
        mesh=mesh,
        in_specs=in_specs,
        out_specs=out_specs,
        check_vma=False,
    )
```

```python
import functools

import jax
import jax.numpy as jnp
from jax import lax
from jax.experimental import pallas as pl
from jax.experimental.pallas import tpu as pltpu
from jax.sharding import PartitionSpec as P

HEADS = 16
HEAD = 64
EPSILON = 1e-06
BF = jnp.bfloat16
F32 = jnp.float32
VMEM = pl.BlockSpec(memory_space=pltpu.VMEM)
SMEM = pl.BlockSpec(memory_space=pltpu.SMEM)
ANY = pl.BlockSpec(memory_space=pl.ANY)
STAGE = None
DEAR = {'feed_forward_gradients': 90}
WAITS = {'first': (), 'qgoz': ('kvz',), 'qgox': ('kvk',), 'qgon': ('kvk',), 'ffg': ('kvx',), 'kvn': (), 'ffa': ('up', 'upb'), 'att': (), 'nmd': ('ffa',), 'ffb': ('bo',), 'ffr': ('bt',), 'fs': ('bg',), 'mid': ('ffr',), 'mo': ('mid',), 'mt1': ('mid',), 's2': ('inn',), 'gra': ('s1',), 's3': ('gra',), 'out': ('oc', 'mg'), 'ent': ('kc',), 'ks': ('ent',), 'os': ('kc',), 'fw': ('ks',), 'up': ('kvf',), 'of': ('fw',)}


def cost(name):
    return pl.CostEstimate(flops=1 + DEAR.get(name, 0) * 10**9, bytes_accessed=1, transcendentals=0)


def inverse_rms(values):
    return lax.rsqrt(jnp.mean(values * values, axis=-1, keepdims=True) + EPSILON)


def dot(left, right):
    return jnp.dot(left, right, preferred_element_type=F32)


def dot_nt(left, right):
    return lax.dot_general(left, right, (((1,), (1,)), ((), ())), preferred_element_type=F32)


def dot_tn(left, right):
    return lax.dot_general(left, right, (((0,), (0,)), ((), ())), preferred_element_type=F32)


def swap(value, axis, bit, size):
    return lax.ppermute(value, axis, [(i, i ^ bit) for i in range(size)])


def tie(value, *others):
    return lax.optimization_barrier((value,) + others)[0]


class Plan:
    def __init__(self, mesh_shape, width):
        self.seq = mesh_shape["seq"]
        self.batch = mesh_shape["batch"]
        self.rows = width // self.seq
        self.fast = self.seq == 8 and self.batch == 4
        self.place = lax.axis_index("seq")
        self.lane = lax.axis_index("batch")
        self.nz = 4 if self.fast else self.seq
        self.span = width // self.nz
        self.groups = [[z * 2 + x for z in range(self.nz)] for x in range(2)]

    def half(self, bit):
        return (self.lane // bit) % 2

    def bases(self, bits):
        first = jnp.zeros((1,), jnp.int32)
        if self.fast:
            size = self.rows
            x = self.place % 2
            first = jnp.stack([x * size, (1 - x) * size])
            for bit in bits:
                size //= 2
                mine = self.half(bit)
                first = jnp.concatenate([first + mine * size, first + (1 - mine) * size])
        return first.astype(jnp.int32)

    def mine(self, shard, bits):
        if self.fast:
            for bit in bits:
                m, rows, w = shard.shape
                shard = lax.dynamic_slice(shard, (0, self.half(bit) * (rows // 2), 0), (m, rows // 2, w))
        return shard

    def along(self, mine, direct):
        if not self.fast:
            return lax.all_gather(mine, "seq", axis=0)
        if direct:
            copies = jnp.broadcast_to(mine[None], (self.nz,) + mine.shape)
            return lax.all_to_all(copies, "seq", 0, 0, axis_index_groups=self.groups)
        return lax.all_gather(mine, "seq", axis=0, axis_index_groups=self.groups)

    def across(self, near):
        return [near, swap(near, "seq", 1, self.seq)] if self.fast else [near]

    def pair(self, pieces, bit):
        return pieces + [swap(p, "batch", bit, 4) for p in pieces] if self.fast else pieces

    def sum_along(self, near, direct=False):
        if direct:
            z = self.place // 2
            total = lax.dynamic_index_in_dim(near, z, 0, keepdims=False).astype(F32)
            for k in range(1, self.nz):
                sent = lax.dynamic_index_in_dim(near, z ^ k, 0, keepdims=False)
                pairs = [(i, i ^ (2 * k)) for i in range(self.seq)]
                total = total + lax.ppermute(sent, "seq", pairs).astype(F32)
            return total.astype(BF)
        if near.shape[1] == 3:
            got = lax.all_to_all(near, "seq", 0, 0, axis_index_groups=self.groups)
            return jnp.sum(got.astype(F32), axis=0).astype(BF)
        return lax.psum_scatter(near, "seq", scatter_dimension=0, axis_index_groups=self.groups)

    def join(self, mine, bit, axis):
        other = swap(mine, "batch", bit, self.batch)
        lower = self.half(bit) == 0
        return jnp.concatenate([jnp.where(lower, mine, other), jnp.where(lower, other, mine)], axis=axis)


def add(left, right):
    return (left.astype(F32) + right.astype(F32)).astype(BF)


def params(mib):
    return pltpu.CompilerParams(vmem_limit_bytes=mib * 1024 * 1024)


def staged(name, body, out_shape, in_specs, out_specs, scratch):
    ins = [i for i, spec in enumerate(in_specs) if spec is STAGE]
    outs = [i for i, spec in enumerate(out_specs) if spec is STAGE]
    n_in, n_out, n_own = len(in_specs), len(out_specs), len(scratch)

    def kernel(*refs):
        operands, results = list(refs[:n_in]), list(refs[n_in : n_in + n_out])
        own, extra = refs[n_in + n_out : n_in + n_out + n_own], refs[n_in + n_out + n_own :]
        in_sem, out_sem = extra[-2:]
        loads, stores = {}, {}
        for k, i in enumerate(ins):
            loads[i] = pltpu.make_async_copy(operands[i], extra[k], in_sem.at[k])
            operands[i] = extra[k]
        for k, i in enumerate(outs):
            held = extra[len(ins) + k]
            stores[i] = pltpu.make_async_copy(held, results[i], out_sem.at[k])
            results[i] = held
        start_all(loads.values())
        flushed = []

        def ready(*some):
            for i in some or list(loads):
                if i in loads:
                    loads.pop(i).wait()

        def flush(*some):
            for i in some:
                if i in stores and i not in flushed:
                    flushed.append(i)
                    stores[i].start()

        body(ready, flush, *operands, *results, *own)
        ready()
        flush(*stores)
        wait_all(stores.values())

    def call(*operands):
        return pl.pallas_call(
            kernel,
            out_shape=out_shape,
            in_specs=[ANY if spec is STAGE else spec for spec in in_specs],
            out_specs=[ANY if spec is STAGE else spec for spec in out_specs],
            scratch_shapes=list(scratch)
            + [pltpu.VMEM(operands[i].shape, operands[i].dtype) for i in ins]
            + [pltpu.VMEM(out_shape[i].shape, out_shape[i].dtype) for i in outs]
            + [pltpu.SemaphoreType.DMA((max(1, len(ins)),)), pltpu.SemaphoreType.DMA((max(1, len(outs)),))],
            compiler_params=params(60),
            cost_estimate=cost(name),
            name=name,
        )(*operands)

    return call


def low_lanes():
    return lax.broadcasted_iota(jnp.int32, (1, 128), 1) < HEAD


def spread(state):
    low = low_lanes()
    zero = jnp.zeros_like(state)
    return jnp.concatenate([jnp.where(low, state, zero), jnp.where(low, zero, state)], axis=0)


def squeeze(full):
    return jnp.where(low_lanes(), full[:HEAD], full[HEAD:])


def head_sums(values):
    row = lax.broadcasted_iota(jnp.int32, (128, 128), 0) < HEAD
    col = lax.broadcasted_iota(jnp.int32, (128, 128), 1) < HEAD
    ones = (row == col).astype(BF)
    high = values.astype(BF)
    rest = values - high.astype(F32)
    mid = rest.astype(BF)
    return dot(high, ones) + dot(mid, ones)


def block(i, size=256):
    return pl.ds(pl.multiple_of(i * size, size), size)


def fetch(base_ref, pieces, weight, sem, picks):
    return [
        [
            pltpu.make_async_copy(
                piece.at[:, pick],
                weight.at[:, k, pl.ds(pl.multiple_of(base_ref[b], 16), piece.shape[2]), :],
                sem.at[k, b],
            )
            for b, piece in enumerate(pieces)
        ]
        for k, pick in enumerate(picks)
    ]


def hand_out(base_ref, grads, outs, sem):
    m = grads.shape[1]
    return [
        [
            pltpu.make_async_copy(
                grads.at[:, k, pl.ds(pl.multiple_of(base_ref[b], 16), out.shape[-2]), :],
                out.at[:, k],
                sem.at[k, b],
            )
            for b, out in enumerate(outs)
        ]
        for k in range(m)
    ]


def piece_shapes(plan, m, part, w, count):
    return [jax.ShapeDtypeStruct((plan.nz, m, part, w), BF)] * (count if plan.fast else 1)


def start_all(copies):
    for c in copies:
        c.start()


def wait_all(copies):
    for c in copies:
        c.wait()


def soft(x):
    e = jnp.exp(-jnp.abs(x))
    return jnp.maximum(x, 0.0) + jnp.log1p(e), jnp.where(x >= 0.0, 1.0, e) / (1.0 + e)


def kv_body(plan, nb, ready, flush, base_ref, tokens_ref, gain_ref, tail_ref, *refs):
    pieces = refs[:nb]
    normed_ref, keys_ref, sig_ref, values_ref, fresh_ref, weight, sem = refs[nb:]
    d = tokens_ref.shape[1]
    copies = fetch(base_ref, pieces, weight, sem, (0, 1))
    for c in copies:
        start_all(c)
    ready()

    def norm(i, _):
        source = tokens_ref[block(i), :].astype(F32)
        normed_ref[block(i), :] = (source * inverse_rms(source) * gain_ref[...]).astype(BF)
        return 0

    lax.fori_loop(0, 2, norm, 0)
    flush(0)
    wait_all(copies[0])

    def key_part(j, _):
        linear = dot(normed_ref[...], weight[:, 0, :, block(j)].reshape(d, 256))
        plus, sig = soft(linear)
        keys_ref[:, block(j)] = plus.astype(BF)
        sig_ref[:, block(j)] = sig.astype(BF)
        return 0

    lax.fori_loop(0, d // 256, key_part, 0)
    flush(1, 2)
    wait_all(copies[1])

    def value_part(j, _):
        linear = dot(normed_ref[...], weight[:, 1, :, block(j)].reshape(d, 256))
        values_ref[:, block(j)] = linear.astype(BF)
        return 0

    lax.fori_loop(0, d // 256, value_part, 0)
    flush(3)

    def states(i, _):
        rows, lanes = block(i // 8), block(i % 8, 128)
        tail = tail_ref[rows, :].astype(BF)
        fresh_ref[i] = squeeze(dot_tn(keys_ref[rows, lanes], values_ref[rows, lanes] * tail))
        return 0

    lax.fori_loop(0, 16, states, 0, unroll=2)


def kv_call(plan, bases, tokens, gain, tail, pieces):
    nb = len(pieces)
    count, d = tokens.shape
    shape = jax.ShapeDtypeStruct((count, d), BF)
    return staged(
        "keys_values",
        functools.partial(kv_body, plan, nb),
        [shape] * 4 + [jax.ShapeDtypeStruct((16, HEAD, 128), F32)],
        [SMEM, STAGE, VMEM, VMEM] + [ANY] * nb,
        [STAGE] * 5,
        [
            pltpu.VMEM((plan.nz, 2, plan.span, d), BF),
            pltpu.SemaphoreType.DMA((2, nb)),
        ],
    )(bases, tokens, gain, tail, *pieces)


def qg_body(plan, nb, ready, flush, base_ref, normed_ref, *refs):
    pieces = refs[:nb]
    query_ref, sig_ref, gate_ref, weight, sem = refs[nb:]
    d = normed_ref.shape[1]
    copies = fetch(base_ref, pieces, weight, sem, (0, 1))
    for c in copies:
        start_all(c)
    ready()
    wait_all(copies[0])

    def query_part(j, _):
        linear = dot(normed_ref[...], weight[:, 0, :, block(j)].reshape(d, 256))
        plus, sig = soft(linear)
        query_ref[:, block(j)] = plus.astype(BF)
        sig_ref[:, block(j)] = sig.astype(BF)
        return 0

    lax.fori_loop(0, d // 256, query_part, 0)
    flush(0, 1)
    wait_all(copies[1])

    def gate_part(j, _):
        linear = dot(normed_ref[...], weight[:, 1, :, block(j)].reshape(d, 256))
        gate_ref[:, block(j)] = jax.nn.sigmoid(linear)
        return 0

    lax.fori_loop(0, d // 256, gate_part, 0)


def qg_call(plan, bases, normed, pieces):
    nb = len(pieces)
    count, d = normed.shape
    shape = jax.ShapeDtypeStruct((count, d), BF)
    return staged(
        "query_gate",
        functools.partial(qg_body, plan, nb),
        [shape, shape, jax.ShapeDtypeStruct((count, d), F32)],
        [SMEM, STAGE] + [ANY] * nb,
        [STAGE] * 3,
        [
            pltpu.VMEM((plan.nz, 2, plan.span, d), BF),
            pltpu.SemaphoreType.DMA((2, nb)),
        ],
    )(bases, normed, *pieces)


def pair_mask(segcol_ref, segrow_ref, r):
    t = lax.broadcasted_iota(jnp.int32, (256, 256), 0)
    s = lax.broadcasted_iota(jnp.int32, (256, 256), 1)
    return (segcol_ref[block(r), :] == segrow_ref[r]) & (t >= s)


def attend_body(
    plan, nb, ready, flush, base_ref, query_ref, keys_ref, values_ref, gate_ref, state_ref, segcol_ref, segrow_ref,
    gain_ref, tokens_ref, midgain_ref, *refs
):
    pieces = refs[:nb]
    attended_ref, gated_ref, middle_ref, normed_ref, mask_ref, weight, sem = refs[nb:]
    d = query_ref.shape[1]
    (copies,) = fetch(base_ref, pieces, weight, sem, (2,))
    start_all(copies)
    ready(1, 2, 3, 4, 5)
    for r in range(2):
        mask_ref[r] = pair_mask(segcol_ref, segrow_ref, r).astype(F32)

    def pair(i, _):
        r = i // 8
        rows, lanes = block(r), block(i % 8, 128)
        low = low_lanes()
        mask = mask_ref[r]
        q, k, v = query_ref[rows, lanes], keys_ref[rows, lanes], values_ref[rows, lanes]
        zero = jnp.zeros_like(q)
        inherit = (segcol_ref[rows, :] == 0.0).astype(BF)
        q0, q1 = jnp.where(low, q, zero), jnp.where(low, zero, q)
        w0 = (dot_nt(q0, k) * mask).astype(BF)
        w1 = (dot_nt(q1, k) * mask).astype(BF)
        carried = dot(q * inherit, spread(state_ref[i]))
        attended = jnp.where(low, dot(w0, v), dot(w1, v)) + carried
        inverse = lax.rsqrt(head_sums(attended * attended) * (1.0 / HEAD) + EPSILON)
        headed = attended * inverse * gain_ref[:, lanes]
        attended_ref[rows, lanes] = attended
        gated_ref[rows, lanes] = (headed * gate_ref[rows, lanes]).astype(BF)
        return 0

    lax.fori_loop(0, 16, pair, 0, unroll=2)
    flush(0, 1)
    wait_all(copies)

    ready()

    def project(j, _):
        out = dot(gated_ref[...], weight[:, 0, :, block(j)].reshape(d, 256))
        middle_ref[:, block(j)] = tokens_ref[:, block(j)].astype(F32) + out
        return 0

    lax.fori_loop(0, d // 256, project, 0)
    flush(2)

    def norm(i, _):
        middle = middle_ref[block(i), :]
        normed_ref[block(i), :] = (middle * inverse_rms(middle) * midgain_ref[...]).astype(BF)
        return 0

    lax.fori_loop(0, 2, norm, 0)


def attend_call(plan, bases, query, keys, values, gate, state, segcol, segrow, gain, tokens, midgain, pieces):
    nb = len(pieces)
    count, d = query.shape
    low, high = jax.ShapeDtypeStruct((count, d), BF), jax.ShapeDtypeStruct((count, d), F32)
    return staged(
        "attend",
        functools.partial(attend_body, plan, nb),
        [high, low, high, low],
        [SMEM] + [STAGE] * 5 + [VMEM] * 3 + [STAGE, VMEM] + [ANY] * nb,
        [STAGE] * 4,
        [
            pltpu.VMEM((2, 256, 256), F32),
            pltpu.VMEM((plan.nz, 1, plan.span, d), BF),
            pltpu.SemaphoreType.DMA((1, nb)),
        ],
    )(bases, query, keys, values, gate, state, segcol, segrow, gain, tokens, midgain, *pieces)


def mid_body(
    plan, nb, ready, flush, base_ref, back_ref, got_ref, middle_ref, midgain_ref, upstream_ref, gate_ref, attended_ref,
    gain_ref, query_ref, segcol_ref, *refs
):
    pieces = refs[:nb]
    midback_ref, branch_ref, gateback_ref, attback_ref, direct_ref, gains_ref, gated_back, weight, sem = refs[nb:]
    d = query_ref.shape[1]
    (copies,) = fetch(base_ref, pieces, weight, sem, (2,))
    start_all(copies)
    ready(1, 2, 3, 5)

    def norm(i, total):
        rows = block(i, 128)
        dy = back_ref[rows, :].astype(F32) + got_ref[rows, :].astype(F32)
        v = middle_ref[rows, :]
        r = inverse_rms(v)
        scaled = dy * midgain_ref[...]
        mean = jnp.mean(scaled * v, axis=-1, keepdims=True)
        back = upstream_ref[rows, :].astype(F32) + r * scaled - v * (r * r * r * mean)
        midback_ref[rows, :] = back
        branch_ref[rows, :] = back.astype(BF)
        return total + jnp.sum(dy * v * r, axis=0, keepdims=True)

    gains_ref[0:1, :] = lax.fori_loop(0, 4, norm, jnp.zeros((1, d), F32))
    flush(0, 1)
    wait_all(copies)

    slabs = 256 // plan.span

    def through(j, _):
        out_w = weight[pl.ds(j * slabs, slabs), 0].reshape(256, d)
        gated_back[:, block(j)] = dot_nt(branch_ref[...], out_w)
        return 0

    lax.fori_loop(0, d // 256, through, 0)

    ready()

    def pair(p, _):
        lanes = block(p, 128)
        gain = gain_ref[:, lanes]
        total = jnp.zeros((1, 128), F32)
        for r in range(2):
            rows = pl.ds(r * 256, 256)
            att = attended_ref[rows, lanes]
            inverse = lax.rsqrt(head_sums(att * att) * (1.0 / HEAD) + EPSILON)
            gate = gate_ref[rows, lanes]
            back = gated_back[rows, lanes]
            unit = att * inverse
            gateback_ref[rows, lanes] = (back * (unit * gain) * gate * (1.0 - gate)).astype(BF)
            dy = back * gate
            total = total + jnp.sum(dy * unit, axis=0, keepdims=True)
            scaled = dy * gain
            mean = head_sums(scaled * unit) * (1.0 / HEAD)
            attback = (inverse * (scaled - unit * mean)).astype(BF)
            attback_ref[rows, lanes] = attback
            inherit = (segcol_ref[rows, :] == 0.0).astype(BF)
            direct_ref[r * 8 + p] = squeeze(dot_tn(query_ref[rows, lanes] * inherit, attback))
        gains_ref[1:2, lanes] = total
        return 0

    lax.fori_loop(0, 8, pair, 0)


def mid_call(plan, bases, back, got, middle, midgain, upstream, gate, attended, gain, query, segcol, pieces):
    nb = len(pieces)
    count, d = query.shape
    low, high = jax.ShapeDtypeStruct((count, d), BF), jax.ShapeDtypeStruct((count, d), F32)
    return staged(
        "middle_back",
        functools.partial(mid_body, plan, nb),
        [
            high, low, low, low,
            jax.ShapeDtypeStruct((16, HEAD, 128), F32),
            jax.ShapeDtypeStruct((2, d), F32),
        ],
        [SMEM] + [STAGE] * 3 + [VMEM] + [STAGE] * 3 + [VMEM, STAGE, VMEM] + [ANY] * nb,
        [STAGE] * 5 + [VMEM],
        [
            pltpu.VMEM((count, d), F32),
            pltpu.VMEM((plan.nz, 1, plan.span, d), BF),
            pltpu.SemaphoreType.DMA((1, nb)),
        ],
    )(bases, back, got, middle, midgain, upstream, gate, attended, gain, query, segcol, *pieces)


def turn_rows(source_ref, turned):
    def turn(i, _):
        turned[block(i), :] = source_ref[:, block(i)].T
        return 0

    lax.fori_loop(0, source_ref.shape[1] // 256, turn, 0)


def gradient_rows(plan, turned, right_ref, grads, k):
    d = turned.shape[0]
    slabs = 256 // plan.span

    def features(i, _):
        value = dot(turned[block(i), :], right_ref[...]).astype(BF)
        grads[pl.ds(i * slabs, slabs), k] = value.reshape(slabs, plan.span, d)
        return 0

    lax.fori_loop(0, d // 256, features, 0)


def grads_body(plan, which, ready, flush, base_ref, *refs):
    m, n = len(which), max(which) + 1
    lefts, rights = refs[:n], refs[n : n + m]
    outs = refs[n + m : -3]
    turned, grads, sem = refs[-3:]
    copies = hand_out(base_ref, grads, outs, sem)
    for k in range(m):
        if k == 0 or which[k] != which[k - 1]:
            ready(1 + which[k])
            turn_rows(lefts[which[k]], turned)
        ready(1 + n + k)
        gradient_rows(plan, turned, rights[k], grads, k)
        start_all(copies[k])
    for k in range(m):
        wait_all(copies[k])


def grads_call(plan, bases, lefts, which, rights):
    m = len(rights)
    count, d = lefts[0].shape
    outs = piece_shapes(plan, m, plan.rows // 2 if plan.fast else plan.rows, d, 4)
    return staged(
        "square_gradients",
        functools.partial(grads_body, plan, which),
        outs,
        [SMEM] + [STAGE] * (len(lefts) + m),
        [ANY] * len(outs),
        [
            pltpu.VMEM((d, count), BF),
            pltpu.VMEM((plan.nz, m, plan.span, d), BF),
            pltpu.SemaphoreType.DMA((m, len(outs))),
        ],
    )(bases, *lefts, *rights)


def inner_body(
    plan, ready, flush, query_ref, keys_ref, values_ref, qsig_ref, attback_ref, state_ref, segcol_ref, segrow_ref,
    qback_ref, kin_ref, vin_ref, mask_ref, turn_ref
):
    for r in range(2):
        mask = pair_mask(segcol_ref, segrow_ref, r).astype(F32)
        mask_ref[r] = mask
        turn_ref[r] = mask.T

    ready()

    def pair(i, _):
        r = i // 8
        rows, lanes = block(r), block(i % 8, 128)
        low = low_lanes()
        mask, mask_t = mask_ref[r], turn_ref[r]
        q, k, v, ab = (x[rows, lanes] for x in (query_ref, keys_ref, values_ref, attback_ref))
        zero = jnp.zeros_like(q)
        inherit = (segcol_ref[rows, :] == 0.0).astype(BF)
        halves = []
        for h in range(2):
            pick = (lambda x: jnp.where(low, x, zero)) if h == 0 else (lambda x: jnp.where(low, zero, x))
            k_h, v_h, ab_h = pick(k), pick(v), pick(ab)
            w_t = (dot_nt(k_h, q) * mask_t).astype(BF)
            sb = (dot_nt(ab_h, v) * mask).astype(BF)
            sb_t = (dot_nt(v_h, ab) * mask_t).astype(BF)
            halves.append((dot(sb, k), dot(sb_t, q), dot(w_t, ab)))
        qb, kb, vb = (jnp.where(low, a, b) for a, b in zip(*halves))
        qb = qb + dot_nt(ab * inherit, spread(state_ref[i]))
        qback_ref[rows, lanes] = (qb * qsig_ref[rows, lanes].astype(F32)).astype(BF)
        kin_ref[rows, lanes] = kb
        vin_ref[rows, lanes] = vb
        return 0

    lax.fori_loop(0, 16, pair, 0, unroll=2)


def inner_call(plan, query, keys, values, qsig, attback, state, segcol, segrow):
    count, d = query.shape
    low, high = jax.ShapeDtypeStruct((count, d), BF), jax.ShapeDtypeStruct((count, d), F32)
    return staged(
        "attend_back",
        functools.partial(inner_body, plan),
        [low, high, high],
        [STAGE] * 6 + [VMEM] * 2,
        [STAGE] * 3,
        [pltpu.VMEM((2, 256, 256), F32), pltpu.VMEM((2, 256, 256), F32)],
    )(query, keys, values, qsig, attback, state, segcol, segrow)


def outer_body(
    plan, sides, ready, flush, base_ref, keys_ref, values_ref, ksig_ref, kin_ref, vin_ref, after_ref, segcol_ref, segrow_ref,
    normed_ref, *refs
):
    outs = refs[:sides]
    kback_ref, vback_ref, turned, grads, sem = refs[sides:]
    ready(9)
    copies = hand_out(base_ref, grads, outs, sem)

    turn_rows(normed_ref, turned)
    ready()

    def pair(i, _):
        r = i // 8
        rows, lanes = block(r), block(i % 8, 128)
        tail = (segcol_ref[rows, :] == segrow_ref[r][:, 255:256]).astype(F32)
        after = spread(after_ref[i])
        kb = kin_ref[rows, lanes] + dot_nt(values_ref[rows, lanes], after) * tail
        vb = vin_ref[rows, lanes] + dot(keys_ref[rows, lanes], after) * tail
        kback_ref[rows, lanes] = (kb * ksig_ref[rows, lanes].astype(F32)).astype(BF)
        vback_ref[rows, lanes] = vb.astype(BF)
        return 0

    lax.fori_loop(0, 16, pair, 0, unroll=2)
    flush(sides, sides + 1)
    for k, right in enumerate((kback_ref, vback_ref)):
        gradient_rows(plan, turned, right, grads, k)
        start_all(copies[k])
    for k in range(2):
        wait_all(copies[k])


def outer_call(plan, bases, keys, values, ksig, kin, vin, after, segcol, segrow, normed):
    count, d = keys.shape
    outs = piece_shapes(plan, 2, plan.rows // 2 if plan.fast else plan.rows, d, 4)
    low = jax.ShapeDtypeStruct((count, d), BF)
    got = staged(
        "key_value_gradients",
        functools.partial(outer_body, plan, len(outs)),
        outs + [low] * 2,
        [SMEM] + [STAGE] * 6 + [VMEM] * 2 + [STAGE],
        [ANY] * len(outs) + [STAGE] * 2,
        [
            pltpu.VMEM((d, count), BF),
            pltpu.VMEM((plan.nz, 2, plan.span, d), BF),
            pltpu.SemaphoreType.DMA((2, len(outs))),
        ],
    )(bases, keys, values, ksig, kin, vin, after, segcol, segrow, normed)
    return got[: len(outs)], got[len(outs) :]


def entry_body(plan, nb, ready, flush, base_ref, tokens_ref, gain_ref, midback_ref, qb_ref, kb_ref, vb_ref, gb_ref, *refs):
    kv, qg = refs[:nb], refs[nb : 2 * nb]
    out_ref, gains_ref, total, weight, more, sem = refs[2 * nb :]
    d = tokens_ref.shape[1]
    copies = fetch(base_ref, qg, weight, sem.at[0], (0, 1)) + fetch(
        base_ref, kv, more, sem.at[1], (0, 1)
    )
    for c in copies:
        start_all(c)
    slabs = 256 // plan.span
    for c, (back, scr, k) in zip(
        copies, ((qb_ref, weight, 0), (gb_ref, weight, 1), (kb_ref, more, 0), (vb_ref, more, 1))
    ):
        wait_all(c)
        first = back is qb_ref
        ready({id(qb_ref): 4, id(kb_ref): 5, id(vb_ref): 6, id(gb_ref): 7}[id(back)])

        def through(j, _, back=back, scr=scr, k=k, first=first):
            rows_w = scr[pl.ds(j * slabs, slabs), k].reshape(256, d)
            value = dot_nt(back[...], rows_w)
            if first:
                total[:, block(j)] = value
            else:
                total[:, block(j)] += value
            return 0

        lax.fori_loop(0, d // 256, through, 0)

    ready()

    def norm(i, gains):
        rows = block(i, 128)
        dy = total[rows, :]
        v = tokens_ref[rows, :].astype(F32)
        r = inverse_rms(v)
        scaled = dy * gain_ref[...]
        mean = jnp.mean(scaled * v, axis=-1, keepdims=True)
        out_ref[rows, :] = midback_ref[rows, :] + r * scaled - v * (r * r * r * mean)
        return gains + jnp.sum(dy * v * r, axis=0, keepdims=True)

    gains_ref[...] = lax.fori_loop(0, 4, norm, jnp.zeros((1, d), F32))


def entry_call(plan, bases, tokens, gain, midback, qb, kb, vb, gb, kv, qg):
    nb = len(kv)
    count, d = tokens.shape
    return staged(
        "entry_back",
        functools.partial(entry_body, plan, nb),
        [jax.ShapeDtypeStruct((count, d), F32), jax.ShapeDtypeStruct((1, d), F32)],
        [SMEM, STAGE, VMEM] + [STAGE] * 5 + [ANY] * (2 * nb),
        [STAGE, VMEM],
        [
            pltpu.VMEM((count, d), F32),
            pltpu.VMEM((plan.nz, 2, plan.span, d), BF),
            pltpu.VMEM((plan.nz, 2, plan.span, d), BF),
            pltpu.SemaphoreType.DMA((2, 2, nb)),
        ],
    )(bases, tokens, gain, midback, qb, kb, vb, gb, *kv, *qg)


def blocks(base_ref, pieces, whole, sem, inward):
    d = whole.shape[2]
    copies = []
    for k in range(3):
        copies.append([])
        for b, piece in enumerate(pieces):
            n = piece.shape[0]
            for z in range(n):
                lanes = pl.ds(pl.multiple_of(base_ref[b] + z * (d // n), 128), 128)
                ends = (piece.at[z, k], whole.at[k, :, lanes])
                copies[-1].append(pltpu.make_async_copy(*(ends if inward else ends[::-1]), sem.at[k, b, z]))
    return copies


def ff_body(nb, ready, flush, base_ref, nm0_ref, nm1_ref, up0_ref, up1_ref, *refs):
    pieces = refs[:nb]
    mixed_refs, back_refs = refs[nb : nb + 2], refs[nb + 2 : nb + 4]
    joined_t, left_t, right_t, weight, joined_s, left_s, right_s, sem = refs[nb + 4 :]
    count, d = nm0_ref.shape
    hidden = weight.shape[1]
    copies = blocks(base_ref, pieces, weight, sem, True)
    for c in copies:
        start_all(c)
    for h, (nm_ref, up_ref) in enumerate(((nm0_ref, up0_ref), (nm1_ref, up1_ref))):
        rows = pl.ds(h * count, count)
        for start in range(0, hidden, 256):
            some = slice(start, min(start + 256, hidden))
            ready(1 + h)
            if h == 0 and start == 0:
                wait_all(copies[0])
            left = dot_nt(nm_ref[...], weight[0, some, :])
            if h == 0 and start == 0:
                wait_all(copies[1])
            right = dot_nt(nm_ref[...], weight[1, some, :])
            ready(3 + h)
            if h == 0 and start == 0:
                wait_all(copies[2])
            joined_back = dot_nt(up_ref[...], weight[2, some, :])
            for value, straight, turned in (
                (left * right, joined_s, joined_t),
                (joined_back * right, left_s, left_t),
                (joined_back * left, right_s, right_t),
            ):
                value = value.astype(BF)
                straight[rows, some] = value
                turned[some, rows] = value.T

    flush(4, 5, 6)

    def through(j, _):
        for h in range(2):
            rows = pl.ds(h * count, count)
            mixed_refs[h][:, block(j)] = dot(joined_s[rows, :], weight[2, :, block(j)]).astype(BF)
            back = dot(left_s[rows, :], weight[0, :, block(j)]) + dot(right_s[rows, :], weight[1, :, block(j)])
            back_refs[h][:, block(j)] = back.astype(BF)
        return 0

    lax.fori_loop(0, d // 256, through, 0)


def ff_call(bases, nm, up, pieces):
    nb = len(pieces)
    n, three, hidden, _ = pieces[0].shape
    count, d = nm[0].shape
    whole, some = jax.ShapeDtypeStruct((count, d), BF), jax.ShapeDtypeStruct((hidden, 2 * count), BF)
    return staged(
        "feed_forward",
        functools.partial(ff_body, nb),
        [whole] * 4 + [some] * 3,
        [SMEM] + [STAGE] * 4 + [ANY] * nb,
        [STAGE] * 7,
        [pltpu.VMEM((three, hidden, d), BF)]
        + [pltpu.VMEM((2 * count, hidden), BF)] * 3
        + [pltpu.SemaphoreType.DMA((3, nb, n))],
    )(bases, *nm, *up, *pieces)


def ffgrad_body(ready, flush, base_ref, *refs):
    nms, ups = refs[:4], refs[4:8]
    joined, left, right = [refs[8 + k : 14 : 3] for k in range(3)]
    outs, (grads, sem) = refs[14:-2], refs[-2:]
    count, d = nms[0].shape
    copies = blocks(base_ref, outs, grads, sem, False)
    for k, (turned, straight) in enumerate(((left, nms), (right, nms), (joined, ups))):

        ready(*((1, 2, 3, 4, 10, 13), (11, 14), ())[k])

        def some(j, _, k=k, turned=turned, straight=straight):
            value = None
            for h in range(4):
                part = dot(turned[h // 2][:, pl.ds(h % 2 * count, count)], straight[h][:, block(j)])
                value = part if value is None else value + part
            grads[k, :, block(j)] = value.astype(BF)
            return 0

        lax.fori_loop(0, d // 256, some, 0)
        start_all(copies[k])
    for k in range(3):
        wait_all(copies[k])


def ffgrad_call(bases, nms, ups, first, second, shapes):
    hidden = first[0].shape[0]
    d = nms[0].shape[1]
    return staged(
        "feed_forward_gradients",
        ffgrad_body,
        [jax.ShapeDtypeStruct(shape, BF) for shape in shapes],
        [SMEM] + [STAGE] * 14,
        [ANY] * len(shapes),
        [
            pltpu.VMEM((3, hidden, d), BF),
            pltpu.SemaphoreType.DMA((3, len(shapes), shapes[0][0])),
        ],
    )(bases, *nms, *ups, *first, *second)


def beyond(order, step, size):
    return [(i, i + order * step) for i in range(size) if 0 <= i + order * step < size]


class Chain:
    def __init__(self, own, keep, order, size):
        self.total, self.before = own, jnp.zeros_like(own)
        self.whole, self.between = keep[:, None, None], jnp.ones_like(keep)[:, None, None]
        self.order, self.size, self.reach = order, size, 1

    def step(self, *others):
        rows, n, lanes = self.total.shape
        flags = jnp.broadcast_to(self.whole, (rows, 16, lanes))
        sent = tie(jnp.concatenate([self.total, flags], axis=1).astype(BF), *others)
        received = lax.ppermute(sent, "seq", beyond(self.order, self.reach, self.size))
        got, got_whole = received[:, :n].astype(F32), received[:, n : n + 1, :1].astype(F32)
        self.before = self.before + self.between * got
        self.total = self.total + self.whole * got
        self.between, self.whole = self.between * got_whole, self.whole * got_whole
        self.reach *= 2
        return received

    def result(self):
        while self.reach < self.size:
            self.step()
        return self.before.astype(BF).reshape(-1, HEAD, 128)


def shards(
    mesh_shape,
    tokens,
    starts,
    entry_gain,
    query_weight,
    key_weight,
    value_weight,
    gate_weight,
    head_gain,
    output_weight,
    middle_gain,
    left_weight,
    right_weight,
    down_weight,
    cotangent,
):
    rows_here, span, width = tokens.shape
    count = rows_here * span
    hidden = left_weight.shape[1]
    plan = Plan(mesh_shape, width)
    seq = plan.seq
    by_whole, by_half, by_quarter = jnp.zeros((1,), jnp.int32), plan.bases((1,)), plan.bases((2, 1))

    place = jnp.arange(span)
    segment = dot(starts.astype(BF), (place[:, None] <= place[None, :]).astype(BF))
    last = segment[:, span - 1 :]
    keep = (last[:, 0] == 0).astype(F32)
    tail = (segment == last).astype(F32).reshape(count, 1)
    segcol, segrow = segment.reshape(count, 1), segment.reshape(rows_here, 1, span)
    source = tokens.reshape(count, width)
    entry_row, head_row, mid_row = (g.reshape(1, width) for g in (entry_gain, head_gain, middle_gain))

    def scan(own, order):
        return Chain(own.reshape(rows_here, -1, 128), keep, order, seq)

    done = {}

    def held(name, value):
        return tie(value, *(done[other] for other in WAITS.get(name, ()) if other in done))

    def note(name, value):
        done[name] = value
        return value

    def send(name, value, axis, bit):
        return note(name, swap(held(name, value), axis, bit, plan.seq if axis == "seq" else plan.batch))

    def quarter(weights):
        return plan.mine(jnp.stack(weights), (2, 1))

    kv_z = note("kvz", plan.along(quarter([key_weight, value_weight]), True))
    qgo_z = quarter([query_weight, gate_weight, output_weight])
    qgo_z = note("qgoz", plan.along(held("qgoz", qgo_z), True))
    mine = hidden // 4
    stack = lax.dynamic_slice(
        jnp.stack([left_weight.T, right_weight.T, down_weight]),
        (0, plan.lane * mine, 0),
        (3, mine, plan.rows),
    )
    ff_seq = lax.all_gather(held("ffg", stack), "seq", axis=0)
    if plan.rows != 128:
        ff_seq = ff_seq.transpose(1, 2, 0, 3).reshape(3, mine, width // 128, 128).transpose(2, 0, 1, 3)
    upstream = cotangent.reshape(count, width)
    kv, qgo = [kv_z], [qgo_z]
    if "up" in WAITS.get("first", ()):
        up_above = send("up", upstream, "batch", 2)
    if plan.fast:
        kv.append(send("kvx", kv_z, "seq", 1))
        kv += [send("kvn", kv_z, "batch", 2), send("kvf", kv[1], "batch", 2)]
        kv += [send("kvc", piece, "batch", 1) for piece in kv]
    if plan.fast and "qgox" in WAITS.get("first", ()):
        qgo.append(send("qgox", qgo_z, "seq", 1))
        qgo.append(send("qgon", qgo_z, "batch", 2))

    normed_in, keys, ksig, values, fresh = kv_call(
        plan, held("kvk", by_quarter), source, entry_row, tail, kv
    )
    note("kvk", keys)
    chain = scan(fresh, 1)
    if "r1" in WAITS.get("first", ()):
        note("r1", chain.step(*(done[other] for other in WAITS.get("r1", ()))))
    if plan.fast and len(qgo) == 1:
        qgo.append(send("qgox", qgo_z, "seq", 1))
        qgo.append(send("qgon", qgo_z, "batch", 2))
    if "r1" not in done:
        note("r1", chain.step(*(done[other] for other in WAITS.get("r1", ()) if other in done)))
    if plan.fast:
        qgo.append(send("qgof", qgo[1], "batch", 2))
    note("r2", chain.step(*(done[other] for other in WAITS.get("r2", ()) if other in done)))
    if plan.fast:
        qgo += [send("qgoc", piece, "batch", 1) for piece in qgo]
    if "up" not in done:
        up_above = send("up", upstream, "batch", 2)
    up_all = [upstream, send("upb", upstream, "batch", 1), up_above, send("upd", up_above, "batch", 1)]
    note("r3", chain.step(*(done[other] for other in WAITS.get("r3", ()) if other in done)))
    state = chain.result()
    query, qsig, gate = qg_call(plan, held("qgk", by_quarter), normed_in, qgo)
    note("qgk", query)
    attended, gated, middle, normed_mid = attend_call(
        plan, held("att", by_quarter), query, keys, values, gate, state, segcol, segrow, head_row, source, mid_row, qgo
    )
    note("att", gated)
    nm_above = send("nma", normed_mid, "batch", 2)
    nm_all = [normed_mid, send("nmb", normed_mid, "batch", 1)]
    mixed_0, mixed_1, back_0, back_1, *saved_a = ff_call(held("ffa", by_whole), nm_all, up_all[:2], [ff_seq])
    note("ffa", back_0)
    nm_above = held("nmd", nm_above)
    nm_all += [nm_above, send("nmd", nm_above, "batch", 1)]
    back_own = note("bo", add(back_0, send("bo1", back_1, "batch", 1)))
    mixed_2, mixed_3, back_2, back_3, *saved_b = ff_call(held("ffb", by_whole), nm_all[2:], up_all[2:], [ff_seq])
    note("ffb", back_2)
    back_there = note("bt", add(back_2, send("bt1", back_3, "batch", 1)))
    back_got = send("bg", back_there, "batch", 2)
    ff_terms = ffgrad_call(held("ffr", by_whole), nm_all, up_all, saved_a, saved_b, [ff_seq.shape])
    note("ffr", ff_terms[0])
    ff_share = held("fs", ff_terms[0])
    if plan.rows != 128:
        ff_share = ff_share.transpose(1, 2, 0, 3).reshape(3, mine, seq, plan.rows).transpose(2, 0, 1, 3)
    ff_part = note("fs", lax.psum_scatter(ff_share, "seq", scatter_dimension=0))

    midback, branch, gateback, attback, direct, two_gains = mid_call(
        plan, held("mid", by_quarter), back_own, back_got, middle, mid_row, upstream, gate, attended, head_row,
        query, segcol, qgo,
    )
    note("mid", attback)
    chain = scan(direct, -1)
    note("s1", chain.step())
    qback, kin, vin = inner_call(plan, query, keys, values, held("inn", qsig), attback, state, segcol, segrow)
    note("inn", kin)
    mixed_own = add(mixed_0, send("mo", mixed_1, "batch", 1))
    mixed_there = note("mt", add(mixed_2, send("mt1", mixed_3, "batch", 1)))
    mixed_got = send("mg", mixed_there, "batch", 2)
    note("s2", chain.step(*(done[other] for other in WAITS.get("s2", ()) if other in done)))
    ogq_terms = grads_call(
        plan, held("gra", by_half), [gated, normed_in], (0, 1, 1), [branch, gateback, qback]
    )
    note("gra", ogq_terms[0])

    def finish(part):
        return plan.join(add(part, swap(part, "batch", 2, 4)), 1, 1).astype(F32)

    def quarters(part):
        above = swap(part, "batch", 2, plan.batch)
        lower = plan.half(2) == 0
        mine = jnp.stack([jnp.where(lower, part, above), jnp.where(lower, above, part)])
        return mine, swap(mine, "batch", 1, plan.batch)

    if plan.fast and "oc" in WAITS.get("first", ()):
        ogq_far = note("oc", add(ogq_terms[1], send("oc1", ogq_terms[3], "batch", 1)))
        ogq_near = add(ogq_terms[0], send("oc0", ogq_terms[2], "batch", 1))
        ogq_got = send("ox", ogq_far, "seq", 1)
    note("s3", chain.step(*(done[other] for other in WAITS.get("s3", ()) if other in done)))
    if plan.fast and "oc" not in done:
        ogq_far = note("oc", add(ogq_terms[1], send("oc1", ogq_terms[3], "batch", 1)))
        ogq_near = add(ogq_terms[0], send("oc0", ogq_terms[2], "batch", 1))
        ogq_got = send("ox", ogq_far, "seq", 1)
    after = chain.result()
    kv_terms, (kback, vback) = outer_call(
        plan, held("out", by_half), keys, values, ksig, kin, vin, after, segcol, segrow, normed_in
    )
    note("out", kback)
    if plan.fast:
        kv_far = note("kc", add(kv_terms[1], send("kc1", kv_terms[3], "batch", 1)))
        kv_got = send("kx", kv_far, "seq", 1)
        kv_near = add(kv_terms[0], send("kc0", kv_terms[2], "batch", 1))
    input_gradient, entry_term = entry_call(
        plan, held("ent", by_quarter), source, entry_row, midback, qback, kback, vback, gateback, kv, qgo
    )
    note("ent", entry_term)
    input_gradient = input_gradient.reshape(tokens.shape)
    mixed = (middle + (mixed_own.astype(F32) + held("mx", mixed_got).astype(F32))).astype(BF)
    mixed = mixed.reshape(tokens.shape)
    if plan.fast:
        kv_sum = note("ks", add(kv_near, held("ks", kv_got)))
        kv_part = note("kz", plan.sum_along(kv_sum, True))
        ogq_sum = note("os", add(ogq_near, held("os", ogq_got)))
        ogq_part = note("oz", plan.sum_along(ogq_sum))
        wide = quarters(held("fw", ff_part))
        note("fw", wide[0])
        output_total, gate_total, query_total = finish(held("of", ogq_part))
        key_total, value_total = finish(held("kf", kv_part))
    else:
        wide = quarters(ff_part)
        output_total, gate_total, query_total, key_total, value_total = (
            total
            for term in (ogq_terms, kv_terms)
            for total in lax.psum(lax.psum_scatter(term[0], "seq", scatter_dimension=0), "batch").astype(F32)
        )
    own, other = wide
    lower = plan.half(1) == 0
    first, second = jnp.where(lower, own, other), jnp.where(lower, other, own)
    wide = jnp.concatenate([first[0], second[0], first[1], second[1]], axis=1).astype(F32)
    left_total, right_total, down_total = wide[0].T, wide[1].T, wide[2]
    gains = held("gains", jnp.concatenate([two_gains, entry_term]))
    if plan.fast:
        for axis, size in (("batch", plan.batch), ("seq", seq)):
            step = 1
            while step < size:
                gains = gains + swap(gains, axis, step, size)
                step *= 2
    else:
        gains = lax.psum(gains, ("seq", "batch"))
    gains = lax.dynamic_slice(gains, (0, plan.place * plan.rows), (3, plan.rows))
    return (
        mixed,
        input_gradient,
        gains[2],
        query_total,
        key_total,
        value_total,
        gate_total,
        gains[1],
        output_total,
        gains[0],
        left_total,
        right_total,
        down_total,
    )


def solution(mesh):
    row, cut, wide = P("batch", "seq", None), P("seq", None), P(None, "seq")
    in_specs = (row, P("batch", "seq"), P(), cut, cut, cut, cut, P(), cut, P(), cut, cut, wide, row)
    out_specs = (row, row, P("seq"), cut, cut, cut, cut, P("seq"), cut, P("seq"), cut, cut, wide)
    return jax.shard_map(
        functools.partial(shards, dict(mesh.shape)),
        mesh=mesh,
        in_specs=in_specs,
        out_specs=out_specs,
        check_vma=False,
    )
```
